32 devices in a mesh: gx: 8 (over z, y), gy: 4 (over x, core).
Axes of the slice: x: 2, y: 2, z: 4, core: 2. Of those that a mesh axis runs over, the one named last changes fastest.
Arguments:
- pressure: float32 [12, 256, 512], P(None, 'gx', 'gy'), may hold values from 0.5 to 1.5
- saturation: float32 [2, 12, 256, 512], P(None, None, 'gx', 'gy'), may hold values from 0.05 to 0.35
- permeability: float32 [3, 12, 256, 512], P(None, None, 'gx', 'gy'), may hold values from 0.25 to 8
- pore_volume: float32 [12, 256, 512], P(None, 'gx', 'gy'), may hold values from 0.5 to 8
- cell_depth: float32 [12, 256, 512], P(None, 'gx', 'gy'), may hold values from -4 to 4
- residual: float32 [3, 12, 256, 512], P(None, None, 'gx', 'gy'), may hold values from -12 to 12
- upstream_flags: int32 [12, 256, 512], P(None, 'gx', 'gy'), may hold values from 0 to 7
- perf_cell: int32 [32, 1024], P(('gx', 'gy')), may hold values from 0 to 49151
- perf_well: int32 [32, 1024], P(('gx', 'gy')), may hold values from -1 to 1023, as said below
- perf_index: float32 [32, 1024], P(('gx', 'gy')), may hold values from 0.5 to 4
- well_mode: int32 [1024], P(('gx', 'gy')), may hold values from 0 to 1
- well_target: float32 [1024], P(('gx', 'gy')), may hold values from 0.2 to 1.2
Outputs:
- new_pressure: float32 [12, 256, 512], P(None, 'gx', 'gy')
- well_bhp: float32 [1024], P(('gx', 'gy'))
The draws below stay inside these ranges and needn't reach their ends.
Inputs may be any that keep to these rules, and one draw needn't show every extreme that they name: `upstream_flags`: bit 1 set: the cell is upstream on its face towards the next cell along x; bit 2: along y; bit 4: along z. `perf_cell`: the local cell number, within its row's block of columns, of the perforated cell. `perf_well`: -1 marks an empty slot; in each row the live slots come first; every well has at least one live slot; in every draw some row has all 1024 slots live. `well_mode`: 0: the well holds its bottom-hole pressure at well_target; 1: it produces well_target.
All inputs are finite; a program needn't handle non-finite values.
Results may differ from the reference program's by a relative error of at most 0.0003.
Values sent between devices are 32-bit elements; how exact they have to be, the bound alone decides.
No kernel may reach another device: no remote copies, remote signals or barrier semaphores. Data moves between devices by JAX's collectives and lax.ppermute only.
A program may use at most 64 MiB of HBM per device.

```python
import math
import jax
import jax.numpy as jnp
from jax import lax

NZ = 12
CX = 32
CY = 128
W_DEV = 32
PERF_DEV = 1024
SWEEPS = 2
NX = 256
NY = 512
WELLS = 1024
N_GX = 8
N_GY = 4
DEVICES = 32


def draw_perf_well(key, part):
    subkeys = jax.random.split(jax.random.fold_in(key, 7), 5)
    device_row = jnp.arange(DEVICES, dtype=jnp.int32)[:, None]
    slot_index = jnp.arange(PERF_DEV, dtype=jnp.int32)[None, :]
    drawn_count = jax.random.randint(subkeys[0], (DEVICES, 1), PERF_DEV // 8, PERF_DEV // 4 + 1)
    crowded = jax.random.randint(subkeys[1], (DEVICES, 1), 0, 8)
    fullest = jax.random.randint(subkeys[2], (), 0, DEVICES)
    live_count = jnp.where((crowded == 0) | (device_row == fullest), PERF_DEV, drawn_count)
    well_order = jax.random.permutation(subkeys[3], WELLS).astype(jnp.int32)
    home_well = well_order[device_row * W_DEV + jnp.minimum(slot_index, W_DEV - 1)]
    others = jax.random.randint(subkeys[4], (DEVICES, PERF_DEV), 0, WELLS)
    chosen = jnp.where(slot_index < W_DEV, home_well, others)
    return jnp.where(slot_index < live_count, chosen, -1).astype(jnp.int32)


def with_ends(array, key, smallest, top_value):
    longest = array.shape.index(max(array.shape))
    spots = []
    for shift in (0, 1):
        where = [jax.random.randint(jax.random.fold_in(key, axis), (), 0, length) for axis, length in enumerate(array.shape)]
        where[longest] = (where[longest] + shift) % array.shape[longest]
        spots.append(tuple(where))
    return array.at[spots[0]].set(smallest).at[spots[1]].set(top_value)


def levels(stream_key, dims, cuts, smallest, largest):
    gain, own = 1.0, jax.random.fold_in(stream_key, 6)
    for dim, shards_of in cuts:
        heights = jnp.exp(jax.random.uniform(jax.random.fold_in(own, dim), (shards_of,), jnp.float32, smallest / len(cuts), largest / len(cuts)))
        gain = gain * jnp.repeat(heights, dims[dim] // shards_of).reshape([-1 if axis == dim else 1 for axis in range(len(dims))])
    return gain


def normal_values(own_key, dims, scale, limit, shards=(), held_as=jnp.bfloat16):
    array = scale * jax.random.normal(own_key, dims, jnp.float32)
    if shards:
        array = array * levels(own_key, dims, shards, -0.22, 0.18)
    return jnp.clip(array, -limit, limit).astype(held_as)


def setup_inputs(seed: int = 0) -> dict:
    seeds = jax.random.split(jax.random.key(seed), 13)
    pressure = jnp.clip(0.5 + 1.0 * jax.random.uniform(seeds[0], (NZ, NX, NY), jnp.float32) ** levels(seeds[0], (NZ, NX, NY), ((1, 8), (2, 4)), -0.2, 0.2), 0.5, 1.5)
    saturation = jnp.clip(0.05 + 0.29999999 * jax.random.uniform(seeds[1], (2, NZ, NX, NY), jnp.float32) ** levels(seeds[1], (2, NZ, NX, NY), ((2, 8), (3, 4)), -0.2, 0.2), 0.05, 0.35)
    permeability = jnp.clip(jnp.exp(math.log(8.0) - 3.465736 * jax.random.uniform(seeds[2], (3, NZ, NX, NY), jnp.float32) ** levels(seeds[2], (3, NZ, NX, NY), ((2, 8), (3, 4)), -0.2, 0.2)), 0.25, 8.0)
    pore_volume = jnp.clip(jnp.exp(math.log(8.0) - 2.7725887 * jax.random.uniform(seeds[3], (NZ, NX, NY), jnp.float32) ** levels(seeds[3], (NZ, NX, NY), ((1, 8), (2, 4)), -0.2, 0.2)), 0.5, 8.0)
    cell_depth = normal_values(seeds[4], (NZ, NX, NY), 1.0, 4.0, ((1, 8), (2, 4)), jnp.float32)
    residual = normal_values(seeds[5], (3, NZ, NX, NY), 2.0, 12.0, ((2, 8), (3, 4)), jnp.float32)
    upstream_flags = with_ends(jax.random.randint(seeds[6], (NZ, NX, NY), 0, 8), jax.random.fold_in(seeds[6], 1), 0, 7).astype(jnp.int32)
    perf_cell = with_ends(jax.random.randint(seeds[7], (DEVICES, PERF_DEV), 0, NZ * CX * CY), jax.random.fold_in(seeds[7], 1), 0, (NZ * CX * CY) - 1).astype(jnp.int32)
    perf_well = draw_perf_well(jax.random.fold_in(seeds[12], 71), 0)
    perf_index = jnp.clip(jnp.exp(math.log(4.0) - 2.0794415 * jax.random.uniform(seeds[9], (DEVICES, PERF_DEV), jnp.float32) ** levels(seeds[9], (DEVICES, PERF_DEV), ((0, 32),), -0.2, 0.2)), 0.5, 4.0)
    well_mode = with_ends(jax.random.randint(seeds[10], (WELLS,), 0, 2), jax.random.fold_in(seeds[10], 1), 0, 1).astype(jnp.int32)
    well_target = jnp.clip(0.2 + 1 * jax.random.uniform(seeds[11], (WELLS,), jnp.float32) ** levels(seeds[11], (WELLS,), ((0, 32),), -0.2, 0.2), 0.2, 1.2)
    return {"pressure": pressure, "saturation": saturation, "permeability": permeability, "pore_volume": pore_volume, "cell_depth": cell_depth, "residual": residual, "upstream_flags": upstream_flags, "perf_cell": perf_cell, "perf_well": perf_well, "perf_index": perf_index, "well_mode": well_mode, "well_target": well_target}


MU_OIL = 2.0
MU_WATER = 1.0
MU_GAS = 0.2
COMP_OIL = 0.2
COMP_WATER = 0.05
GRAV_OIL = 0.4
GRAV_WATER = 0.5
GRAV_GAS = 0.08
RELAXATION = 0.8


def phase_weights(pressure):
    b_oil = 1.0 + COMP_OIL * (pressure - 1.0)
    b_water = 1.0 + COMP_WATER * (pressure - 1.0)
    return (1.0 / b_oil, 1.0 / b_water, 1.0 / pressure)


def phase_mobility(pressure, sat_water, sat_gas):
    sat_oil = 1.0 - sat_water - sat_gas
    b_oil = 1.0 + COMP_OIL * (pressure - 1.0)
    b_water = 1.0 + COMP_WATER * (pressure - 1.0)
    return (sat_oil * sat_oil * b_oil / MU_OIL, sat_water * sat_water * b_water / MU_WATER, sat_gas * sat_gas * pressure / MU_GAS)


def storage_term(weights, sat_water, sat_gas):
    sat_oil = 1.0 - sat_water - sat_gas
    return sat_oil * COMP_OIL * weights[0] + sat_water * COMP_WATER * weights[1] + sat_gas * weights[2]


def flag_bits(flag_code):
    bit_x = jnp.mod(flag_code, 2.0)
    remainder = (flag_code - bit_x) * 0.5
    bit_y = jnp.mod(remainder, 2.0)
    return bit_x, bit_y, (remainder - bit_y) * 0.5


def face_terms(weights, mob_center, mob_beside, perm_center, perm_beside, center_up, depth_drop):
    transmit = 2.0 * perm_center * perm_beside / (perm_center + perm_beside)
    coupling = jnp.zeros_like(transmit)
    gravity = jnp.zeros_like(transmit)
    for weight, center, beside, lift_rate in zip(weights, mob_center, mob_beside, (GRAV_OIL, GRAV_WATER, GRAV_GAS)):
        flux_term = weight * (transmit * jnp.where(center_up, center, beside))
        coupling = coupling + flux_term
        gravity = gravity + flux_term * lift_rate
    return coupling, gravity * depth_drop


def direction_terms(weights, center, plus_side, minus_side, bit_center, bit_minus):
    coup_plus, grav_plus = face_terms(weights, center[0], plus_side[0], center[1], plus_side[1], bit_center > 0.5, center[2] - plus_side[2])
    coup_minus, grav_minus = face_terms(weights, center[0], minus_side[0], center[1], minus_side[1], bit_minus < 0.5, center[2] - minus_side[2])
    return (coup_plus, coup_minus), grav_plus + grav_minus


def neighbour(grid_field, axis_dim, offset):
    padding = [(0, 0)] * grid_field.ndim
    padding[axis_dim] = (1, 1)
    padded = jnp.pad(grid_field, padding)
    return lax.slice_in_dim(padded, 1 + offset, 1 + offset + grid_field.shape[axis_dim], axis=axis_dim)


def coupled_sum(couplings, besides):
    running = couplings[0] * besides[0]
    for coupling, beside in zip(couplings[1:], besides[1:]):
        running = running + coupling * beside
    return running


def reference(pressure, saturation, permeability, pore_volume, cell_depth, residual, upstream_flags, perf_cell, perf_well, perf_index, well_mode, well_target):
    sat_water, sat_gas = saturation[0], saturation[1]
    weights = phase_weights(pressure)
    mobility = phase_mobility(pressure, sat_water, sat_gas)
    storage = pore_volume * storage_term(weights, sat_water, sat_gas)
    flag_parts = flag_bits(upstream_flags.astype(jnp.float32))
    couplings = ()
    gravity = jnp.zeros_like(pressure)
    for direction, axis_dim in ((0, 1), (1, 2), (2, 0)):
        center = (mobility, permeability[direction], cell_depth)
        plus_side = (tuple(neighbour(phase_field, axis_dim, 1) for phase_field in mobility), neighbour(permeability[direction], axis_dim, 1), neighbour(cell_depth, axis_dim, 1))
        minus_side = (tuple(neighbour(phase_field, axis_dim, -1) for phase_field in mobility), neighbour(permeability[direction], axis_dim, -1), neighbour(cell_depth, axis_dim, -1))
        coupled, grav_part = direction_terms(weights, center, plus_side, minus_side, flag_parts[direction], neighbour(flag_parts[direction], axis_dim, -1))
        couplings = couplings + coupled
        gravity = gravity + grav_part
    faces_total = couplings[0] + couplings[1] + couplings[2] + couplings[3] + couplings[4] + couplings[5]
    combined = weights[0] * residual[0] + weights[1] * residual[1] + weights[2] * residual[2]
    rhs_base = (storage * pressure - combined) + gravity
    total_mob = weights[0] * mobility[0] + weights[1] * mobility[1] + weights[2] * mobility[2]
    devices_row = jnp.arange(N_GX * N_GY, dtype=jnp.int32)[:, None]
    perf_layer = perf_cell // (CX * CY)
    cell_x = (devices_row // N_GY) * CX + (perf_cell // CY) % CX
    cell_y = (devices_row % N_GY) * CY + perf_cell % CY
    is_live = perf_well >= 0
    well_ids = jnp.where(is_live, perf_well, 0).reshape(-1)
    perf_factor = jnp.where(is_live, perf_index * total_mob[perf_layer, cell_x, cell_y], 0.0)
    well_base = jax.ops.segment_sum(perf_factor.reshape(-1), well_ids, num_segments=WELLS)
    well_diag = jnp.zeros_like(pressure).at[perf_layer, cell_x, cell_y].add(perf_factor)
    total_diag = (storage + faces_total) + well_diag
    current = pressure
    well_bhp = well_target
    for sweep_index in range(SWEEPS):
        at_perf = current[perf_layer, cell_x, cell_y]
        well_part = jax.ops.segment_sum((perf_factor * at_perf).reshape(-1), well_ids, num_segments=WELLS)
        well_bhp = jnp.where(well_mode == 0, well_target, (well_part - well_target) / well_base)
        perf_bhp = perf_factor * well_bhp[well_ids].reshape(perf_factor.shape)
        well_rhs = jnp.zeros_like(pressure).at[perf_layer, cell_x, cell_y].add(perf_bhp)
        besides = (neighbour(current, 1, 1), neighbour(current, 1, -1), neighbour(current, 2, 1), neighbour(current, 2, -1), neighbour(current, 0, 1), neighbour(current, 0, -1))
        current = current + RELAXATION * (((rhs_base + well_rhs) - total_diag * current) + coupled_sum(couplings, besides)) / total_diag
    return current, well_bhp
```

```python
import jax
import jax.numpy as jnp
from jax import lax
from jax.experimental import pallas as pl
from jax.experimental.pallas import tpu as pltpu
from jax.sharding import PartitionSpec as P

COMP_OIL = 0.2
COMP_WATER = 0.05
GRAV_OIL = 0.4
GRAV_WATER = 0.5
GRAV_GAS = 0.08
RELAXATION = 0.8
LANES = 128
PLANES = 6
EDGE = 8

F32 = jnp.float32
BF16 = jnp.bfloat16
AXES = ("gx", "gy")


def nn(a, b):
    return lax.dot_general(a, b, (((1,), (0,)), ((), ())), preferred_element_type=F32)


def nt(a, b):
    return lax.dot_general(a, b, (((1,), (1,)), ((), ())), preferred_element_type=F32)


def halves(x):
    high = x.astype(BF16).astype(F32)
    return high, x - high


def iota(shape, dim):
    return lax.broadcasted_iota(jnp.int32, shape, dim)


def hot(index, count):
    return iota((count, index.shape[1]), 0) == index


def ones_of(mask):
    return jnp.where(mask, 1.0, 0.0).astype(BF16)


def bits_of(n):
    assert n & (n - 1) == 0
    return n.bit_length() - 1


def places(index, width):
    return lax.shift_right_arithmetic(index, bits_of(width)), lax.bitwise_and(index, width - 1)


def cell_gather(fields, row, lane):
    rows, lanes = fields[0].shape
    pick = ones_of(hot(lane, lanes))
    pick = jnp.concatenate([pick, pick], axis=0)
    at_row = hot(row, rows)
    found = []
    for field in fields:
        both = jnp.concatenate([part.astype(BF16) for part in halves(field)], axis=1)
        found.append(jnp.sum(jnp.where(at_row, nn(both, pick), 0.0), axis=0, keepdims=True))
    return found


def cell_scatter(value, row, lane, rows, lanes):
    spread = jnp.where(hot(lane, lanes), value, 0.0)
    spread = jnp.concatenate([part.astype(BF16) for part in halves(spread)], axis=0)
    total = nt(ones_of(hot(row, rows)), spread)
    return total[:, :lanes] + total[:, lanes:]


def well_scatter(values, row, lane, rows):
    mine = hot(row, rows)
    stack = []
    for value in values:
        stack.extend(halves(jnp.where(mine, value, 0.0)))
    total = nt(jnp.concatenate(stack, axis=0).astype(BF16), ones_of(hot(lane, LANES)))
    return [
        total[2 * i * rows : (2 * i + 1) * rows] + total[(2 * i + 1) * rows : (2 * i + 2) * rows]
        for i in range(len(values))
    ]


def well_gather(field, row, lane):
    rows = field.shape[0]
    both = jnp.concatenate(halves(field), axis=0).astype(BF16)
    found = nn(both, ones_of(hot(lane, LANES)))
    return jnp.sum(
        jnp.where(hot(row, rows), found[:rows] + found[rows:], 0.0), axis=0, keepdims=True
    )


def total_mobility(sat_water, sat_gas):
    sat_oil = 1.0 - sat_water - sat_gas
    return 0.5 * sat_oil * sat_oil + sat_water * sat_water + 5.0 * (sat_gas * sat_gas)


def phase_mobility(pressure, sat_water, sat_gas):
    sat_oil = 1.0 - sat_water - sat_gas
    b_oil = 1.0 + COMP_OIL * (pressure - 1.0)
    b_water = 1.0 + COMP_WATER * (pressure - 1.0)
    return (
        sat_oil * sat_oil * b_oil * 0.5,
        sat_water * sat_water * b_water,
        sat_gas * sat_gas * pressure * 5.0,
    )


def live_index(well_ref, index_ref):
    return jnp.where(well_ref[...] >= 0, index_ref[...], 0.0)


def first_wells(press_ref, sat_ref, cell_ref, well_ref, index_ref, mode_ref, target_ref, out_ref):
    layers, width, lanes = press_ref.shape
    rows = layers * width
    owned = mode_ref.shape[1]
    group = LANES // owned
    me = lax.axis_index(AXES)
    row, lane = places(cell_ref[...], lanes)
    well_row, well_lane = places(well_ref[...], LANES)
    sat = sat_ref[...].reshape(2, rows, lanes)
    mobility = total_mobility(sat[0], sat[1])
    press = press_ref[...].reshape(rows, lanes)
    at_mob, at_press = cell_gather([mobility, mobility * press], row, lane)
    index = live_index(well_ref, index_ref)
    chunk_rows = first_rows(out_ref)
    well_rows = (chunk_rows - 2) // 2
    part, base = well_scatter([index * at_press, index * at_mob], well_row, well_lane, well_rows)
    here = lax.shift_right_logical(iota((1, LANES), 1), bits_of(owned)) == lax.rem(me, group)
    controls = [
        jnp.where(here, jnp.concatenate([ref[...].astype(F32)] * group, axis=1), 0.0)
        for ref in (mode_ref, target_ref)
    ]
    block = jnp.concatenate([part, base] + controls, axis=0)
    block = jnp.concatenate([block] * 4, axis=0)
    height = block.shape[0]
    for i in range(out_ref.shape[0] // height):
        out_ref[i * height : (i + 1) * height, :] = block


def first_rows(out_ref):
    count = lax.axis_size("gx") * lax.axis_size("gy")
    return out_ref.shape[0] // count


def pack(after_ref, press_ref, sat_ref, perm_ref, depth_ref, flag_ref, xup_ref, xdn_ref, yup_ref, ydn_ref):
    layers, width, lanes = press_ref.shape
    rows = layers * width
    flags = flag_ref[...]
    bit_y = lax.bitwise_and(lax.shift_right_logical(flags, 1), 1).astype(F32)
    last = width - 1
    for edge, out_ref in ((last, xup_ref), (0, xdn_ref)):
        fields = [
            press_ref[:, edge, :],
            sat_ref[0, :, edge, :],
            sat_ref[1, :, edge, :],
            perm_ref[0, :, edge, :],
            depth_ref[:, edge, :],
            lax.bitwise_and(flag_ref[:, edge, :], 1).astype(F32),
        ]
        for i, field in enumerate(fields):
            out_ref[i * layers : (i + 1) * layers, :] = field
    planes = [press_ref[...], sat_ref[0], sat_ref[1], perm_ref[1], depth_ref[...], bit_y]
    pick_row, pick_lane = iota((2 * EDGE, 2 * lanes), 0), lax.rem(iota((2 * EDGE, 2 * lanes), 1), lanes)
    total = jnp.zeros((2 * EDGE, rows), F32)
    for i, plane in enumerate(planes):
        both = jnp.concatenate([part.astype(BF16) for part in halves(plane.reshape(rows, lanes))], axis=1)
        pick = ones_of(
            ((pick_row == i) & (pick_lane == lanes - 1)) | ((pick_row == EDGE + i) & (pick_lane == 0))
        )
        total = total + nt(pick, both)
    yup_ref[...] = total[:EDGE]
    ydn_ref[...] = total[EDGE:]


def upright(rows_list, lanes):
    stack = jnp.concatenate(rows_list, axis=0)
    stack = jnp.concatenate([stack, jnp.zeros((lanes - stack.shape[0], stack.shape[1]), F32)], axis=0)
    return jnp.transpose(stack)


def faces(perm, perm_next, mob, mob_next, first_up):
    transmit = 2.0 * perm * perm_next / (perm + perm_next)
    return [transmit * jnp.where(first_up, a, b) for a, b in zip(mob, mob_next)]


def main_terms(
    press_ref, sat_ref, perm_ref, pore_ref, depth_ref, res_ref, flag_ref, cell_ref, well_ref, index_ref,
    xup_ref, xdn_ref, yup_ref, ydn_ref,
    coup_ref, rhs_ref, gain_ref, start_ref, mob_ref,
    side_ref, share_ref,
):
    layers, width, lanes = press_ref.shape
    rows = layers * width
    row, lane = places(cell_ref[...], lanes)
    share_ref[...] = cell_scatter(live_index(well_ref, index_ref), row, lane, rows, lanes)
    stand = upright([yup_ref[...], ydn_ref[...]], lanes)
    stand = jnp.concatenate([part.astype(BF16) for part in halves(stand)], axis=1)
    wide = (2 * lanes, PLANES * lanes)
    from_lane = lax.rem(iota(wide, 0), lanes)
    to_plane, to_lane = places(iota(wide, 1), lanes)
    side_ref[...] = nn(
        stand,
        ones_of(
            ((from_lane == to_plane) & (to_lane == 0))
            | ((from_lane == to_plane + EDGE) & (to_lane == lanes - 1))
        ),
    )
    sub = iota((width, lanes), 0)
    along = iota((width, lanes), 1)
    x_first, x_last = sub == 0, sub == width - 1
    y_first, y_last = along == 0, along == lanes - 1

    def x_next(a, edge):
        return jnp.where(x_last, edge, pltpu.roll(a, width - 1, 0))

    def x_prev(a, edge):
        return jnp.where(x_first, edge, pltpu.roll(a, 1, 0))

    def y_next(a, edge):
        return jnp.where(y_last, edge, pltpu.roll(a, lanes - 1, 1))

    def y_prev(a, edge):
        return jnp.where(y_first, edge, pltpu.roll(a, 1, 1))

    def layer(z):
        press = press_ref[z]
        return press, phase_mobility(press, sat_ref[0, z], sat_ref[1, z])

    this = layer(0)
    before = None
    for z in range(layers):
        press, mob = this
        following = layer(z + 1) if z + 1 < layers else None
        sat_water, sat_gas = sat_ref[0, z], sat_ref[1, z]
        sat_oil = 1.0 - sat_water - sat_gas
        depth = depth_ref[z]
        flags = flag_ref[z]
        w_oil = 1.0 / (1.0 + COMP_OIL * (press - 1.0))
        w_water = 1.0 / (1.0 + COMP_WATER * (press - 1.0))
        w_gas = 1.0 / press
        storage = pore_ref[z] * (
            sat_oil * COMP_OIL * w_oil + sat_water * COMP_WATER * w_water + sat_gas * w_gas
        )
        couplings, besides, gravity = [], [], jnp.zeros_like(press)

        def add(flux, drop, beside):
            nonlocal gravity
            oil, water, gas = w_oil * flux[0], w_water * flux[1], w_gas * flux[2]
            couplings.append(oil + water + gas)
            gravity = gravity + (GRAV_OIL * oil + GRAV_WATER * water + GRAV_GAS * gas) * drop
            besides.append(beside)

        perm = perm_ref[0, z]
        up = [xup_ref[i * layers + z : i * layers + z + 1, :] for i in range(PLANES)]
        dn = [xdn_ref[i * layers + z : i * layers + z + 1, :] for i in range(PLANES)]
        mob_up, mob_dn = phase_mobility(*up[:3]), phase_mobility(*dn[:3])
        bit = lax.bitwise_and(flags, 1) > 0
        flux = faces(
            perm, x_next(perm, dn[3]), mob, [x_next(a, b) for a, b in zip(mob, mob_dn)], bit
        )
        drop = depth - x_next(depth, dn[4])
        add(flux, drop, x_next(press, dn[0]))
        edge = faces(up[3], perm[:1], mob_up, [a[:1] for a in mob], up[5] > 0.5)
        add(
            [x_prev(a, b) for a, b in zip(flux, edge)],
            -x_prev(drop, up[4] - depth[:1]),
            x_prev(press, up[0]),
        )
        perm = perm_ref[1, z]
        side = [
            side_ref[z * width : (z + 1) * width, i * lanes : (i + 1) * lanes] for i in range(PLANES)
        ]
        mob_side = phase_mobility(*side[:3])
        bit = lax.bitwise_and(flags, 2) > 0
        flux = faces(
            perm, y_next(perm, side[3]), mob, [y_next(a, b) for a, b in zip(mob, mob_side)], bit
        )
        drop = depth - y_next(depth, side[4])
        add(flux, drop, y_next(press, side[0]))
        edge = faces(side[3], perm, mob_side, mob, side[5] > 0.5)
        add(
            [y_prev(a, b) for a, b in zip(flux, edge)],
            -y_prev(drop, side[4] - depth),
            y_prev(press, side[0]),
        )
        if following is not None:
            bit = lax.bitwise_and(flags, 4) > 0
            flux = faces(perm_ref[2, z], perm_ref[2, z + 1], mob, following[1], bit)
            drop = depth - depth_ref[z + 1]
            add(flux, drop, following[0])
            after = (flux, drop, press)
        else:
            coup_ref[4, z] = jnp.zeros_like(press)
            after = None
        if before is not None:
            add(before[0], -before[1], before[2])
        else:
            coup_ref[5, z] = jnp.zeros_like(press)
        names = [0, 1, 2, 3] + ([4] if following is not None else []) + ([5] if before is not None else [])
        mobility = total_mobility(sat_water, sat_gas)
        diag = storage + mobility * share_ref[z * width : (z + 1) * width, :]
        for coupling in couplings:
            diag = diag + coupling
        scale = RELAXATION / diag
        rhs = (
            storage * press
            - (w_oil * res_ref[0, z] + w_water * res_ref[1, z] + w_gas * res_ref[2, z])
            + gravity
        )
        rhs = scale * rhs
        start = (1.0 - RELAXATION) * press + rhs
        for name, coupling, beside in zip(names, couplings, besides):
            scaled = scale * coupling
            coup_ref[name, z] = scaled
            start = start + scaled * beside
        rhs_ref[z] = rhs
        gain_ref[z] = scale * mobility
        start_ref[z] = start
        mob_ref[z] = mobility
        before, this = after, following


def slot_bhp(bhp, well_ref, index_ref):
    well_row, well_lane = places(well_ref[...], LANES)
    return live_index(well_ref, index_ref) * well_gather(bhp, well_row, well_lane)


def first_update(
    sums_ref, cell_ref, well_ref, index_ref, start_ref, gain_ref, mob_ref,
    cur_ref, out_ref, xup_ref, xdn_ref, known_ref,
):
    layers, width, lanes = start_ref.shape
    rows = layers * width
    count = lax.axis_size("gx") * lax.axis_size("gy")
    chunk = sums_ref.shape[0] // count
    well_rows = (chunk - 2) // 2
    group = count // well_rows
    my = lax.axis_index("gy")
    part = sums_ref[0:well_rows, :]
    base = sums_ref[well_rows : 2 * well_rows, :]
    for d in range(1, count):
        part = part + sums_ref[d * chunk : d * chunk + well_rows, :]
        base = base + sums_ref[d * chunk + well_rows : d * chunk + 2 * well_rows, :]
    controls = []
    for k in (2 * well_rows, 2 * well_rows + 1):
        total = sums_ref[pl.ds(k, well_rows, stride=group * chunk), :]
        for j in range(1, group):
            total = total + sums_ref[pl.ds(j * chunk + k, well_rows, stride=group * chunk), :]
        controls.append(total)
    mode, target = controls
    bhp = jnp.where(mode < 0.5, target, (part - target) / base)
    known_ref[0] = mode
    known_ref[1] = target
    known_ref[2] = base
    row, lane = places(cell_ref[...], lanes)
    well_row, well_lane = places(well_ref[...], LANES)
    push = cell_scatter(slot_bhp(bhp, well_ref, index_ref), row, lane, rows, lanes)
    start = start_ref[...].reshape(rows, lanes)
    gain = gain_ref[...].reshape(rows, lanes)
    current = start + gain * push
    cur_ref[...] = current.reshape(layers, width, lanes)
    xup_ref[...] = cur_ref[:, width - 1, :]
    xdn_ref[...] = cur_ref[:, 0, :]
    (at_cell,) = cell_gather([mob_ref[...].reshape(rows, lanes) * current], row, lane)
    (part,) = well_scatter([live_index(well_ref, index_ref) * at_cell], well_row, well_lane, well_rows)
    both = jnp.concatenate([half.astype(BF16) for half in halves(current)], axis=1)
    pick_row, pick_lane = iota((2 * EDGE, 2 * lanes), 0), lax.rem(iota((2 * EDGE, 2 * lanes), 1), lanes)
    rims = nt(
        ones_of(((pick_row == 0) & (pick_lane == lanes - 1)) | ((pick_row == 1) & (pick_lane == 0))), both
    )
    pieces = rows // LANES
    split = [
        jnp.concatenate([rims[r : r + 1, i * LANES : (i + 1) * LANES] for i in range(pieces)], axis=0)
        for r in range(2)
    ]
    height = well_rows + pieces
    ends = lax.axis_size("gy")
    for d in range(count):
        out_ref[d * height : d * height + well_rows, :] = part
        out_ref[d * height + well_rows : (d + 1) * height, :] = jnp.where(
            d % ends > my, split[0], split[1]
        )


def last_update(
    sums_ref, known_ref, cell_ref, well_ref, index_ref, cur_ref, coup_ref, rhs_ref, gain_ref,
    xup_ref, xdn_ref, out_ref, bhp_ref, push_ref, side_ref,
):
    layers, width, lanes = cur_ref.shape
    rows = layers * width
    count = lax.axis_size("gx") * lax.axis_size("gy")
    height = sums_ref.shape[0] // count
    well_rows = known_ref.shape[1]
    pieces = height - well_rows
    me = lax.axis_index(AXES)
    part = sums_ref[0:well_rows, :]
    for d in range(1, count):
        part = part + sums_ref[d * height : d * height + well_rows, :]
    bhp = jnp.where(known_ref[0] < 0.5, known_ref[1], (part - known_ref[1]) / known_ref[2])
    owned = bhp_ref.shape[1]
    group = LANES // owned
    line = jnp.sum(
        jnp.where(iota(bhp.shape, 0) == me // group, bhp, 0.0), axis=0, keepdims=True
    )
    line = pltpu.roll(line, lax.rem(LANES - lax.rem(me, group) * owned, LANES), 1)
    bhp_ref[...] = line[:, :owned]
    row, lane = places(cell_ref[...], lanes)
    push_ref[...] = cell_scatter(slot_bhp(bhp, well_ref, index_ref), row, lane, rows, lanes)
    strips = []
    for beside in (jnp.maximum(me - 1, 0), jnp.minimum(me + 1, count - 1)):
        strips.append(
            jnp.concatenate(
                [sums_ref[pl.ds(beside * height + well_rows + i, 1), :] for i in range(pieces)], axis=1
            )
        )
    side_ref[...] = upright(strips, lanes)
    sub = iota((width, lanes), 0)
    along = iota((width, lanes), 1)
    for z in range(layers):
        here = slice(z * width, (z + 1) * width)
        current = cur_ref[z]
        side = side_ref[here, :]
        besides = [
            jnp.where(sub == width - 1, xdn_ref[z : z + 1, :], pltpu.roll(current, width - 1, 0)),
            jnp.where(sub == 0, xup_ref[z : z + 1, :], pltpu.roll(current, 1, 0)),
            jnp.where(along == lanes - 1, pltpu.roll(side, lanes - 2, 1), pltpu.roll(current, lanes - 1, 1)),
            jnp.where(along == 0, side, pltpu.roll(current, 1, 1)),
            cur_ref[z + 1] if z + 1 < layers else None,
            cur_ref[z - 1] if z > 0 else None,
        ]
        total = (1.0 - RELAXATION) * current + rhs_ref[z] + gain_ref[z] * push_ref[here, :]
        for i, beside in enumerate(besides):
            if beside is not None:
                total = total + coup_ref[i, z] * beside
        out_ref[z] = total


def call(kernel, out_shapes, args, scratch=(), flops=1_000_000):
    shapes = [jax.ShapeDtypeStruct(s, F32) for s in out_shapes]
    return pl.pallas_call(
        kernel,
        out_shape=shapes,
        in_specs=[pl.BlockSpec(memory_space=pltpu.VMEM)] * len(args),
        out_specs=[pl.BlockSpec(memory_space=pltpu.VMEM)] * len(shapes),
        scratch_shapes=[pltpu.VMEM(s, F32) for s in scratch],
        compiler_params=pltpu.CompilerParams(vmem_limit_bytes=32 * 1024 * 1024),
        cost_estimate=pl.CostEstimate(flops=flops, bytes_accessed=4_000_000, transcendentals=0),
    )(*args)


def everyone(rows, count):
    height = rows.shape[0] // count
    swapped = lax.all_to_all(rows.reshape(count, height, 1, LANES), AXES, 0, 0, tiled=True)
    return swapped.reshape(rows.shape)


def shifted(up, down, axis):
    count = lax.axis_size(axis)
    return (
        lax.ppermute(up, axis, [(i, i + 1) for i in range(count - 1)]),
        lax.ppermute(down, axis, [(i + 1, i) for i in range(count - 1)]),
    )


def body(
    pressure, saturation, permeability, pore_volume, cell_depth, residual, upstream_flags,
    perf_cell, perf_well, perf_index, well_mode, well_target,
):
    layers, width, lanes = pressure.shape
    rows = layers * width
    count = lax.axis_size("gx") * lax.axis_size("gy")
    owned = well_mode.shape[0]
    well_rows = owned * count // LANES
    chunk = 2 * well_rows + 2
    (sums,) = call(
        first_wells,
        [(count * chunk, LANES)],
        [pressure, saturation, perf_cell, perf_well, perf_index, well_mode[None], well_target[None]],
    )
    gathered = everyone(sums, count)
    xup, xdn, yup, ydn = call(
        pack,
        [(PLANES * layers, lanes)] * 2 + [(EDGE, rows)] * 2,
        [sums[:8], pressure, saturation, permeability, cell_depth, upstream_flags],
    )
    xup, xdn = shifted(xup, xdn, "gx")
    yup, ydn = shifted(yup, ydn, "gy")
    grid = (layers, width, lanes)
    coup, rhs, gain, start, mobility = call(
        main_terms,
        [(6,) + grid, grid, grid, grid, grid],
        [
            pressure, saturation, permeability, pore_volume, cell_depth, residual, upstream_flags,
            perf_cell, perf_well, perf_index, xup, xdn, yup, ydn,
        ],
        [(rows, PLANES * lanes), (rows, lanes)],
    )
    pieces = rows // LANES
    current, sums, xup, xdn, known = call(
        first_update,
        [grid, (count * (well_rows + pieces), LANES), (layers, lanes), (layers, lanes), (3, well_rows, LANES)],
        [gathered, perf_cell, perf_well, perf_index, start, gain, mobility],
    )
    gathered = everyone(sums, count)
    xup, xdn = shifted(xup, xdn, "gx")
    out, bhp = call(
        last_update,
        [grid, (1, owned)],
        [gathered, known, perf_cell, perf_well, perf_index, current, coup, rhs, gain, xup, xdn],
        [(rows, lanes), (rows, lanes)],
    )
    return out, bhp[0]


def solution(mesh):
    return jax.shard_map(
        body,
        mesh=mesh,
        in_specs=(
            P(None, "gx", "gy"),
            P(None, None, "gx", "gy"),
            P(None, None, "gx", "gy"),
            P(None, "gx", "gy"),
            P(None, "gx", "gy"),
            P(None, None, "gx", "gy"),
            P(None, "gx", "gy"),
            P(("gx", "gy"), None),
            P(("gx", "gy"), None),
            P(("gx", "gy"), None),
            P(("gx", "gy")),
            P(("gx", "gy")),
        ),
        out_specs=(P(None, "gx", "gy"), P(("gx", "gy"))),
        check_vma=False,
    )
```

```python
import jax
import jax.numpy as jnp
from jax import lax
from jax.experimental import pallas as pl
from jax.experimental.pallas import tpu as pltpu
from jax.sharding import PartitionSpec as P

COMP_OIL = 0.2
COMP_WATER = 0.05
GRAV_OIL = 0.4
GRAV_WATER = 0.5
GRAV_GAS = 0.08
RELAXATION = 0.8
LANES = 128
PLANES = 6
FIELDS = 7
EDGE = 8

F32 = jnp.float32
BF16 = jnp.bfloat16
AXES = ("gx", "gy")


def nn(a, b):
    return lax.dot_general(a, b, (((1,), (0,)), ((), ())), preferred_element_type=F32)


def nt(a, b):
    return lax.dot_general(a, b, (((1,), (1,)), ((), ())), preferred_element_type=F32)


def halves(x):
    high = x.astype(BF16).astype(F32)
    return high, x - high


def iota(shape, dim):
    return lax.broadcasted_iota(jnp.int32, shape, dim)


def hot(index, count):
    return iota((count, index.shape[1]), 0) == index


def ones_of(mask):
    return jnp.where(mask, 1.0, 0.0).astype(BF16)


def bits_of(n):
    assert n & (n - 1) == 0
    return n.bit_length() - 1


def places(index, width):
    return lax.shift_right_arithmetic(index, bits_of(width)), lax.bitwise_and(index, width - 1)


def cell_gather(fields, row, lane):
    rows, lanes = fields[0].shape
    pick = ones_of(hot(lane, lanes))
    pick = jnp.concatenate([pick, pick], axis=0)
    at_row = hot(row, rows)
    found = []
    for field in fields:
        both = jnp.concatenate([part.astype(BF16) for part in halves(field)], axis=1)
        found.append(jnp.sum(jnp.where(at_row, nn(both, pick), 0.0), axis=0, keepdims=True))
    return found


def cell_scatter(value, row, lane, rows, lanes):
    spread = jnp.where(hot(lane, lanes), value, 0.0)
    spread = jnp.concatenate([part.astype(BF16) for part in halves(spread)], axis=0)
    total = nt(ones_of(hot(row, rows)), spread)
    return total[:, :lanes] + total[:, lanes:]


def well_scatter(values, row, lane, rows):
    mine = hot(row, rows)
    stack = []
    for value in values:
        stack.extend(halves(jnp.where(mine, value, 0.0)))
    total = nt(jnp.concatenate(stack, axis=0).astype(BF16), ones_of(hot(lane, LANES)))
    return [
        total[2 * i * rows : (2 * i + 1) * rows] + total[(2 * i + 1) * rows : (2 * i + 2) * rows]
        for i in range(len(values))
    ]


def well_gather(field, row, lane):
    rows = field.shape[0]
    both = jnp.concatenate(halves(field), axis=0).astype(BF16)
    found = nn(both, ones_of(hot(lane, LANES)))
    return jnp.sum(
        jnp.where(hot(row, rows), found[:rows] + found[rows:], 0.0), axis=0, keepdims=True
    )


def total_mobility(sat_water, sat_gas):
    sat_oil = 1.0 - sat_water - sat_gas
    return 0.5 * sat_oil * sat_oil + sat_water * sat_water + 5.0 * (sat_gas * sat_gas)


def phase_mobility(pressure, sat_water, sat_gas):
    sat_oil = 1.0 - sat_water - sat_gas
    b_oil = 1.0 + COMP_OIL * (pressure - 1.0)
    b_water = 1.0 + COMP_WATER * (pressure - 1.0)
    return (
        sat_oil * sat_oil * b_oil * 0.5,
        sat_water * sat_water * b_water,
        sat_gas * sat_gas * pressure * 5.0,
    )


def live_index(well_ref, index_ref):
    return jnp.where(well_ref[...] >= 0, index_ref[...], 0.0)


def fetch(sources, holds, sems):
    copies = [
        pltpu.make_async_copy(source, hold, sems.at[i])
        for i, (source, hold) in enumerate(zip(sources, holds))
    ]
    for copy in copies:
        copy.start()
    return copies


def first_wells(*refs):
    count = (len(refs) - 2) // 2
    sources, out_ref, holds, sems = refs[:count], refs[count], refs[count + 1 : -1], refs[-1]
    for copy in fetch(sources, holds, sems):
        copy.wait()
    press_ref, sat_ref, cell_ref, well_ref, index_ref, mode_ref, target_ref = holds
    layers, width, lanes = press_ref.shape
    rows = layers * width
    owned = mode_ref.shape[1]
    group = LANES // owned
    me = lax.axis_index(AXES)
    row, lane = places(cell_ref[...], lanes)
    well_row, well_lane = places(well_ref[...], LANES)
    sat = sat_ref[...].reshape(2, rows, lanes)
    mobility = total_mobility(sat[0], sat[1])
    press = press_ref[...].reshape(rows, lanes)
    at_mob, at_press = cell_gather([mobility, mobility * press], row, lane)
    index = live_index(well_ref, index_ref)
    chunk_rows = first_rows(out_ref)
    well_rows = (chunk_rows - 2) // 2
    part, base = well_scatter([index * at_press, index * at_mob], well_row, well_lane, well_rows)
    here = lax.shift_right_logical(iota((1, LANES), 1), bits_of(owned)) == lax.rem(me, group)
    controls = [
        jnp.where(here, jnp.concatenate([ref[...].astype(F32)] * group, axis=1), 0.0)
        for ref in (mode_ref, target_ref)
    ]
    block = jnp.concatenate([part, base] + controls, axis=0)
    block = jnp.concatenate([block] * 4, axis=0)
    height = block.shape[0]
    for i in range(out_ref.shape[0] // height):
        out_ref[i * height : (i + 1) * height, :] = block


def first_rows(out_ref):
    count = lax.axis_size("gx") * lax.axis_size("gy")
    return out_ref.shape[0] // count


def is_even(axis):
    return lax.rem(lax.axis_index(axis), 2) == 0


def pack(
    after_ref, press_ref, sat_ref, perm_ref, depth_ref, source_ref, xa_ref, xb_ref, ya_ref, yb_ref, flag_ref, sem
):
    layers, width, lanes = press_ref.shape
    rows = layers * width
    copy = pltpu.make_async_copy(source_ref, flag_ref, sem)
    copy.start()
    pick_row, pick_lane = iota((2 * EDGE, 2 * lanes), 0), lax.rem(iota((2 * EDGE, 2 * lanes), 1), lanes)

    def rim(i, plane):
        both = jnp.concatenate([part.astype(BF16) for part in halves(plane.reshape(rows, lanes))], axis=1)
        pick = ones_of(
            ((pick_row == i) & (pick_lane == lanes - 1)) | ((pick_row == EDGE + i) & (pick_lane == 0))
        )
        return nt(pick, both)

    total = rim(0, press_ref[...])
    for i, plane in enumerate([sat_ref[0], sat_ref[1], perm_ref[1], depth_ref[...]]):
        total = total + rim(i + 1, plane)
    copy.wait()
    bit_y = lax.bitwise_and(lax.shift_right_logical(flag_ref[...], 1), 1).astype(F32)
    total = total + rim(PLANES - 1, bit_y)
    last = width - 1
    x_even, y_even = is_even("gx"), is_even("gy")
    ends = [
        [
            press_ref[:, edge, :],
            sat_ref[0, :, edge, :],
            sat_ref[1, :, edge, :],
            perm_ref[0, :, edge, :],
            depth_ref[:, edge, :],
            lax.bitwise_and(flag_ref[:, edge, :], 1).astype(F32),
        ]
        for edge in (last, 0)
    ]
    for i, (high, low) in enumerate(zip(*ends)):
        xa_ref[i * layers : (i + 1) * layers, :] = jnp.where(x_even, high, low)
        xb_ref[i * layers : (i + 1) * layers, :] = jnp.where(x_even, low, high)
    ya_ref[...] = jnp.where(y_even, total[:EDGE], total[EDGE:])
    yb_ref[...] = jnp.where(y_even, total[EDGE:], total[:EDGE])


def upright(rows_list, lanes):
    stack = jnp.concatenate(rows_list, axis=0)
    stack = jnp.concatenate([stack, jnp.zeros((lanes - stack.shape[0], stack.shape[1]), F32)], axis=0)
    return jnp.transpose(stack)


def faces(perm, perm_next, mob, mob_next, first_up):
    transmit = 2.0 * perm * perm_next / (perm + perm_next)
    return [transmit * jnp.where(first_up, a, b) for a, b in zip(mob, mob_next)]


def main_terms(*refs):
    sources, refs, sems = refs[:FIELDS], refs[FIELDS:-1], refs[-1]
    refs, holds = refs[:-FIELDS], refs[-FIELDS:]
    press_ref, sat_ref, perm_ref, pore_ref, depth_ref, res_ref, flag_ref = holds
    copies = fetch(sources, holds, sems)
    (
        sums_ref, cell_ref, well_ref, index_ref, xa_ref, xb_ref, ya_ref, yb_ref,
        cur_ref, out_ref, oxa_ref, oxb_ref, known_ref, coup_ref, rhs_ref, gain_ref,
        start_ref, mob_ref, side_ref, share_ref, xup_ref, xdn_ref,
    ) = refs
    layers, width, lanes = press_ref.shape
    rows = layers * width
    row, lane = places(cell_ref[...], lanes)
    share_ref[...] = cell_scatter(live_index(well_ref, index_ref), row, lane, rows, lanes)
    x_even, y_even = is_even("gx"), is_even("gy")
    xup_ref[...] = jnp.where(x_even, xb_ref[...], xa_ref[...])
    xdn_ref[...] = jnp.where(x_even, xa_ref[...], xb_ref[...])
    ya, yb = ya_ref[...], yb_ref[...]
    stand = upright([jnp.where(y_even, yb, ya), jnp.where(y_even, ya, yb)], lanes)
    stand = jnp.concatenate([part.astype(BF16) for part in halves(stand)], axis=1)
    wide = (2 * lanes, PLANES * lanes)
    from_lane = lax.rem(iota(wide, 0), lanes)
    to_plane, to_lane = places(iota(wide, 1), lanes)
    side_ref[...] = nn(
        stand,
        ones_of(
            ((from_lane == to_plane) & (to_lane == 0))
            | ((from_lane == to_plane + EDGE) & (to_lane == lanes - 1))
        ),
    )
    for copy in copies:
        copy.wait()
    sub = iota((width, lanes), 0)
    along = iota((width, lanes), 1)
    x_first, x_last = sub == 0, sub == width - 1
    y_first, y_last = along == 0, along == lanes - 1

    def x_next(a, edge):
        return jnp.where(x_last, edge, pltpu.roll(a, width - 1, 0))

    def x_prev(a, edge):
        return jnp.where(x_first, edge, pltpu.roll(a, 1, 0))

    def y_next(a, edge):
        return jnp.where(y_last, edge, pltpu.roll(a, lanes - 1, 1))

    def y_prev(a, edge):
        return jnp.where(y_first, edge, pltpu.roll(a, 1, 1))

    def layer(z):
        press = press_ref[z]
        return press, phase_mobility(press, sat_ref[0, z], sat_ref[1, z])

    this = layer(0)
    before = None
    for z in range(layers):
        press, mob = this
        following = layer(z + 1) if z + 1 < layers else None
        sat_water, sat_gas = sat_ref[0, z], sat_ref[1, z]
        sat_oil = 1.0 - sat_water - sat_gas
        depth = depth_ref[z]
        flags = flag_ref[z]
        w_oil = 1.0 / (1.0 + COMP_OIL * (press - 1.0))
        w_water = 1.0 / (1.0 + COMP_WATER * (press - 1.0))
        w_gas = 1.0 / press
        storage = pore_ref[z] * (
            sat_oil * COMP_OIL * w_oil + sat_water * COMP_WATER * w_water + sat_gas * w_gas
        )
        couplings, besides, gravity = [], [], jnp.zeros_like(press)

        def add(flux, drop, beside):
            nonlocal gravity
            oil, water, gas = w_oil * flux[0], w_water * flux[1], w_gas * flux[2]
            couplings.append(oil + water + gas)
            gravity = gravity + (GRAV_OIL * oil + GRAV_WATER * water + GRAV_GAS * gas) * drop
            besides.append(beside)

        perm = perm_ref[0, z]
        up = [xup_ref[i * layers + z : i * layers + z + 1, :] for i in range(PLANES)]
        dn = [xdn_ref[i * layers + z : i * layers + z + 1, :] for i in range(PLANES)]
        mob_up, mob_dn = phase_mobility(*up[:3]), phase_mobility(*dn[:3])
        bit = lax.bitwise_and(flags, 1) > 0
        flux = faces(
            perm, x_next(perm, dn[3]), mob, [x_next(a, b) for a, b in zip(mob, mob_dn)], bit
        )
        drop = depth - x_next(depth, dn[4])
        add(flux, drop, x_next(press, dn[0]))
        edge = faces(up[3], perm[:1], mob_up, [a[:1] for a in mob], up[5] > 0.5)
        add(
            [x_prev(a, b) for a, b in zip(flux, edge)],
            -x_prev(drop, up[4] - depth[:1]),
            x_prev(press, up[0]),
        )
        perm = perm_ref[1, z]
        side = [
            side_ref[z * width : (z + 1) * width, i * lanes : (i + 1) * lanes] for i in range(PLANES)
        ]
        mob_side = phase_mobility(*side[:3])
        bit = lax.bitwise_and(flags, 2) > 0
        flux = faces(
            perm, y_next(perm, side[3]), mob, [y_next(a, b) for a, b in zip(mob, mob_side)], bit
        )
        drop = depth - y_next(depth, side[4])
        add(flux, drop, y_next(press, side[0]))
        edge = faces(side[3], perm, mob_side, mob, side[5] > 0.5)
        add(
            [y_prev(a, b) for a, b in zip(flux, edge)],
            -y_prev(drop, side[4] - depth),
            y_prev(press, side[0]),
        )
        if following is not None:
            bit = lax.bitwise_and(flags, 4) > 0
            flux = faces(perm_ref[2, z], perm_ref[2, z + 1], mob, following[1], bit)
            drop = depth - depth_ref[z + 1]
            add(flux, drop, following[0])
            after = (flux, drop, press)
        else:
            coup_ref[4, z] = jnp.zeros_like(press)
            after = None
        if before is not None:
            add(before[0], -before[1], before[2])
        else:
            coup_ref[5, z] = jnp.zeros_like(press)
        names = [0, 1, 2, 3] + ([4] if following is not None else []) + ([5] if before is not None else [])
        mobility = total_mobility(sat_water, sat_gas)
        diag = storage + mobility * share_ref[z * width : (z + 1) * width, :]
        for coupling in couplings:
            diag = diag + coupling
        scale = RELAXATION / diag
        rhs = (
            storage * press
            - (w_oil * res_ref[0, z] + w_water * res_ref[1, z] + w_gas * res_ref[2, z])
            + gravity
        )
        rhs = scale * rhs
        start = (1.0 - RELAXATION) * press + rhs
        for name, coupling, beside in zip(names, couplings, besides):
            scaled = scale * coupling
            coup_ref[name, z] = scaled
            start = start + scaled * beside
        rhs_ref[z] = rhs
        gain_ref[z] = scale * mobility
        start_ref[z] = start
        mob_ref[z] = mobility
        before, this = after, following
    first_update(
        sums_ref, cell_ref, well_ref, index_ref, start_ref, gain_ref, mob_ref,
        cur_ref, out_ref, oxa_ref, oxb_ref, known_ref,
    )


def slot_bhp(bhp, well_ref, index_ref):
    well_row, well_lane = places(well_ref[...], LANES)
    return live_index(well_ref, index_ref) * well_gather(bhp, well_row, well_lane)


def first_update(
    sums_ref, cell_ref, well_ref, index_ref, start_ref, gain_ref, mob_ref,
    cur_ref, out_ref, xa_ref, xb_ref, known_ref,
):
    layers, width, lanes = start_ref.shape
    rows = layers * width
    count = lax.axis_size("gx") * lax.axis_size("gy")
    chunk = sums_ref.shape[0] // count
    well_rows = (chunk - 2) // 2
    group = count // well_rows
    my = lax.axis_index("gy")
    part = sums_ref[0:well_rows, :]
    base = sums_ref[well_rows : 2 * well_rows, :]
    for d in range(1, count):
        part = part + sums_ref[d * chunk : d * chunk + well_rows, :]
        base = base + sums_ref[d * chunk + well_rows : d * chunk + 2 * well_rows, :]
    controls = []
    for k in (2 * well_rows, 2 * well_rows + 1):
        total = sums_ref[pl.ds(k, well_rows, stride=group * chunk), :]
        for j in range(1, group):
            total = total + sums_ref[pl.ds(j * chunk + k, well_rows, stride=group * chunk), :]
        controls.append(total)
    mode, target = controls
    bhp = jnp.where(mode < 0.5, target, (part - target) / base)
    known_ref[0] = mode
    known_ref[1] = target
    known_ref[2] = base
    row, lane = places(cell_ref[...], lanes)
    well_row, well_lane = places(well_ref[...], LANES)
    push = cell_scatter(slot_bhp(bhp, well_ref, index_ref), row, lane, rows, lanes)
    start = start_ref[...].reshape(rows, lanes)
    gain = gain_ref[...].reshape(rows, lanes)
    current = start + gain * push
    cur_ref[...] = current.reshape(layers, width, lanes)
    x_even = is_even("gx")
    high, low = cur_ref[:, width - 1, :], cur_ref[:, 0, :]
    xa_ref[...] = jnp.where(x_even, high, low)
    xb_ref[...] = jnp.where(x_even, low, high)
    (at_cell,) = cell_gather([mob_ref[...].reshape(rows, lanes) * current], row, lane)
    (part,) = well_scatter([live_index(well_ref, index_ref) * at_cell], well_row, well_lane, well_rows)
    both = jnp.concatenate([half.astype(BF16) for half in halves(current)], axis=1)
    pick_row, pick_lane = iota((2 * EDGE, 2 * lanes), 0), lax.rem(iota((2 * EDGE, 2 * lanes), 1), lanes)
    rims = nt(
        ones_of(((pick_row == 0) & (pick_lane == lanes - 1)) | ((pick_row == 1) & (pick_lane == 0))), both
    )
    pieces = rows // LANES
    split = [
        jnp.concatenate([rims[r : r + 1, i * LANES : (i + 1) * LANES] for i in range(pieces)], axis=0)
        for r in range(2)
    ]
    height = well_rows + pieces
    ends = lax.axis_size("gy")
    for d in range(count):
        out_ref[d * height : d * height + well_rows, :] = part
        out_ref[d * height + well_rows : (d + 1) * height, :] = jnp.where(
            d % ends > my, split[0], split[1]
        )


def last_update(
    sums_ref, known_ref, cell_ref, well_ref, index_ref, cur_ref, coup_ref, rhs_ref, gain_ref,
    xa_ref, xb_ref, out_ref, bhp_ref, push_ref, side_ref, xup_ref, xdn_ref,
):
    layers, width, lanes = cur_ref.shape
    rows = layers * width
    count = lax.axis_size("gx") * lax.axis_size("gy")
    height = sums_ref.shape[0] // count
    well_rows = known_ref.shape[1]
    pieces = height - well_rows
    me = lax.axis_index(AXES)
    part = sums_ref[0:well_rows, :]
    for d in range(1, count):
        part = part + sums_ref[d * height : d * height + well_rows, :]
    bhp = jnp.where(known_ref[0] < 0.5, known_ref[1], (part - known_ref[1]) / known_ref[2])
    owned = bhp_ref.shape[1]
    group = LANES // owned
    line = jnp.sum(
        jnp.where(iota(bhp.shape, 0) == me // group, bhp, 0.0), axis=0, keepdims=True
    )
    line = pltpu.roll(line, lax.rem(LANES - lax.rem(me, group) * owned, LANES), 1)
    bhp_ref[...] = line[:, :owned]
    row, lane = places(cell_ref[...], lanes)
    push_ref[...] = cell_scatter(slot_bhp(bhp, well_ref, index_ref), row, lane, rows, lanes)
    strips = []
    for beside in (jnp.maximum(me - 1, 0), jnp.minimum(me + 1, count - 1)):
        strips.append(
            jnp.concatenate(
                [sums_ref[pl.ds(beside * height + well_rows + i, 1), :] for i in range(pieces)], axis=1
            )
        )
    side_ref[...] = upright(strips, lanes)
    x_even = is_even("gx")
    xup_ref[...] = jnp.where(x_even, xb_ref[...], xa_ref[...])
    xdn_ref[...] = jnp.where(x_even, xa_ref[...], xb_ref[...])
    sub = iota((width, lanes), 0)
    along = iota((width, lanes), 1)
    for z in range(layers):
        here = slice(z * width, (z + 1) * width)
        current = cur_ref[z]
        side = side_ref[here, :]
        besides = [
            jnp.where(sub == width - 1, xdn_ref[z : z + 1, :], pltpu.roll(current, width - 1, 0)),
            jnp.where(sub == 0, xup_ref[z : z + 1, :], pltpu.roll(current, 1, 0)),
            jnp.where(along == lanes - 1, pltpu.roll(side, lanes - 2, 1), pltpu.roll(current, lanes - 1, 1)),
            jnp.where(along == 0, side, pltpu.roll(current, 1, 1)),
            cur_ref[z + 1] if z + 1 < layers else None,
            cur_ref[z - 1] if z > 0 else None,
        ]
        total = (1.0 - RELAXATION) * current + rhs_ref[z] + gain_ref[z] * push_ref[here, :]
        for i, beside in enumerate(besides):
            if beside is not None:
                total = total + coup_ref[i, z] * beside
        out_ref[z] = total


def call(kernel, out_shapes, args, scratch=(), spaces=None, vmem=24):
    shapes = [jax.ShapeDtypeStruct(shape, F32) for shape in out_shapes]
    spaces = spaces or [pltpu.VMEM] * len(args)
    args = [
        pltpu.with_memory_space_constraint(arg, space) if space is pltpu.HBM else arg
        for arg, space in zip(args, spaces)
    ]
    return pl.pallas_call(
        kernel,
        out_shape=shapes,
        in_specs=[pl.BlockSpec(memory_space=space) for space in spaces],
        out_specs=[pl.BlockSpec(memory_space=pltpu.VMEM)] * len(shapes),
        scratch_shapes=[pltpu.VMEM(item, F32) if isinstance(item, tuple) else item for item in scratch],
        compiler_params=pltpu.CompilerParams(vmem_limit_bytes=vmem * 1024 * 1024),
        cost_estimate=pl.CostEstimate(flops=1_000_000, bytes_accessed=4_000_000, transcendentals=0),
    )(*args)


def everyone(rows, count):
    height = rows.shape[0] // count
    swapped = lax.all_to_all(rows.reshape(count, height, 1, LANES), AXES, 0, 0, tiled=True)
    return swapped.reshape(rows.shape)


def swapped(first, second, axis):
    count = lax.axis_size(axis)
    pairs = [(i, i ^ 1) for i in range(count) if i ^ 1 < count]
    others = [(i, i + 1 if i % 2 else i - 1) for i in range(count)]
    others = [(i, j) for i, j in others if 0 <= j < count]
    return lax.ppermute(first, axis, pairs), lax.ppermute(second, axis, others)


def body(
    pressure, saturation, permeability, pore_volume, cell_depth, residual, upstream_flags,
    perf_cell, perf_well, perf_index, well_mode, well_target,
):
    layers, width, lanes = pressure.shape
    rows = layers * width
    count = lax.axis_size("gx") * lax.axis_size("gy")
    owned = well_mode.shape[0]
    well_rows = owned * count // LANES
    chunk = 2 * well_rows + 2
    operands = [pressure, saturation, perf_cell, perf_well, perf_index, well_mode[None], well_target[None]]
    (sums,) = call(
        first_wells,
        [(count * chunk, LANES)],
        operands,
        [pltpu.VMEM(a.shape, a.dtype) for a in operands] + [pltpu.SemaphoreType.DMA((len(operands),))],
        [pltpu.HBM] * len(operands),
    )
    gathered = everyone(sums, count)
    xa, xb, ya, yb = call(
        pack,
        [(PLANES * layers, lanes)] * 2 + [(EDGE, rows)] * 2,
        [sums, pressure, saturation, permeability, cell_depth, upstream_flags],
        [pltpu.VMEM(upstream_flags.shape, upstream_flags.dtype), pltpu.SemaphoreType.DMA],
        [pl.ANY] + [pltpu.VMEM] * 4 + [pltpu.HBM],
    )
    xa, xb = swapped(xa, xb, "gx")
    ya, yb = swapped(ya, yb, "gy")
    grid = (layers, width, lanes)
    pieces = rows // LANES
    fields = [pressure, saturation, permeability, pore_volume, cell_depth, residual, upstream_flags]
    current, sums, xa, xb, known, coup, rhs, gain = call(
        main_terms,
        [
            grid, (count * (well_rows + pieces), LANES), (layers, lanes), (layers, lanes), (3, well_rows, LANES),
            (6,) + grid, grid, grid,
        ],
        fields + [gathered, perf_cell, perf_well, perf_index, xa, xb, ya, yb],
        [grid, grid, (rows, PLANES * lanes), (rows, lanes), (PLANES * layers, lanes), (PLANES * layers, lanes)]
        + [pltpu.VMEM(a.shape, a.dtype) for a in fields]
        + [pltpu.SemaphoreType.DMA((FIELDS,))],
        [pltpu.HBM] * FIELDS + [pltpu.VMEM] * 8,
    )
    gathered = everyone(sums, count)
    xa, xb = swapped(xa, xb, "gx")
    out, bhp = call(
        last_update,
        [grid, (1, owned)],
        [gathered, known, perf_cell, perf_well, perf_index, current, coup, rhs, gain, xa, xb],
        [(rows, lanes), (rows, lanes), (layers, lanes), (layers, lanes)],
    )
    return out, bhp[0]


def solution(mesh):
    return jax.shard_map(
        body,
        mesh=mesh,
        in_specs=(
            P(None, "gx", "gy"),
            P(None, None, "gx", "gy"),
            P(None, None, "gx", "gy"),
            P(None, "gx", "gy"),
            P(None, "gx", "gy"),
            P(None, None, "gx", "gy"),
            P(None, "gx", "gy"),
            P(("gx", "gy"), None),
            P(("gx", "gy"), None),
            P(("gx", "gy"), None),
            P(("gx", "gy")),
            P(("gx", "gy")),
        ),
        out_specs=(P(None, "gx", "gy"), P(("gx", "gy"))),
        check_vma=False,
    )
```

```python
import jax
import jax.numpy as jnp
from jax import lax
from jax.experimental import pallas as pl
from jax.experimental.pallas import tpu as pltpu
from jax.sharding import PartitionSpec as P

COMP_OIL = 0.2
COMP_WATER = 0.05
GRAV_OIL = 0.4
GRAV_WATER = 0.5
GRAV_GAS = 0.08
RELAXATION = 0.8
LANES = 128
PLANES = 6
INPUTS = 12
PRESS, SAT, PERM, DEPTH, PORE, RES, GRIDS = 0, 1, 3, 6, 7, 8, 11
DIAG, RHS, COUP, MOB, AROUND = 1, 2, 3, 9, 10
CURRENT, SCALE, GAIN = 0, 1, 10
EDGE = 8

F32 = jnp.float32
BF16 = jnp.bfloat16
AXES = ("gx", "gy")


def nn(a, b):
    return lax.dot_general(a, b, (((1,), (0,)), ((), ())), preferred_element_type=F32)


def nt(a, b):
    return lax.dot_general(a, b, (((1,), (1,)), ((), ())), preferred_element_type=F32)


def halves(x):
    high = x.astype(BF16).astype(F32)
    return high, x - high


def iota(shape, dim):
    return lax.broadcasted_iota(jnp.int32, shape, dim)


def hot(index, count):
    return iota((count, index.shape[1]), 0) == index


def ones_of(mask):
    return jnp.where(mask, 1.0, 0.0).astype(BF16)


def bits_of(n):
    assert n & (n - 1) == 0
    return n.bit_length() - 1


def places(index, width):
    return lax.shift_right_arithmetic(index, bits_of(width)), lax.bitwise_and(index, width - 1)


def cell_pick(row, lane, rows, lanes):
    pick = ones_of(hot(lane, lanes))
    return jnp.concatenate([pick, pick], axis=0), hot(row, rows)


def cell_find(field, pick, at_row):
    both = jnp.concatenate([part.astype(BF16) for part in halves(field)], axis=1)
    return jnp.sum(jnp.where(at_row, nn(both, pick), 0.0), axis=0, keepdims=True)


def cell_scatter(value, row, lane, rows, lanes):
    spread = jnp.where(hot(lane, lanes), value, 0.0)
    spread = jnp.concatenate([part.astype(BF16) for part in halves(spread)], axis=0)
    total = nt(ones_of(hot(row, rows)), spread)
    return total[:, :lanes] + total[:, lanes:]


def well_scatter(values, row, lane, rows):
    mine = hot(row, rows)
    stack = []
    for value in values:
        stack.extend(halves(jnp.where(mine, value, 0.0)))
    total = nt(jnp.concatenate(stack, axis=0).astype(BF16), ones_of(hot(lane, LANES)))
    return [
        total[2 * i * rows : (2 * i + 1) * rows] + total[(2 * i + 1) * rows : (2 * i + 2) * rows]
        for i in range(len(values))
    ]


def well_gather(field, row, lane):
    rows = field.shape[0]
    both = jnp.concatenate(halves(field), axis=0).astype(BF16)
    found = nn(both, ones_of(hot(lane, LANES)))
    return jnp.sum(
        jnp.where(hot(row, rows), found[:rows] + found[rows:], 0.0), axis=0, keepdims=True
    )


def total_mobility(sat_water, sat_gas):
    sat_oil = 1.0 - sat_water - sat_gas
    return 0.5 * sat_oil * sat_oil + sat_water * sat_water + 5.0 * (sat_gas * sat_gas)


def phase_mobility(pressure, sat_water, sat_gas):
    sat_oil = 1.0 - sat_water - sat_gas
    b_oil = 1.0 + COMP_OIL * (pressure - 1.0)
    b_water = 1.0 + COMP_WATER * (pressure - 1.0)
    return (
        sat_oil * sat_oil * b_oil * 0.5,
        sat_water * sat_water * b_water,
        sat_gas * sat_gas * pressure * 5.0,
    )


def live_index(well_ref, index_ref):
    return jnp.where(well_ref[...] >= 0, index_ref[...], 0.0)


def fetch(sources, holds, sems):
    copies = [
        pltpu.make_async_copy(source, hold, sems.at[i])
        for i, (source, hold) in enumerate(zip(sources, holds))
    ]
    for copy in copies:
        copy.start()
    return copies


def repeat_out(block_ref, out_ref, sem):
    height = block_ref.shape[0]
    copies = [
        pltpu.make_async_copy(block_ref, out_ref.at[pl.ds(i * height, height)], sem.at[i])
        for i in range(out_ref.shape[0] // height)
    ]
    for copy in copies:
        copy.start()
    return copies


def first_rows(out_ref):
    count = lax.axis_size("gx") * lax.axis_size("gy")
    return out_ref.shape[0] // count


def is_even(axis):
    return lax.rem(lax.axis_index(axis), 2) == 0


def opening(*refs):
    inputs, sems, out_sems = refs[:INPUTS], refs[-2], refs[-1]
    sums_ref, yb_ref, xb_ref, xa_ref, ya_ref, grid_ref, flag_ref = refs[INPUTS : INPUTS + 7]
    cell_ref, well_ref, index_ref, mode_ref, target_ref, block_ref = refs[INPUTS + 7 : -2]
    slot_refs = [cell_ref, well_ref, index_ref, mode_ref, target_ref]
    sat_ref, perm_ref = grid_ref.at[SAT : SAT + 2], grid_ref.at[PERM : PERM + 3]
    holds = slot_refs + [
        sat_ref, grid_ref.at[PRESS], perm_ref, grid_ref.at[DEPTH], flag_ref,
        grid_ref.at[PORE], grid_ref.at[RES : RES + 3],
    ]
    copies = fetch(inputs, holds, sems)
    layers, width, lanes = flag_ref.shape
    rows = layers * width
    owned = mode_ref.shape[1]
    group = LANES // owned
    me = lax.axis_index(AXES)
    for copy in copies[: len(slot_refs)]:
        copy.wait()
    row, lane = places(cell_ref[...], lanes)
    well_row, well_lane = places(well_ref[...], LANES)
    pick, at_row = cell_pick(row, lane, rows, lanes)
    index = live_index(well_ref, index_ref)
    chunk_rows = first_rows(sums_ref)
    here = lax.shift_right_logical(iota((1, LANES), 1), bits_of(owned)) == lax.rem(me, group)
    controls = [
        jnp.where(here, jnp.concatenate([ref[...].astype(F32)] * group, axis=1), 0.0)
        for ref in (mode_ref, target_ref)
    ]
    later = copies[len(slot_refs) :]
    later[0].wait()
    mobility = total_mobility(grid_ref[SAT].reshape(rows, lanes), grid_ref[SAT + 1].reshape(rows, lanes))
    at_mob = cell_find(mobility, pick, at_row)
    later[1].wait()
    at_press = cell_find(mobility * grid_ref[PRESS].reshape(rows, lanes), pick, at_row)
    sums = well_scatter([index * at_press, index * at_mob], well_row, well_lane, (chunk_rows - 2) // 2)
    block = jnp.concatenate(sums + controls, axis=0)
    block_ref[...] = jnp.concatenate([block] * (block_ref.shape[0] // chunk_rows), axis=0)
    outgoing = repeat_out(block_ref, sums_ref, out_sems)
    pick_row, pick_lane = iota((2 * EDGE, 2 * lanes), 0), lax.rem(iota((2 * EDGE, 2 * lanes), 1), lanes)

    def rim(i, plane):
        both = jnp.concatenate([part.astype(BF16) for part in halves(plane.reshape(rows, lanes))], axis=1)
        pick = ones_of(
            ((pick_row == i) & (pick_lane == lanes - 1)) | ((pick_row == EDGE + i) & (pick_lane == 0))
        )
        return nt(pick, both)

    total = rim(0, grid_ref[PRESS]) + rim(1, grid_ref[SAT]) + rim(2, grid_ref[SAT + 1])
    later[2].wait()
    total = total + rim(3, grid_ref[PERM + 1])
    later[3].wait()
    total = total + rim(4, grid_ref[DEPTH])
    later[4].wait()
    bit_y = lax.bitwise_and(lax.shift_right_logical(flag_ref[...], 1), 1).astype(F32)
    total = total + rim(PLANES - 1, bit_y)
    x_even, y_even = is_even("gx"), is_even("gy")
    last = width - 1
    ends = [
        [
            grid_ref[PRESS, :, edge, :],
            grid_ref[SAT, :, edge, :],
            grid_ref[SAT + 1, :, edge, :],
            grid_ref[PERM, :, edge, :],
            grid_ref[DEPTH, :, edge, :],
            lax.bitwise_and(flag_ref[:, edge, :], 1).astype(F32),
        ]
        for edge in (last, 0)
    ]
    for i, (high, low) in enumerate(zip(*ends)):
        xa_ref[i * layers : (i + 1) * layers, :] = jnp.where(x_even, high, low)
        xb_ref[i * layers : (i + 1) * layers, :] = jnp.where(x_even, low, high)
    ya_ref[...] = jnp.where(y_even, total[:EDGE], total[EDGE:])
    yb_ref[...] = jnp.where(y_even, total[EDGE:], total[:EDGE])
    for copy in later[5:] + outgoing:
        copy.wait()


def upright(rows_list, lanes):
    stack = jnp.concatenate(rows_list, axis=0)
    stack = jnp.concatenate([stack, jnp.zeros((lanes - stack.shape[0], stack.shape[1]), F32)], axis=0)
    return jnp.transpose(stack)


def inverse(x):
    guess = pl.reciprocal(x, approx=True)
    return guess * (2.0 - x * guess)


def phase_weights(pressure):
    b_oil = 1.0 + COMP_OIL * (pressure - 1.0)
    b_water = 1.0 + COMP_WATER * (pressure - 1.0)
    whole = inverse(b_oil * b_water * pressure)
    other = pressure * whole
    return b_water * other, b_oil * other, b_oil * b_water * whole


def faces(perm, perm_next, mob, mob_next, first_up):
    transmit = 2.0 * perm * perm_next * inverse(perm + perm_next)
    return [transmit * jnp.where(first_up, a, b) for a, b in zip(mob, mob_next)]


def weighted(weights, flux):
    oil, water, gas = (w * f for w, f in zip(weights, flux))
    return oil + water + gas, GRAV_OIL * oil + GRAV_WATER * water + GRAV_GAS * gas


def outer_face(own, other, own_up):
    mob, mob_other = phase_mobility(*own[:3]), phase_mobility(*other[:3])
    coupling, lift = weighted(phase_weights(own[0]), faces(own[3], other[3], mob, mob_other, own_up))
    return coupling, lift * (own[4] - other[4]), coupling * other[0]


def main_terms(given_ref, after_ref, flag_ref, cell_ref, well_ref, index_ref, grid_ref, share_ref):
    layers, width, lanes = flag_ref.shape
    rows = layers * width
    row, lane = places(cell_ref[...], lanes)
    share_ref[...] = cell_scatter(live_index(well_ref, index_ref), row, lane, rows, lanes)
    x_last = iota((width, lanes), 0) == width - 1
    y_last = iota((width, lanes), 1) == lanes - 1

    def layer(z):
        press = grid_ref[PRESS, z]
        return press, phase_mobility(press, grid_ref[SAT, z], grid_ref[SAT + 1, z])

    this = layer(0)
    before = None
    for z in range(layers):
        press, mob = this
        following = layer(z + 1) if z + 1 < layers else None
        sat_water, sat_gas = grid_ref[SAT, z], grid_ref[SAT + 1, z]
        sat_oil = 1.0 - sat_water - sat_gas
        depth = grid_ref[DEPTH, z]
        flags = flag_ref[z]
        weights = phase_weights(press)
        storage = grid_ref[PORE, z] * (
            sat_oil * COMP_OIL * weights[0] + sat_water * COMP_WATER * weights[1] + sat_gas * weights[2]
        )
        mobility = total_mobility(sat_water, sat_gas)
        diag = storage + mobility * share_ref[z * width : (z + 1) * width, :]
        rhs = storage * press
        for i, weight in enumerate(weights):
            rhs = rhs - weight * grid_ref[RES + i, z]
        around = jnp.zeros_like(press)
        couplings = {}

        def add(name, flux, drop, beside):
            nonlocal diag, rhs, around
            coupling, lift = weighted(weights, flux)
            couplings[name] = coupling
            diag = diag + coupling
            rhs = rhs + lift * drop
            around = around + coupling * beside

        for dim, size, end, bit in ((0, width, x_last, 1), (1, lanes, y_last, 2)):
            perm = grid_ref[PERM + dim, z]
            perm_next = jnp.where(end, 0.0, pltpu.roll(perm, size - 1, dim))
            up = lax.bitwise_and(flags, bit) > 0
            flux = faces(perm, perm_next, mob, [pltpu.roll(a, size - 1, dim) for a in mob], up)
            drop = depth - pltpu.roll(depth, size - 1, dim)
            add(2 * dim, flux, drop, pltpu.roll(press, size - 1, dim))
            add(2 * dim + 1, [pltpu.roll(a, 1, dim) for a in flux], -pltpu.roll(drop, 1, dim), pltpu.roll(press, 1, dim))
        if following is not None:
            up = lax.bitwise_and(flags, 4) > 0
            flux = faces(grid_ref[PERM + 2, z], grid_ref[PERM + 2, z + 1], mob, following[1], up)
            drop = depth - grid_ref[DEPTH, z + 1]
            add(4, flux, drop, following[0])
        if before is not None:
            add(5, before[0], -before[1], before[2])
        if following is not None:
            before = (flux, drop, press)
        for name, coupling in couplings.items():
            grid_ref[COUP + name, z] = coupling
        grid_ref[DIAG, z] = diag
        grid_ref[RHS, z] = rhs
        grid_ref[AROUND, z] = around
        grid_ref[MOB, z] = mobility
        this = following


def slot_bhp(bhp, well_ref, index_ref):
    well_row, well_lane = places(well_ref[...], LANES)
    return live_index(well_ref, index_ref) * well_gather(bhp, well_row, well_lane)


def sides(a, b, axis):
    even = is_even(axis)
    return jnp.where(even, a, b), jnp.where(even, b, a)


def first_update(
    given_ref, sums_ref, cell_ref, well_ref, index_ref,
    own_yb_ref, own_xb_ref, own_xa_ref, own_ya_ref, yb_ref, xb_ref, xa_ref, ya_ref,
    grid_ref, out_ref, oxb_ref, oxa_ref, known_ref, bound_ref, flank_ref,
    side_ref, push_ref, block_ref, sems,
):
    layers, width, lanes = grid_ref.shape[1:]
    rows = layers * width
    (high, low), (nxt, prev) = (
        sides(own_xa_ref[...], own_xb_ref[...], "gx"), sides(xa_ref[...], xb_ref[...], "gx")
    )
    high, low, nxt, prev = (
        [rim[i * layers : (i + 1) * layers] for i in range(PLANES)] for rim in (high, low, nxt, prev)
    )
    for where, edge, terms in (
        (0, width - 1, outer_face(high, nxt, high[5] > 0.5)),
        (1, 0, outer_face(low, prev, prev[5] < 0.5)),
    ):
        bound_ref[where] = terms[0]
        for name, term in zip((DIAG, RHS, AROUND), terms):
            grid_ref[name, :, edge, :] = grid_ref[name, :, edge, :] + term
    (high, low), (nxt, prev) = (
        sides(own_ya_ref[...], own_yb_ref[...], "gy"), sides(ya_ref[...], yb_ref[...], "gy")
    )
    high, low, nxt, prev = ([rim[i : i + 1] for i in range(PLANES)] for rim in (high, low, nxt, prev))
    after = outer_face(high, nxt, high[5] > 0.5)
    behind = outer_face(low, prev, prev[5] < 0.5)
    flank_ref[0:1, :] = after[0]
    flank_ref[1:2, :] = behind[0]
    stand = upright(list(behind + after), lanes)
    stand = jnp.concatenate([part.astype(BF16) for part in halves(stand)], axis=1)
    wide = (2 * lanes, 3 * lanes)
    from_lane = lax.rem(iota(wide, 0), lanes)
    to_plane, to_lane = places(iota(wide, 1), lanes)
    side_ref[...] = nn(
        stand,
        ones_of(
            ((from_lane == to_plane) & (to_lane == 0)) | ((from_lane == to_plane + 3) & (to_lane == lanes - 1))
        ),
    )
    count = lax.axis_size("gx") * lax.axis_size("gy")
    chunk = sums_ref.shape[0] // count
    well_rows = (chunk - 2) // 2
    group = count // well_rows
    my = lax.axis_index("gy")
    part = sums_ref[0:well_rows, :]
    base = sums_ref[well_rows : 2 * well_rows, :]
    for d in range(1, count):
        part = part + sums_ref[d * chunk : d * chunk + well_rows, :]
        base = base + sums_ref[d * chunk + well_rows : d * chunk + 2 * well_rows, :]
    controls = []
    for k in (2 * well_rows, 2 * well_rows + 1):
        total = sums_ref[pl.ds(k, well_rows, stride=group * chunk), :]
        for j in range(1, group):
            total = total + sums_ref[pl.ds(j * chunk + k, well_rows, stride=group * chunk), :]
        controls.append(total)
    mode, target = controls
    bhp = jnp.where(mode < 0.5, target, (part - target) / base)
    known_ref[0] = mode
    known_ref[1] = target
    known_ref[2] = base
    row, lane = places(cell_ref[...], lanes)
    well_row, well_lane = places(well_ref[...], LANES)
    push_ref[...] = cell_scatter(slot_bhp(bhp, well_ref, index_ref), row, lane, rows, lanes)
    for z in range(layers):
        here = slice(z * width, (z + 1) * width)
        diag, rhs, around = (
            grid_ref[name, z] + side_ref[here, i * lanes : (i + 1) * lanes]
            for i, name in enumerate((DIAG, RHS, AROUND))
        )
        scale = RELAXATION * inverse(diag)
        rhs = scale * rhs
        gain = scale * grid_ref[MOB, z]
        current = (1.0 - RELAXATION) * grid_ref[PRESS, z] + rhs + scale * around + gain * push_ref[here, :]
        grid_ref[SCALE, z] = scale
        grid_ref[RHS, z] = rhs
        grid_ref[GAIN, z] = gain
        grid_ref[CURRENT, z] = current
    current = grid_ref[CURRENT].reshape(rows, lanes)
    oxa_ref[...], oxb_ref[...] = sides(
        grid_ref[CURRENT, :, width - 1, :], grid_ref[CURRENT, :, 0, :], "gx"
    )
    at_cell = cell_find(grid_ref[MOB].reshape(rows, lanes) * current, *cell_pick(row, lane, rows, lanes))
    (part,) = well_scatter([live_index(well_ref, index_ref) * at_cell], well_row, well_lane, well_rows)
    both = jnp.concatenate([half.astype(BF16) for half in halves(current)], axis=1)
    pick_row, pick_lane = iota((2 * EDGE, 2 * lanes), 0), lax.rem(iota((2 * EDGE, 2 * lanes), 1), lanes)
    rims = nt(
        ones_of(((pick_row == 0) & (pick_lane == lanes - 1)) | ((pick_row == 1) & (pick_lane == 0))), both
    )
    pieces = rows // LANES
    split = [
        jnp.concatenate([rims[r : r + 1, i * LANES : (i + 1) * LANES] for i in range(pieces)], axis=0)
        for r in range(2)
    ]
    height = well_rows + pieces
    ends = lax.axis_size("gy")
    for i in range(block_ref.shape[0] // height):
        block_ref[i * height : i * height + well_rows, :] = part
        block_ref[i * height + well_rows : (i + 1) * height, :] = jnp.where(
            i % ends > my, split[0], split[1]
        )
    for copy in repeat_out(block_ref, out_ref, sems):
        copy.wait()


def last_update(
    sums_ref, known_ref, cell_ref, well_ref, index_ref, grid_ref, bound_ref, flank_ref, xb_ref, xa_ref,
    out_ref, bhp_ref, push_ref, side_ref,
):
    layers, width, lanes = out_ref.shape
    rows = layers * width
    count = lax.axis_size("gx") * lax.axis_size("gy")
    height = sums_ref.shape[0] // count
    well_rows = known_ref.shape[1]
    pieces = height - well_rows
    me = lax.axis_index(AXES)
    part = sums_ref[0:well_rows, :]
    for d in range(1, count):
        part = part + sums_ref[d * height : d * height + well_rows, :]
    bhp = jnp.where(known_ref[0] < 0.5, known_ref[1], (part - known_ref[1]) / known_ref[2])
    owned = bhp_ref.shape[1]
    group = LANES // owned
    line = jnp.sum(
        jnp.where(iota(bhp.shape, 0) == me // group, bhp, 0.0), axis=0, keepdims=True
    )
    line = pltpu.roll(line, lax.rem(LANES - lax.rem(me, group) * owned, LANES), 1)
    bhp_ref[...] = line[:, :owned]
    row, lane = places(cell_ref[...], lanes)
    push_ref[...] = cell_scatter(slot_bhp(bhp, well_ref, index_ref), row, lane, rows, lanes)
    strips = []
    for beside in (jnp.maximum(me - 1, 0), jnp.minimum(me + 1, count - 1)):
        strips.append(
            jnp.concatenate(
                [sums_ref[pl.ds(beside * height + well_rows + i, 1), :] for i in range(pieces)], axis=1
            )
        )
    side_ref[...] = upright([flank_ref[1:2, :] * strips[0], flank_ref[0:1, :] * strips[1]], lanes)
    along = iota((width, lanes), 1)
    nxt, prev = sides(xa_ref[...], xb_ref[...], "gx")
    for z in range(layers):
        here = slice(z * width, (z + 1) * width)
        current = grid_ref[CURRENT, z]
        side = side_ref[here, :]
        around = jnp.where(along == 0, side, jnp.where(along == lanes - 1, pltpu.roll(side, lanes - 2, 1), 0.0))
        besides = [
            pltpu.roll(current, width - 1, 0),
            pltpu.roll(current, 1, 0),
            pltpu.roll(current, lanes - 1, 1),
            pltpu.roll(current, 1, 1),
            grid_ref[CURRENT, z + 1] if z + 1 < layers else None,
            grid_ref[CURRENT, z - 1] if z > 0 else None,
        ]
        for i, beside in enumerate(besides):
            if beside is not None:
                around = around + grid_ref[COUP + i, z] * beside
        out_ref[z] = (
            (1.0 - RELAXATION) * current
            + grid_ref[RHS, z]
            + grid_ref[GAIN, z] * push_ref[here, :]
            + grid_ref[SCALE, z] * around
        )
    for where, edge, beyond in ((0, width - 1, nxt), (1, 0, prev)):
        out_ref[:, edge, :] = out_ref[:, edge, :] + grid_ref[SCALE, :, edge, :] * (bound_ref[where] * beyond)


def call(kernel, outs, args, scratch=(), spaces=None, out_spaces=None, aliases=None):
    shapes = [jax.ShapeDtypeStruct(item, F32) if isinstance(item, tuple) else item for item in outs]
    spaces = spaces or [pltpu.VMEM] * len(args)
    out_spaces = out_spaces or [pltpu.VMEM] * len(outs)
    args = [
        pltpu.with_memory_space_constraint(arg, space) if space is pltpu.HBM else arg
        for arg, space in zip(args, spaces)
    ]
    return pl.pallas_call(
        kernel,
        out_shape=shapes,
        in_specs=[pl.BlockSpec(memory_space=space) for space in spaces],
        out_specs=[pl.BlockSpec(memory_space=space) for space in out_spaces],
        scratch_shapes=[pltpu.VMEM(item, F32) if isinstance(item, tuple) else item for item in scratch],
        input_output_aliases=aliases or {},
        compiler_params=pltpu.CompilerParams(vmem_limit_bytes=24 * 1024 * 1024),
        cost_estimate=pl.CostEstimate(flops=1_000_000, bytes_accessed=4_000_000, transcendentals=0),
    )(*args)


def whole_tiles(height, step, count):
    chunks = step
    while chunks * height % 8:
        chunks += step
    assert count % chunks == 0
    return chunks * height


def everyone(rows, count):
    height = rows.shape[0] // count
    swapped = lax.all_to_all(rows.reshape(count, height, 1, LANES), AXES, 0, 0, tiled=True)
    return swapped.reshape(rows.shape)


def to_pair(block, axis):
    count = lax.axis_size(axis)
    return lax.ppermute(block, axis, [(i, i ^ 1) for i in range(count) if i ^ 1 < count])


def to_other(block, axis):
    count = lax.axis_size(axis)
    ends = [(i, i + 1 if i % 2 else i - 1) for i in range(count)]
    return lax.ppermute(block, axis, [(i, j) for i, j in ends if 0 <= j < count])


def body(
    pressure, saturation, permeability, pore_volume, cell_depth, residual, upstream_flags,
    perf_cell, perf_well, perf_index, well_mode, well_target,
):
    layers, width, lanes = pressure.shape
    rows = layers * width
    count = lax.axis_size("gx") * lax.axis_size("gy")
    owned = well_mode.shape[0]
    well_rows = owned * count // LANES
    chunk = 2 * well_rows + 2
    grid = (layers, width, lanes)
    slots = [perf_cell, perf_well, perf_index]
    operands = slots + [
        well_mode[None], well_target[None], saturation, pressure, permeability, cell_depth,
        upstream_flags, pore_volume, residual,
    ]
    height = whole_tiles(chunk, 1, count)
    sums, yb, xb, xa, ya, given, flags = call(
        opening,
        [
            (count * chunk, LANES), (EDGE, rows), (PLANES * layers, lanes), (PLANES * layers, lanes),
            (EDGE, rows), (GRIDS,) + grid, jax.ShapeDtypeStruct(grid, upstream_flags.dtype),
        ],
        operands,
        [pltpu.VMEM(a.shape, a.dtype) for a in operands[:5]]
        + [(height, LANES), pltpu.SemaphoreType.DMA((INPUTS,))]
        + [pltpu.SemaphoreType.DMA((count * chunk // height,))],
        [pltpu.HBM] * INPUTS,
        [pltpu.HBM] + [pltpu.VMEM] * 6,
    )
    rims = [yb, xb, xa, ya]
    rims = rims + [to_other(yb, "gy"), to_other(xb, "gx"), to_pair(xa, "gx"), to_pair(ya, "gy")]
    gathered = everyone(sums, count)
    (given,) = call(
        main_terms,
        [(GRIDS,) + grid],
        [given, sums, flags] + slots,
        [(rows, lanes)],
        [pltpu.VMEM, pl.ANY] + [pltpu.VMEM] * 4,
        None,
        {0: 0},
    )
    chunk = well_rows + rows // LANES
    height = whole_tiles(chunk, lax.axis_size("gy"), count)
    given, sums, xb, xa, known, bound, flank = call(
        first_update,
        [
            (GRIDS,) + grid, (count * chunk, LANES), (layers, lanes), (layers, lanes), (3, well_rows, LANES),
            (2, layers, lanes), (EDGE, rows),
        ],
        [given, gathered] + slots + rims,
        [
            (rows, 3 * lanes), (rows, lanes), (height, LANES),
            pltpu.SemaphoreType.DMA((count * chunk // height,)),
        ],
        None,
        [pltpu.VMEM, pltpu.HBM] + [pltpu.VMEM] * 5,
        {0: 0},
    )
    gathered = everyone(sums, count)
    xb = to_other(xb, "gx")
    xa = to_pair(xa, "gx")
    out, bhp = call(
        last_update,
        [grid, (1, owned)],
        [gathered, known] + slots + [given, bound, flank, xb, xa],
        [(rows, lanes), (rows, lanes)],
    )
    return out, bhp[0]


def solution(mesh):
    return jax.shard_map(
        body,
        mesh=mesh,
        in_specs=(
            P(None, "gx", "gy"),
            P(None, None, "gx", "gy"),
            P(None, None, "gx", "gy"),
            P(None, "gx", "gy"),
            P(None, "gx", "gy"),
            P(None, None, "gx", "gy"),
            P(None, "gx", "gy"),
            P(("gx", "gy"), None),
            P(("gx", "gy"), None),
            P(("gx", "gy"), None),
            P(("gx", "gy")),
            P(("gx", "gy")),
        ),
        out_specs=(P(None, "gx", "gy"), P(("gx", "gy"))),
        check_vma=False,
    )
```

```python
import jax
import jax.numpy as jnp
from jax import lax
from jax.experimental import pallas as pl
from jax.experimental.pallas import tpu as pltpu
from jax.sharding import PartitionSpec as P

COMP_OIL = 0.2
COMP_WATER = 0.05
GRAV_OIL = 0.4
GRAV_WATER = 0.5
GRAV_GAS = 0.08
RELAXATION = 0.8
LANES = 128
PLANES = 6
INPUTS = 12
PRESS, SAT, PERM, DEPTH, PORE, RES, GRIDS = 0, 1, 3, 6, 7, 8, 11
DIAG, RHS, COUP, MOB, AROUND = 1, 2, 3, 9, 10
CURRENT, SCALE, GAIN = 0, 1, 10
EDGE = 8

F32 = jnp.float32
BF16 = jnp.bfloat16
AXES = ("gx", "gy")


def nn(a, b):
    return lax.dot_general(a, b, (((1,), (0,)), ((), ())), preferred_element_type=F32)


def nt(a, b):
    return lax.dot_general(a, b, (((1,), (1,)), ((), ())), preferred_element_type=F32)


def halves(x):
    high = x.astype(BF16).astype(F32)
    return high, x - high


def iota(shape, dim):
    return lax.broadcasted_iota(jnp.int32, shape, dim)


def hot(index, count):
    return iota((count, index.shape[1]), 0) == index


def ones_of(mask):
    return jnp.where(mask, 1.0, 0.0).astype(BF16)


def bits_of(n):
    assert n & (n - 1) == 0
    return n.bit_length() - 1


def places(index, width):
    return lax.shift_right_arithmetic(index, bits_of(width)), lax.bitwise_and(index, width - 1)


def cell_pick(row, lane, rows, lanes):
    pick = ones_of(hot(lane, lanes))
    return jnp.concatenate([pick, pick], axis=0), hot(row, rows)


def cell_find(field, pick, at_row):
    both = jnp.concatenate([part.astype(BF16) for part in halves(field)], axis=1)
    return jnp.sum(jnp.where(at_row, nn(both, pick), 0.0), axis=0, keepdims=True)


def cell_scatter(value, row, lane, rows, lanes):
    spread = jnp.where(hot(lane, lanes), value, 0.0)
    spread = jnp.concatenate([part.astype(BF16) for part in halves(spread)], axis=0)
    total = nt(ones_of(hot(row, rows)), spread)
    return total[:, :lanes] + total[:, lanes:]


def well_scatter(values, row, lane, rows):
    mine = hot(row, rows)
    stack = []
    for value in values:
        stack.extend(halves(jnp.where(mine, value, 0.0)))
    total = nt(jnp.concatenate(stack, axis=0).astype(BF16), ones_of(hot(lane, LANES)))
    return [
        total[2 * i * rows : (2 * i + 1) * rows] + total[(2 * i + 1) * rows : (2 * i + 2) * rows]
        for i in range(len(values))
    ]


def well_gather(field, row, lane):
    rows = field.shape[0]
    both = jnp.concatenate(halves(field), axis=0).astype(BF16)
    found = nn(both, ones_of(hot(lane, LANES)))
    return jnp.sum(
        jnp.where(hot(row, rows), found[:rows] + found[rows:], 0.0), axis=0, keepdims=True
    )


def total_mobility(sat_water, sat_gas):
    sat_oil = 1.0 - sat_water - sat_gas
    return 0.5 * sat_oil * sat_oil + sat_water * sat_water + 5.0 * (sat_gas * sat_gas)


def phase_mobility(pressure, sat_water, sat_gas):
    sat_oil = 1.0 - sat_water - sat_gas
    b_oil = 1.0 + COMP_OIL * (pressure - 1.0)
    b_water = 1.0 + COMP_WATER * (pressure - 1.0)
    return (
        sat_oil * sat_oil * b_oil * 0.5,
        sat_water * sat_water * b_water,
        sat_gas * sat_gas * pressure * 5.0,
    )


def live_index(well_ref, index_ref):
    return jnp.where(well_ref[...] >= 0, index_ref[...], 0.0)


def fetch(sources, holds, sems):
    copies = [
        pltpu.make_async_copy(source, hold, sems.at[i])
        for i, (source, hold) in enumerate(zip(sources, holds))
    ]
    for copy in copies:
        copy.start()
    return copies


def repeat_out(block_ref, out_ref, sem):
    height = block_ref.shape[0]
    copies = [
        pltpu.make_async_copy(block_ref, out_ref.at[pl.ds(i * height, height)], sem.at[i])
        for i in range(out_ref.shape[0] // height)
    ]
    for copy in copies:
        copy.start()
    return copies


def first_rows(out_ref):
    count = lax.axis_size("gx") * lax.axis_size("gy")
    return out_ref.shape[0] // count


def is_even(axis):
    return lax.rem(lax.axis_index(axis), 2) == 0


def opening(*refs):
    inputs, sems, out_sems = refs[:INPUTS], refs[-2], refs[-1]
    sums_ref, yb_ref, xb_ref, xa_ref, ya_ref, grid_ref, flag_ref = refs[INPUTS : INPUTS + 7]
    cell_ref, well_ref, index_ref, mode_ref, target_ref, block_ref, lying_ref = refs[INPUTS + 7 : -2]
    slot_refs = [cell_ref, well_ref, index_ref, mode_ref, target_ref]
    sat_ref, perm_ref = grid_ref.at[SAT : SAT + 2], grid_ref.at[PERM : PERM + 3]
    holds = slot_refs + [
        sat_ref, grid_ref.at[PRESS], perm_ref, grid_ref.at[DEPTH], flag_ref,
        grid_ref.at[PORE], grid_ref.at[RES : RES + 3],
    ]
    copies = fetch(inputs, holds, sems)
    layers, width, lanes = flag_ref.shape
    rows = layers * width
    owned = mode_ref.shape[1]
    group = LANES // owned
    me = lax.axis_index(AXES)
    for copy in copies[: len(slot_refs)]:
        copy.wait()
    row, lane = places(cell_ref[...], lanes)
    well_row, well_lane = places(well_ref[...], LANES)
    pick, at_row = cell_pick(row, lane, rows, lanes)
    index = live_index(well_ref, index_ref)
    chunk_rows = first_rows(sums_ref)
    here = lax.shift_right_logical(iota((1, LANES), 1), bits_of(owned)) == lax.rem(me, group)
    controls = [
        jnp.where(here, jnp.concatenate([ref[...].astype(F32)] * group, axis=1), 0.0)
        for ref in (mode_ref, target_ref)
    ]
    later = copies[len(slot_refs) :]
    later[0].wait()
    mobility = total_mobility(grid_ref[SAT].reshape(rows, lanes), grid_ref[SAT + 1].reshape(rows, lanes))
    at_mob = cell_find(mobility, pick, at_row)
    later[1].wait()
    at_press = cell_find(mobility * grid_ref[PRESS].reshape(rows, lanes), pick, at_row)
    sums = well_scatter([index * at_press, index * at_mob], well_row, well_lane, (chunk_rows - 2) // 2)
    block = jnp.concatenate(sums + controls, axis=0)
    block_ref[...] = jnp.concatenate([block] * (block_ref.shape[0] // chunk_rows), axis=0)
    outgoing = repeat_out(block_ref, sums_ref, out_sems)
    pair = lax.shift_right_logical(iota((rows, lanes), 1), 1)

    def rim(total, i, plane):
        return jnp.where(pair == i, pltpu.roll(plane.reshape(rows, lanes), 2 * i + 1, 1), total)

    total = rim(jnp.zeros((rows, lanes), F32), 0, grid_ref[PRESS])
    total = rim(rim(total, 1, grid_ref[SAT]), 2, grid_ref[SAT + 1])
    later[2].wait()
    total = rim(total, 3, grid_ref[PERM + 1])
    later[3].wait()
    total = rim(total, 4, grid_ref[DEPTH])
    later[4].wait()
    bit_y = lax.bitwise_and(lax.shift_right_logical(flag_ref[...], 1), 1).astype(F32)
    total = rim(total, PLANES - 1, bit_y)
    pieces = [
        (i * 2 * EDGE, jnp.transpose(total[i * LANES : (i + 1) * LANES])[: 2 * EDGE])
        for i in range(rows // LANES)
    ]
    for first, piece in pieces:
        lying_ref[first : first + 2 * EDGE, :] = piece
    high, low = (
        jnp.concatenate([lying_ref[pl.ds(first + k, EDGE, stride=2), :] for first, _ in pieces], axis=1)
        for k in range(2)
    )
    x_even, y_even = is_even("gx"), is_even("gy")
    ya_ref[...] = jnp.where(y_even, high, low)
    yb_ref[...] = jnp.where(y_even, low, high)
    last = width - 1
    ends = [
        [
            grid_ref[PRESS, :, edge, :],
            grid_ref[SAT, :, edge, :],
            grid_ref[SAT + 1, :, edge, :],
            grid_ref[PERM, :, edge, :],
            grid_ref[DEPTH, :, edge, :],
            lax.bitwise_and(flag_ref[:, edge, :], 1).astype(F32),
        ]
        for edge in (last, 0)
    ]
    for i, (high, low) in enumerate(zip(*ends)):
        xa_ref[i * layers : (i + 1) * layers, :] = jnp.where(x_even, high, low)
        xb_ref[i * layers : (i + 1) * layers, :] = jnp.where(x_even, low, high)
    for copy in later[5:] + outgoing:
        copy.wait()


def upright(rows_list, lanes):
    stack = jnp.concatenate(rows_list, axis=0)
    stack = jnp.concatenate([stack, jnp.zeros((lanes - stack.shape[0], stack.shape[1]), F32)], axis=0)
    return jnp.transpose(stack)


def inverse(x):
    guess = pl.reciprocal(x, approx=True)
    return guess * (2.0 - x * guess)


def phase_weights(pressure):
    b_oil = 1.0 + COMP_OIL * (pressure - 1.0)
    b_water = 1.0 + COMP_WATER * (pressure - 1.0)
    whole = inverse(b_oil * b_water * pressure)
    other = pressure * whole
    return b_water * other, b_oil * other, b_oil * b_water * whole


def faces(perm, perm_next, mob, mob_next, first_up):
    transmit = 2.0 * perm * perm_next * inverse(perm + perm_next)
    return [transmit * jnp.where(first_up, a, b) for a, b in zip(mob, mob_next)]


def weighted(weights, flux):
    oil, water, gas = (w * f for w, f in zip(weights, flux))
    return oil + water + gas, GRAV_OIL * oil + GRAV_WATER * water + GRAV_GAS * gas


def outer_face(own, other, own_up):
    mob, mob_other = phase_mobility(*own[:3]), phase_mobility(*other[:3])
    coupling, lift = weighted(phase_weights(own[0]), faces(own[3], other[3], mob, mob_other, own_up))
    return coupling, lift * (own[4] - other[4]), coupling * other[0]


def main_terms(given_ref, after_ref, flag_ref, cell_ref, well_ref, index_ref, grid_ref, share_ref):
    layers, width, lanes = flag_ref.shape
    rows = layers * width
    row, lane = places(cell_ref[...], lanes)
    share_ref[...] = cell_scatter(live_index(well_ref, index_ref), row, lane, rows, lanes)
    x_last = iota((width, lanes), 0) == width - 1
    y_last = iota((width, lanes), 1) == lanes - 1

    def layer(z):
        press = grid_ref[PRESS, z]
        return press, phase_mobility(press, grid_ref[SAT, z], grid_ref[SAT + 1, z])

    this = layer(0)
    before = None
    for z in range(layers):
        press, mob = this
        following = layer(z + 1) if z + 1 < layers else None
        sat_water, sat_gas = grid_ref[SAT, z], grid_ref[SAT + 1, z]
        sat_oil = 1.0 - sat_water - sat_gas
        depth = grid_ref[DEPTH, z]
        flags = flag_ref[z]
        weights = phase_weights(press)
        storage = grid_ref[PORE, z] * (
            sat_oil * COMP_OIL * weights[0] + sat_water * COMP_WATER * weights[1] + sat_gas * weights[2]
        )
        mobility = total_mobility(sat_water, sat_gas)
        diag = storage + mobility * share_ref[z * width : (z + 1) * width, :]
        rhs = storage * press
        for i, weight in enumerate(weights):
            rhs = rhs - weight * grid_ref[RES + i, z]
        around = jnp.zeros_like(press)
        couplings = {}

        def add(name, flux, drop, beside):
            nonlocal diag, rhs, around
            coupling, lift = weighted(weights, flux)
            couplings[name] = coupling
            diag = diag + coupling
            rhs = rhs + lift * drop
            around = around + coupling * beside

        for dim, size, end, bit in ((0, width, x_last, 1), (1, lanes, y_last, 2)):
            perm = grid_ref[PERM + dim, z]
            perm_next = jnp.where(end, 0.0, pltpu.roll(perm, size - 1, dim))
            up = lax.bitwise_and(flags, bit) > 0
            flux = faces(perm, perm_next, mob, [pltpu.roll(a, size - 1, dim) for a in mob], up)
            drop = depth - pltpu.roll(depth, size - 1, dim)
            add(2 * dim, flux, drop, pltpu.roll(press, size - 1, dim))
            add(2 * dim + 1, [pltpu.roll(a, 1, dim) for a in flux], -pltpu.roll(drop, 1, dim), pltpu.roll(press, 1, dim))
        if following is not None:
            up = lax.bitwise_and(flags, 4) > 0
            flux = faces(grid_ref[PERM + 2, z], grid_ref[PERM + 2, z + 1], mob, following[1], up)
            drop = depth - grid_ref[DEPTH, z + 1]
            add(4, flux, drop, following[0])
        if before is not None:
            add(5, before[0], -before[1], before[2])
        if following is not None:
            before = (flux, drop, press)
        for name, coupling in couplings.items():
            grid_ref[COUP + name, z] = coupling
        grid_ref[DIAG, z] = diag
        grid_ref[RHS, z] = rhs
        grid_ref[AROUND, z] = around
        grid_ref[MOB, z] = mobility
        this = following


def slot_bhp(bhp, well_ref, index_ref):
    well_row, well_lane = places(well_ref[...], LANES)
    return live_index(well_ref, index_ref) * well_gather(bhp, well_row, well_lane)


def sides(a, b, axis):
    even = is_even(axis)
    return jnp.where(even, a, b), jnp.where(even, b, a)


def close_ends(nxt, prev, axis):
    me = lax.axis_index(axis)
    nxt[3] = jnp.where(me < lax.axis_size(axis) - 1, nxt[3], 0.0)
    prev[3] = jnp.where(me > 0, prev[3], 0.0)


def first_update(
    given_ref, sums_ref, cell_ref, well_ref, index_ref,
    own_yb_ref, own_xb_ref, own_xa_ref, own_ya_ref, yb_ref, xb_ref, xa_ref, ya_ref,
    grid_ref, out_ref, oxb_ref, oxa_ref, known_ref, bound_ref, flank_ref,
    side_ref, push_ref, block_ref, sems,
):
    layers, width, lanes = grid_ref.shape[1:]
    rows = layers * width
    (high, low), (nxt, prev) = (
        sides(own_xa_ref[...], own_xb_ref[...], "gx"), sides(xa_ref[...], xb_ref[...], "gx")
    )
    high, low, nxt, prev = (
        [rim[i * layers : (i + 1) * layers] for i in range(PLANES)] for rim in (high, low, nxt, prev)
    )
    close_ends(nxt, prev, "gx")
    for where, edge, terms in (
        (0, width - 1, outer_face(high, nxt, high[5] > 0.5)),
        (1, 0, outer_face(low, prev, prev[5] < 0.5)),
    ):
        bound_ref[where] = terms[0]
        for name, term in zip((DIAG, RHS, AROUND), terms):
            grid_ref[name, :, edge, :] = grid_ref[name, :, edge, :] + term
    (high, low), (nxt, prev) = (
        sides(own_ya_ref[...], own_yb_ref[...], "gy"), sides(ya_ref[...], yb_ref[...], "gy")
    )
    high, low, nxt, prev = ([rim[i : i + 1] for i in range(PLANES)] for rim in (high, low, nxt, prev))
    close_ends(nxt, prev, "gy")
    after = outer_face(high, nxt, high[5] > 0.5)
    behind = outer_face(low, prev, prev[5] < 0.5)
    flank_ref[0:1, :] = after[0]
    flank_ref[1:2, :] = behind[0]
    stand = upright(list(behind + after), lanes)
    stand = jnp.concatenate([part.astype(BF16) for part in halves(stand)], axis=1)
    wide = (2 * lanes, 3 * lanes)
    from_lane = lax.rem(iota(wide, 0), lanes)
    to_plane, to_lane = places(iota(wide, 1), lanes)
    side_ref[...] = nn(
        stand,
        ones_of(
            ((from_lane == to_plane) & (to_lane == 0)) | ((from_lane == to_plane + 3) & (to_lane == lanes - 1))
        ),
    )
    count = lax.axis_size("gx") * lax.axis_size("gy")
    chunk = sums_ref.shape[0] // count
    well_rows = (chunk - 2) // 2
    group = count // well_rows
    my = lax.axis_index("gy")
    part = sums_ref[0:well_rows, :]
    base = sums_ref[well_rows : 2 * well_rows, :]
    for d in range(1, count):
        part = part + sums_ref[d * chunk : d * chunk + well_rows, :]
        base = base + sums_ref[d * chunk + well_rows : d * chunk + 2 * well_rows, :]
    controls = []
    for k in (2 * well_rows, 2 * well_rows + 1):
        total = sums_ref[pl.ds(k, well_rows, stride=group * chunk), :]
        for j in range(1, group):
            total = total + sums_ref[pl.ds(j * chunk + k, well_rows, stride=group * chunk), :]
        controls.append(total)
    mode, target = controls
    bhp = jnp.where(mode < 0.5, target, (part - target) / base)
    known_ref[0] = mode
    known_ref[1] = target
    known_ref[2] = base
    row, lane = places(cell_ref[...], lanes)
    well_row, well_lane = places(well_ref[...], LANES)
    push_ref[...] = cell_scatter(slot_bhp(bhp, well_ref, index_ref), row, lane, rows, lanes)
    for z in range(layers):
        here = slice(z * width, (z + 1) * width)
        diag, rhs, around = (
            grid_ref[name, z] + side_ref[here, i * lanes : (i + 1) * lanes]
            for i, name in enumerate((DIAG, RHS, AROUND))
        )
        scale = RELAXATION * inverse(diag)
        rhs = scale * rhs
        gain = scale * grid_ref[MOB, z]
        current = (1.0 - RELAXATION) * grid_ref[PRESS, z] + rhs + scale * around + gain * push_ref[here, :]
        grid_ref[SCALE, z] = scale
        grid_ref[RHS, z] = rhs
        grid_ref[GAIN, z] = gain
        grid_ref[CURRENT, z] = current
    current = grid_ref[CURRENT].reshape(rows, lanes)
    oxa_ref[...], oxb_ref[...] = sides(
        grid_ref[CURRENT, :, width - 1, :], grid_ref[CURRENT, :, 0, :], "gx"
    )
    at_cell = cell_find(grid_ref[MOB].reshape(rows, lanes) * current, *cell_pick(row, lane, rows, lanes))
    (part,) = well_scatter([live_index(well_ref, index_ref) * at_cell], well_row, well_lane, well_rows)
    both = jnp.concatenate([half.astype(BF16) for half in halves(current)], axis=1)
    pick_row, pick_lane = iota((2 * EDGE, 2 * lanes), 0), lax.rem(iota((2 * EDGE, 2 * lanes), 1), lanes)
    rims = nt(
        ones_of(((pick_row == 0) & (pick_lane == lanes - 1)) | ((pick_row == 1) & (pick_lane == 0))), both
    )
    pieces = rows // LANES
    split = [
        jnp.concatenate([rims[r : r + 1, i * LANES : (i + 1) * LANES] for i in range(pieces)], axis=0)
        for r in range(2)
    ]
    height = well_rows + pieces
    ends = lax.axis_size("gy")
    for i in range(block_ref.shape[0] // height):
        block_ref[i * height : i * height + well_rows, :] = part
        block_ref[i * height + well_rows : (i + 1) * height, :] = jnp.where(
            i % ends > my, split[0], split[1]
        )
    for copy in repeat_out(block_ref, out_ref, sems):
        copy.wait()


def last_update(
    sums_ref, known_ref, cell_ref, well_ref, index_ref, grid_ref, bound_ref, flank_ref, xb_ref, xa_ref,
    out_ref, bhp_ref, push_ref, side_ref,
):
    layers, width, lanes = out_ref.shape
    rows = layers * width
    count = lax.axis_size("gx") * lax.axis_size("gy")
    height = sums_ref.shape[0] // count
    well_rows = known_ref.shape[1]
    pieces = height - well_rows
    me = lax.axis_index(AXES)
    part = sums_ref[0:well_rows, :]
    for d in range(1, count):
        part = part + sums_ref[d * height : d * height + well_rows, :]
    bhp = jnp.where(known_ref[0] < 0.5, known_ref[1], (part - known_ref[1]) / known_ref[2])
    owned = bhp_ref.shape[1]
    group = LANES // owned
    line = jnp.sum(
        jnp.where(iota(bhp.shape, 0) == me // group, bhp, 0.0), axis=0, keepdims=True
    )
    line = pltpu.roll(line, lax.rem(LANES - lax.rem(me, group) * owned, LANES), 1)
    bhp_ref[...] = line[:, :owned]
    row, lane = places(cell_ref[...], lanes)
    push_ref[...] = cell_scatter(slot_bhp(bhp, well_ref, index_ref), row, lane, rows, lanes)
    strips = []
    for beside in (jnp.maximum(me - 1, 0), jnp.minimum(me + 1, count - 1)):
        strips.append(
            jnp.concatenate(
                [sums_ref[pl.ds(beside * height + well_rows + i, 1), :] for i in range(pieces)], axis=1
            )
        )
    side_ref[...] = upright([flank_ref[1:2, :] * strips[0], flank_ref[0:1, :] * strips[1]], lanes)
    along = iota((width, lanes), 1)
    nxt, prev = sides(xa_ref[...], xb_ref[...], "gx")
    for z in range(layers):
        here = slice(z * width, (z + 1) * width)
        current = grid_ref[CURRENT, z]
        side = side_ref[here, :]
        around = jnp.where(along == 0, side, jnp.where(along == lanes - 1, pltpu.roll(side, lanes - 2, 1), 0.0))
        besides = [
            pltpu.roll(current, width - 1, 0),
            pltpu.roll(current, 1, 0),
            pltpu.roll(current, lanes - 1, 1),
            pltpu.roll(current, 1, 1),
            grid_ref[CURRENT, z + 1] if z + 1 < layers else None,
            grid_ref[CURRENT, z - 1] if z > 0 else None,
        ]
        for i, beside in enumerate(besides):
            if beside is not None:
                around = around + grid_ref[COUP + i, z] * beside
        out_ref[z] = (
            (1.0 - RELAXATION) * current
            + grid_ref[RHS, z]
            + grid_ref[GAIN, z] * push_ref[here, :]
            + grid_ref[SCALE, z] * around
        )
    for where, edge, beyond in ((0, width - 1, nxt), (1, 0, prev)):
        out_ref[:, edge, :] = out_ref[:, edge, :] + grid_ref[SCALE, :, edge, :] * (bound_ref[where] * beyond)


def call(kernel, outs, args, scratch=(), spaces=None, out_spaces=None, aliases=None):
    shapes = [jax.ShapeDtypeStruct(item, F32) if isinstance(item, tuple) else item for item in outs]
    spaces = spaces or [pltpu.VMEM] * len(args)
    out_spaces = out_spaces or [pltpu.VMEM] * len(outs)
    args = [
        pltpu.with_memory_space_constraint(arg, space) if space is pltpu.HBM else arg
        for arg, space in zip(args, spaces)
    ]
    return pl.pallas_call(
        kernel,
        out_shape=shapes,
        in_specs=[pl.BlockSpec(memory_space=space) for space in spaces],
        out_specs=[pl.BlockSpec(memory_space=space) for space in out_spaces],
        scratch_shapes=[pltpu.VMEM(item, F32) if isinstance(item, tuple) else item for item in scratch],
        input_output_aliases=aliases or {},
        compiler_params=pltpu.CompilerParams(vmem_limit_bytes=24 * 1024 * 1024),
        cost_estimate=pl.CostEstimate(flops=1_000_000, bytes_accessed=4_000_000, transcendentals=0),
    )(*args)


def whole_tiles(height, step, count):
    chunks = step
    while chunks * height % 8:
        chunks += step
    assert count % chunks == 0
    return chunks * height


def everyone(rows, count):
    height = rows.shape[0] // count
    swapped = lax.all_to_all(rows.reshape(count, height, 1, LANES), AXES, 0, 0, tiled=True)
    return swapped.reshape(rows.shape)


def to_pair(block, axis):
    count = lax.axis_size(axis)
    assert count % 2 == 0
    return lax.ppermute(block, axis, [(i, i ^ 1) for i in range(count)])


def to_other(block, axis):
    sizes = {name: lax.axis_size(name) for name in AXES}
    moves = []
    for gx in range(sizes["gx"]):
        for gy in range(sizes["gy"]):
            there = {"gx": gx, "gy": gy}
            away = there[axis] + (1 if there[axis] % 2 else -1)
            if 0 <= away < sizes[axis]:
                there[axis] = away
            else:
                cross = "gy" if axis == "gx" else "gx"
                there[cross] ^= 1
            moves.append((gx * sizes["gy"] + gy, there["gx"] * sizes["gy"] + there["gy"]))
    return lax.ppermute(block, AXES, moves)


def body(
    pressure, saturation, permeability, pore_volume, cell_depth, residual, upstream_flags,
    perf_cell, perf_well, perf_index, well_mode, well_target,
):
    layers, width, lanes = pressure.shape
    rows = layers * width
    count = lax.axis_size("gx") * lax.axis_size("gy")
    owned = well_mode.shape[0]
    well_rows = owned * count // LANES
    chunk = 2 * well_rows + 2
    grid = (layers, width, lanes)
    slots = [perf_cell, perf_well, perf_index]
    operands = slots + [
        well_mode[None], well_target[None], saturation, pressure, permeability, cell_depth,
        upstream_flags, pore_volume, residual,
    ]
    height = whole_tiles(chunk, 1, count)
    sums, yb, xb, xa, ya, given, flags = call(
        opening,
        [
            (count * chunk, LANES), (EDGE, rows), (PLANES * layers, lanes), (PLANES * layers, lanes),
            (EDGE, rows), (GRIDS,) + grid, jax.ShapeDtypeStruct(grid, upstream_flags.dtype),
        ],
        operands,
        [pltpu.VMEM(a.shape, a.dtype) for a in operands[:5]]
        + [(height, LANES), (2 * EDGE * (rows // LANES), LANES), pltpu.SemaphoreType.DMA((INPUTS,))]
        + [pltpu.SemaphoreType.DMA((count * chunk // height,))],
        [pltpu.HBM] * INPUTS,
        [pltpu.HBM] + [pltpu.VMEM] * 6,
    )
    rims = [yb, xb, xa, ya]
    rims = rims + [to_other(yb, "gy"), to_other(xb, "gx"), to_pair(xa, "gx"), to_pair(ya, "gy")]
    gathered = everyone(sums, count)
    (given,) = call(
        main_terms,
        [(GRIDS,) + grid],
        [given, sums, flags] + slots,
        [(rows, lanes)],
        [pltpu.VMEM, pl.ANY] + [pltpu.VMEM] * 4,
        None,
        {0: 0},
    )
    chunk = well_rows + rows // LANES
    height = whole_tiles(chunk, lax.axis_size("gy"), count)
    given, sums, xb, xa, known, bound, flank = call(
        first_update,
        [
            (GRIDS,) + grid, (count * chunk, LANES), (layers, lanes), (layers, lanes), (3, well_rows, LANES),
            (2, layers, lanes), (EDGE, rows),
        ],
        [given, gathered] + slots + rims,
        [
            (rows, 3 * lanes), (rows, lanes), (height, LANES),
            pltpu.SemaphoreType.DMA((count * chunk // height,)),
        ],
        None,
        [pltpu.VMEM, pltpu.HBM] + [pltpu.VMEM] * 5,
        {0: 0},
    )
    gathered = everyone(sums, count)
    xb = to_other(xb, "gx")
    xa = to_pair(xa, "gx")
    out, bhp = call(
        last_update,
        [grid, (1, owned)],
        [gathered, known] + slots + [given, bound, flank, xb, xa],
        [(rows, lanes), (rows, lanes)],
    )
    return out, bhp[0]


def solution(mesh):
    return jax.shard_map(
        body,
        mesh=mesh,
        in_specs=(
            P(None, "gx", "gy"),
            P(None, None, "gx", "gy"),
            P(None, None, "gx", "gy"),
            P(None, "gx", "gy"),
            P(None, "gx", "gy"),
            P(None, None, "gx", "gy"),
            P(None, "gx", "gy"),
            P(("gx", "gy"), None),
            P(("gx", "gy"), None),
            P(("gx", "gy"), None),
            P(("gx", "gy")),
            P(("gx", "gy")),
        ),
        out_specs=(P(None, "gx", "gy"), P(("gx", "gy"))),
        check_vma=False,
    )
```

```python
import jax
import jax.numpy as jnp
from jax import lax
from jax.experimental import pallas as pl
from jax.experimental.pallas import tpu as pltpu
from jax.sharding import PartitionSpec as P

COMP_OIL = 0.2
COMP_WATER = 0.05
GRAV_OIL = 0.4
GRAV_WATER = 0.5
GRAV_GAS = 0.08
RELAXATION = 0.8
LANES = 128
PLANES = 6
INPUTS = 12
PRESS, SAT, PERM, DEPTH, PORE, RES, GRIDS = 0, 1, 3, 6, 7, 8, 11
DIAG, RHS, COUP, MOB, AROUND = 1, 2, 3, 9, 10
CURRENT, SCALE, GAIN = 0, 1, 10
EDGE = 8

F32 = jnp.float32
BF16 = jnp.bfloat16
AXES = ("gx", "gy")


def nn(a, b):
    return lax.dot_general(a, b, (((1,), (0,)), ((), ())), preferred_element_type=F32)


def nt(a, b):
    return lax.dot_general(a, b, (((1,), (1,)), ((), ())), preferred_element_type=F32)


def halves(x):
    high = x.astype(BF16).astype(F32)
    return high, x - high


def iota(shape, dim):
    return lax.broadcasted_iota(jnp.int32, shape, dim)


def hot(index, count):
    return iota((count, index.shape[1]), 0) == index


def ones_of(mask):
    return jnp.where(mask, 1.0, 0.0).astype(BF16)


def bits_of(n):
    assert n & (n - 1) == 0
    return n.bit_length() - 1


def places(index, width):
    return lax.shift_right_arithmetic(index, bits_of(width)), lax.bitwise_and(index, width - 1)


def cell_pick(row, lane, rows, lanes):
    pick = ones_of(hot(lane, lanes))
    return jnp.concatenate([pick, pick], axis=0), hot(row, rows)


def cell_find(field, pick, at_row):
    both = jnp.concatenate([part.astype(BF16) for part in halves(field)], axis=1)
    return jnp.sum(jnp.where(at_row, nn(both, pick), 0.0), axis=0, keepdims=True)


def cell_scatter(value, row, lane, rows, lanes):
    spread = jnp.where(hot(lane, lanes), value, 0.0)
    spread = jnp.concatenate([part.astype(BF16) for part in halves(spread)], axis=0)
    total = nt(ones_of(hot(row, rows)), spread)
    return total[:, :lanes] + total[:, lanes:]


def well_scatter(values, row, lane, rows):
    mine = hot(row, rows)
    stack = []
    for value in values:
        stack.extend(halves(jnp.where(mine, value, 0.0)))
    total = nt(jnp.concatenate(stack, axis=0).astype(BF16), ones_of(hot(lane, LANES)))
    return [
        total[2 * i * rows : (2 * i + 1) * rows] + total[(2 * i + 1) * rows : (2 * i + 2) * rows]
        for i in range(len(values))
    ]


def well_gather(field, row, lane):
    rows = field.shape[0]
    both = jnp.concatenate(halves(field), axis=0).astype(BF16)
    found = nn(both, ones_of(hot(lane, LANES)))
    return jnp.sum(
        jnp.where(hot(row, rows), found[:rows] + found[rows:], 0.0), axis=0, keepdims=True
    )


def total_mobility(sat_water, sat_gas):
    sat_oil = 1.0 - sat_water - sat_gas
    return 0.5 * sat_oil * sat_oil + sat_water * sat_water + 5.0 * (sat_gas * sat_gas)


def phase_mobility(pressure, sat_water, sat_gas):
    sat_oil = 1.0 - sat_water - sat_gas
    b_oil = 1.0 + COMP_OIL * (pressure - 1.0)
    b_water = 1.0 + COMP_WATER * (pressure - 1.0)
    return (
        sat_oil * sat_oil * b_oil * 0.5,
        sat_water * sat_water * b_water,
        sat_gas * sat_gas * pressure * 5.0,
    )


def live_index(well_ref, index_ref):
    return jnp.where(well_ref[...] >= 0, index_ref[...], 0.0)


def fetch(sources, holds, sems):
    copies = [
        pltpu.make_async_copy(source, hold, sems.at[i])
        for i, (source, hold) in enumerate(zip(sources, holds))
    ]
    for copy in copies:
        copy.start()
    return copies


def repeat_out(block_ref, out_ref, sem):
    height = block_ref.shape[0]
    copies = [
        pltpu.make_async_copy(block_ref, out_ref.at[pl.ds(i * height, height)], sem.at[i])
        for i in range(out_ref.shape[0] // height)
    ]
    for copy in copies:
        copy.start()
    return copies


def first_rows(out_ref):
    count = lax.axis_size("gx") * lax.axis_size("gy")
    return out_ref.shape[0] // count


def is_even(axis):
    return lax.rem(lax.axis_index(axis), 2) == 0


def opening(*refs):
    inputs, sems, out_sems = refs[:INPUTS], refs[-2], refs[-1]
    sums_ref, yb_ref, xb_ref, xa_ref, ya_ref, grid_ref, flag_ref = refs[INPUTS : INPUTS + 7]
    cell_ref, well_ref, index_ref, mode_ref, target_ref, block_ref, lying_ref = refs[INPUTS + 7 : -2]
    slot_refs = [cell_ref, well_ref, index_ref, mode_ref, target_ref]
    sat_ref, perm_ref = grid_ref.at[SAT : SAT + 2], grid_ref.at[PERM : PERM + 3]
    holds = slot_refs + [
        sat_ref, grid_ref.at[PRESS], perm_ref, grid_ref.at[DEPTH], flag_ref,
        grid_ref.at[PORE], grid_ref.at[RES : RES + 3],
    ]
    copies = fetch(inputs, holds, sems)
    layers, width, lanes = flag_ref.shape
    rows = layers * width
    owned = mode_ref.shape[1]
    group = LANES // owned
    me = lax.axis_index(AXES)
    for copy in copies[: len(slot_refs)]:
        copy.wait()
    row, lane = places(cell_ref[...], lanes)
    well_row, well_lane = places(well_ref[...], LANES)
    pick, at_row = cell_pick(row, lane, rows, lanes)
    index = live_index(well_ref, index_ref)
    chunk_rows = first_rows(sums_ref)
    here = lax.shift_right_logical(iota((1, LANES), 1), bits_of(owned)) == lax.rem(me, group)
    controls = [
        jnp.where(here, jnp.concatenate([ref[...].astype(F32)] * group, axis=1), 0.0)
        for ref in (mode_ref, target_ref)
    ]
    later = copies[len(slot_refs) :]
    later[0].wait()
    mobility = total_mobility(grid_ref[SAT].reshape(rows, lanes), grid_ref[SAT + 1].reshape(rows, lanes))
    at_mob = cell_find(mobility, pick, at_row)
    later[1].wait()
    at_press = cell_find(mobility * grid_ref[PRESS].reshape(rows, lanes), pick, at_row)
    sums = well_scatter([index * at_press, index * at_mob], well_row, well_lane, (chunk_rows - 2) // 2)
    block = jnp.concatenate(sums + controls, axis=0)
    block_ref[...] = jnp.concatenate([block] * (block_ref.shape[0] // chunk_rows), axis=0)
    outgoing = repeat_out(block_ref, sums_ref, out_sems)
    pair = lax.shift_right_logical(iota((rows, lanes), 1), 1)

    def rim(total, i, plane):
        return jnp.where(pair == i, pltpu.roll(plane.reshape(rows, lanes), 2 * i + 1, 1), total)

    total = rim(jnp.zeros((rows, lanes), F32), 0, grid_ref[PRESS])
    total = rim(rim(total, 1, grid_ref[SAT]), 2, grid_ref[SAT + 1])
    later[2].wait()
    total = rim(total, 3, grid_ref[PERM + 1])
    later[3].wait()
    total = rim(total, 4, grid_ref[DEPTH])
    later[4].wait()
    bit_y = lax.bitwise_and(lax.shift_right_logical(flag_ref[...], 1), 1).astype(F32)
    total = rim(total, PLANES - 1, bit_y)
    pieces = [
        (i * 2 * EDGE, jnp.transpose(total[i * LANES : (i + 1) * LANES])[: 2 * EDGE])
        for i in range(rows // LANES)
    ]
    for first, piece in pieces:
        lying_ref[first : first + 2 * EDGE, :] = piece
    high, low = (
        jnp.concatenate([lying_ref[pl.ds(first + k, EDGE, stride=2), :] for first, _ in pieces], axis=1)
        for k in range(2)
    )
    x_even, y_even = is_even("gx"), is_even("gy")
    ya_ref[...] = jnp.where(y_even, high, low)
    yb_ref[...] = jnp.where(y_even, low, high)
    last = width - 1
    ends = [
        [
            grid_ref[PRESS, :, edge, :],
            grid_ref[SAT, :, edge, :],
            grid_ref[SAT + 1, :, edge, :],
            grid_ref[PERM, :, edge, :],
            grid_ref[DEPTH, :, edge, :],
            lax.bitwise_and(flag_ref[:, edge, :], 1).astype(F32),
        ]
        for edge in (last, 0)
    ]
    for i, (high, low) in enumerate(zip(*ends)):
        xa_ref[i * layers : (i + 1) * layers, :] = jnp.where(x_even, high, low)
        xb_ref[i * layers : (i + 1) * layers, :] = jnp.where(x_even, low, high)
    for copy in later[5:] + outgoing:
        copy.wait()


def upright(rows_list, lanes):
    stack = jnp.concatenate(rows_list, axis=0)
    stack = jnp.concatenate([stack, jnp.zeros((lanes - stack.shape[0], stack.shape[1]), F32)], axis=0)
    return jnp.transpose(stack)


def inverse(x):
    guess = pl.reciprocal(x, approx=True)
    return guess * (2.0 - x * guess)


def phase_weights(pressure):
    b_oil = 1.0 + COMP_OIL * (pressure - 1.0)
    b_water = 1.0 + COMP_WATER * (pressure - 1.0)
    whole = inverse(b_oil * b_water * pressure)
    other = pressure * whole
    return b_water * other, b_oil * other, b_oil * b_water * whole


def faces(perm, perm_next, mob, mob_next, first_up):
    transmit = 2.0 * perm * perm_next * inverse(perm + perm_next)
    return [transmit * jnp.where(first_up, a, b) for a, b in zip(mob, mob_next)]


def weighted(weights, flux):
    oil, water, gas = (w * f for w, f in zip(weights, flux))
    return oil + water + gas, GRAV_OIL * oil + GRAV_WATER * water + GRAV_GAS * gas


def outer_face(own, other, own_up):
    mob, mob_other = phase_mobility(*own[:3]), phase_mobility(*other[:3])
    coupling, lift = weighted(phase_weights(own[0]), faces(own[3], other[3], mob, mob_other, own_up))
    return coupling, lift * (own[4] - other[4]), coupling * other[0]


def main_terms(given_ref, after_ref, flag_ref, cell_ref, well_ref, index_ref, grid_ref, share_ref):
    layers, width, lanes = flag_ref.shape
    rows = layers * width
    row, lane = places(cell_ref[...], lanes)
    share_ref[...] = cell_scatter(live_index(well_ref, index_ref), row, lane, rows, lanes)
    x_last = iota((width, lanes), 0) == width - 1
    y_last = iota((width, lanes), 1) == lanes - 1

    def layer(z):
        press = grid_ref[PRESS, z]
        return press, phase_mobility(press, grid_ref[SAT, z], grid_ref[SAT + 1, z])

    this = layer(0)
    before = None
    for z in range(layers):
        press, mob = this
        following = layer(z + 1) if z + 1 < layers else None
        sat_water, sat_gas = grid_ref[SAT, z], grid_ref[SAT + 1, z]
        sat_oil = 1.0 - sat_water - sat_gas
        depth = grid_ref[DEPTH, z]
        flags = flag_ref[z]
        weights = phase_weights(press)
        storage = grid_ref[PORE, z] * (
            sat_oil * COMP_OIL * weights[0] + sat_water * COMP_WATER * weights[1] + sat_gas * weights[2]
        )
        mobility = total_mobility(sat_water, sat_gas)
        diag = storage + mobility * share_ref[z * width : (z + 1) * width, :]
        rhs = storage * press
        for i, weight in enumerate(weights):
            rhs = rhs - weight * grid_ref[RES + i, z]
        around = jnp.zeros_like(press)
        couplings = {}

        def add(name, flux, drop, beside):
            nonlocal diag, rhs, around
            coupling, lift = weighted(weights, flux)
            couplings[name] = coupling
            diag = diag + coupling
            rhs = rhs + lift * drop
            around = around + coupling * beside

        for dim, size, end, bit in ((0, width, x_last, 1), (1, lanes, y_last, 2)):
            perm = grid_ref[PERM + dim, z]
            perm_next = jnp.where(end, 0.0, pltpu.roll(perm, size - 1, dim))
            up = lax.bitwise_and(flags, bit) > 0
            flux = faces(perm, perm_next, mob, [pltpu.roll(a, size - 1, dim) for a in mob], up)
            drop = depth - pltpu.roll(depth, size - 1, dim)
            add(2 * dim, flux, drop, pltpu.roll(press, size - 1, dim))
            add(2 * dim + 1, [pltpu.roll(a, 1, dim) for a in flux], -pltpu.roll(drop, 1, dim), pltpu.roll(press, 1, dim))
        if following is not None:
            up = lax.bitwise_and(flags, 4) > 0
            flux = faces(grid_ref[PERM + 2, z], grid_ref[PERM + 2, z + 1], mob, following[1], up)
            drop = depth - grid_ref[DEPTH, z + 1]
            add(4, flux, drop, following[0])
        if before is not None:
            add(5, before[0], -before[1], before[2])
        if following is not None:
            before = (flux, drop, press)
        for name, coupling in couplings.items():
            grid_ref[COUP + name, z] = coupling
        grid_ref[DIAG, z] = diag
        grid_ref[RHS, z] = rhs
        grid_ref[AROUND, z] = around
        grid_ref[MOB, z] = mobility
        this = following


def slot_bhp(bhp, well_ref, index_ref):
    well_row, well_lane = places(well_ref[...], LANES)
    return live_index(well_ref, index_ref) * well_gather(bhp, well_row, well_lane)


def sides(a, b, axis):
    even = is_even(axis)
    return jnp.where(even, a, b), jnp.where(even, b, a)


def close_ends(nxt, prev, axis):
    me = lax.axis_index(axis)
    nxt[3] = jnp.where(me < lax.axis_size(axis) - 1, nxt[3], 0.0)
    prev[3] = jnp.where(me > 0, prev[3], 0.0)


def outer_terms(
    given_ref, own_yb_ref, own_xb_ref, own_xa_ref, own_ya_ref, yb_ref, xb_ref, xa_ref, ya_ref,
    grid_ref, bound_ref, flank_ref, side_ref,
):
    layers, width, lanes = grid_ref.shape[1:]
    rows = layers * width
    (high, low), (nxt, prev) = (
        sides(own_xa_ref[...], own_xb_ref[...], "gx"), sides(xa_ref[...], xb_ref[...], "gx")
    )
    high, low, nxt, prev = (
        [rim[i * layers : (i + 1) * layers] for i in range(PLANES)] for rim in (high, low, nxt, prev)
    )
    close_ends(nxt, prev, "gx")
    for where, edge, terms in (
        (0, width - 1, outer_face(high, nxt, high[5] > 0.5)),
        (1, 0, outer_face(low, prev, prev[5] < 0.5)),
    ):
        bound_ref[where] = terms[0]
        for name, term in zip((DIAG, RHS, AROUND), terms):
            grid_ref[name, :, edge, :] = grid_ref[name, :, edge, :] + term
    (high, low), (nxt, prev) = (
        sides(own_ya_ref[...], own_yb_ref[...], "gy"), sides(ya_ref[...], yb_ref[...], "gy")
    )
    high, low, nxt, prev = ([rim[i : i + 1] for i in range(PLANES)] for rim in (high, low, nxt, prev))
    close_ends(nxt, prev, "gy")
    after = outer_face(high, nxt, high[5] > 0.5)
    behind = outer_face(low, prev, prev[5] < 0.5)
    flank_ref[0:1, :] = after[0]
    flank_ref[1:2, :] = behind[0]
    stand = upright(list(behind + after), lanes)
    stand = jnp.concatenate([part.astype(BF16) for part in halves(stand)], axis=1)
    wide = (2 * lanes, 3 * lanes)
    from_lane = lax.rem(iota(wide, 0), lanes)
    to_plane, to_lane = places(iota(wide, 1), lanes)
    side_ref[...] = nn(
        stand,
        ones_of(
            ((from_lane == to_plane) & (to_lane == 0)) | ((from_lane == to_plane + 3) & (to_lane == lanes - 1))
        ),
    )
    for z in range(layers):
        here = slice(z * width, (z + 1) * width)
        diag, rhs, around = (
            grid_ref[name, z] + side_ref[here, i * lanes : (i + 1) * lanes]
            for i, name in enumerate((DIAG, RHS, AROUND))
        )
        scale = RELAXATION * inverse(diag)
        rhs = scale * rhs
        grid_ref[CURRENT, z] = (1.0 - RELAXATION) * grid_ref[PRESS, z] + rhs + scale * around
        grid_ref[SCALE, z] = scale
        grid_ref[RHS, z] = rhs
        grid_ref[GAIN, z] = scale * grid_ref[MOB, z]


def first_update(
    given_ref, sums_ref, cell_ref, well_ref, index_ref,
    grid_ref, out_ref, yb_ref, xb_ref, xa_ref, ya_ref, known_ref, block_ref, sems,
):
    layers, width, lanes = grid_ref.shape[1:]
    rows = layers * width
    count = lax.axis_size("gx") * lax.axis_size("gy")
    chunk = sums_ref.shape[0] // count
    well_rows = (chunk - 2) // 2
    group = count // well_rows
    my = lax.axis_index("gy")
    part = sums_ref[0:well_rows, :]
    base = sums_ref[well_rows : 2 * well_rows, :]
    for d in range(1, count):
        part = part + sums_ref[d * chunk : d * chunk + well_rows, :]
        base = base + sums_ref[d * chunk + well_rows : d * chunk + 2 * well_rows, :]
    controls = []
    for k in (2 * well_rows, 2 * well_rows + 1):
        total = sums_ref[pl.ds(k, well_rows, stride=group * chunk), :]
        for j in range(1, group):
            total = total + sums_ref[pl.ds(j * chunk + k, well_rows, stride=group * chunk), :]
        controls.append(total)
    mode, target = controls
    bhp = jnp.where(mode < 0.5, target, (part - target) / base)
    known_ref[0] = mode
    known_ref[1] = target
    known_ref[2] = base
    row, lane = places(cell_ref[...], lanes)
    well_row, well_lane = places(well_ref[...], LANES)
    push = cell_scatter(slot_bhp(bhp, well_ref, index_ref), row, lane, rows, lanes)
    current = grid_ref[CURRENT].reshape(rows, lanes) + grid_ref[GAIN].reshape(rows, lanes) * push
    grid_ref[CURRENT] = current.reshape(layers, width, lanes)
    xa_ref[...], xb_ref[...] = sides(
        grid_ref[CURRENT, :, width - 1, :], grid_ref[CURRENT, :, 0, :], "gx"
    )
    at_cell = cell_find(grid_ref[MOB].reshape(rows, lanes) * current, *cell_pick(row, lane, rows, lanes))
    (part,) = well_scatter([live_index(well_ref, index_ref) * at_cell], well_row, well_lane, well_rows)
    block_ref[...] = jnp.concatenate([part] * (block_ref.shape[0] // well_rows), axis=0)
    outgoing = repeat_out(block_ref, out_ref, sems)
    both = jnp.concatenate([half.astype(BF16) for half in halves(current)], axis=1)
    pick_row, pick_lane = iota((2 * EDGE, 2 * lanes), 0), lax.rem(iota((2 * EDGE, 2 * lanes), 1), lanes)
    rims = nt(
        ones_of(((pick_row == 0) & (pick_lane == lanes - 1)) | ((pick_row == 1) & (pick_lane == 0))), both
    )
    ya_ref[...], yb_ref[...] = sides(rims[0:1], rims[1:2], "gy")
    for copy in outgoing:
        copy.wait()


def inner_terms(after_ref, grid_ref, out_ref):
    layers, width, lanes = out_ref.shape
    for z in range(layers):
        current = grid_ref[CURRENT, z]
        besides = [
            pltpu.roll(current, width - 1, 0),
            pltpu.roll(current, 1, 0),
            pltpu.roll(current, lanes - 1, 1),
            pltpu.roll(current, 1, 1),
        ]
        around = grid_ref[COUP, z] * besides[0]
        for i in range(1, 4):
            around = around + grid_ref[COUP + i, z] * besides[i]
        if z + 1 < layers:
            around = around + grid_ref[COUP + 4, z] * grid_ref[CURRENT, z + 1]
        if z > 0:
            around = around + grid_ref[COUP + 5, z] * grid_ref[CURRENT, z - 1]
        out_ref[z] = (1.0 - RELAXATION) * current + grid_ref[RHS, z] + grid_ref[SCALE, z] * around


def last_update(
    sums_ref, known_ref, cell_ref, well_ref, index_ref, grid_ref, inner_ref, bound_ref, flank_ref,
    yb_ref, xb_ref, xa_ref, ya_ref, out_ref, bhp_ref, push_ref, side_ref,
):
    layers, width, lanes = out_ref.shape
    rows = layers * width
    count = lax.axis_size("gx") * lax.axis_size("gy")
    height = sums_ref.shape[0] // count
    well_rows = known_ref.shape[1]
    me = lax.axis_index(AXES)
    part = sums_ref[0:well_rows, :]
    for d in range(1, count):
        part = part + sums_ref[d * height : d * height + well_rows, :]
    bhp = jnp.where(known_ref[0] < 0.5, known_ref[1], (part - known_ref[1]) / known_ref[2])
    owned = bhp_ref.shape[1]
    group = LANES // owned
    line = jnp.sum(
        jnp.where(iota(bhp.shape, 0) == me // group, bhp, 0.0), axis=0, keepdims=True
    )
    line = pltpu.roll(line, lax.rem(LANES - lax.rem(me, group) * owned, LANES), 1)
    bhp_ref[...] = line[:, :owned]
    row, lane = places(cell_ref[...], lanes)
    push_ref[...] = cell_scatter(slot_bhp(bhp, well_ref, index_ref), row, lane, rows, lanes)
    nxt, prev = sides(ya_ref[...], yb_ref[...], "gy")
    side_ref[...] = upright([flank_ref[1:2, :] * prev, flank_ref[0:1, :] * nxt], lanes)
    along = iota((width, lanes), 1)
    nxt, prev = sides(xa_ref[...], xb_ref[...], "gx")
    for z in range(layers):
        here = slice(z * width, (z + 1) * width)
        side = side_ref[here, :]
        side = jnp.where(along == 0, side, jnp.where(along == lanes - 1, pltpu.roll(side, lanes - 2, 1), 0.0))
        out_ref[z] = inner_ref[z] + grid_ref[GAIN, z] * push_ref[here, :] + grid_ref[SCALE, z] * side
    for where, edge, beyond in ((0, width - 1, nxt), (1, 0, prev)):
        out_ref[:, edge, :] = out_ref[:, edge, :] + grid_ref[SCALE, :, edge, :] * (bound_ref[where] * beyond)


def call(kernel, outs, args, scratch=(), spaces=None, out_spaces=None, aliases=None):
    shapes = [jax.ShapeDtypeStruct(item, F32) if isinstance(item, tuple) else item for item in outs]
    spaces = spaces or [pltpu.VMEM] * len(args)
    out_spaces = out_spaces or [pltpu.VMEM] * len(outs)
    args = [
        pltpu.with_memory_space_constraint(arg, space) if space is pltpu.HBM else arg
        for arg, space in zip(args, spaces)
    ]
    return pl.pallas_call(
        kernel,
        out_shape=shapes,
        in_specs=[pl.BlockSpec(memory_space=space) for space in spaces],
        out_specs=[pl.BlockSpec(memory_space=space) for space in out_spaces],
        scratch_shapes=[pltpu.VMEM(item, F32) if isinstance(item, tuple) else item for item in scratch],
        input_output_aliases=aliases or {},
        compiler_params=pltpu.CompilerParams(vmem_limit_bytes=24 * 1024 * 1024),
        cost_estimate=pl.CostEstimate(flops=1_000_000, bytes_accessed=4_000_000, transcendentals=0),
    )(*args)


def whole_tiles(height, step, count):
    chunks = step
    while chunks * height % 8:
        chunks += step
    assert count % chunks == 0
    return chunks * height


def everyone(rows, count):
    height = rows.shape[0] // count
    swapped = lax.all_to_all(rows.reshape(count, height, 1, LANES), AXES, 0, 0, tiled=True)
    return swapped.reshape(rows.shape)


def to_pair(block, axis):
    count = lax.axis_size(axis)
    assert count % 2 == 0
    return lax.ppermute(block, axis, [(i, i ^ 1) for i in range(count)])


def to_other(block, axis):
    sizes = {name: lax.axis_size(name) for name in AXES}
    moves = []
    for gx in range(sizes["gx"]):
        for gy in range(sizes["gy"]):
            there = {"gx": gx, "gy": gy}
            away = there[axis] + (1 if there[axis] % 2 else -1)
            if 0 <= away < sizes[axis]:
                there[axis] = away
            else:
                cross = "gy" if axis == "gx" else "gx"
                there[cross] ^= 1
            moves.append((gx * sizes["gy"] + gy, there["gx"] * sizes["gy"] + there["gy"]))
    return lax.ppermute(block, AXES, moves)


def body(
    pressure, saturation, permeability, pore_volume, cell_depth, residual, upstream_flags,
    perf_cell, perf_well, perf_index, well_mode, well_target,
):
    layers, width, lanes = pressure.shape
    rows = layers * width
    count = lax.axis_size("gx") * lax.axis_size("gy")
    owned = well_mode.shape[0]
    well_rows = owned * count // LANES
    chunk = 2 * well_rows + 2
    grid = (layers, width, lanes)
    slots = [perf_cell, perf_well, perf_index]
    operands = slots + [
        well_mode[None], well_target[None], saturation, pressure, permeability, cell_depth,
        upstream_flags, pore_volume, residual,
    ]
    height = whole_tiles(chunk, 1, count)
    sums, yb, xb, xa, ya, given, flags = call(
        opening,
        [
            (count * chunk, LANES), (EDGE, rows), (PLANES * layers, lanes), (PLANES * layers, lanes),
            (EDGE, rows), (GRIDS,) + grid, jax.ShapeDtypeStruct(grid, upstream_flags.dtype),
        ],
        operands,
        [pltpu.VMEM(a.shape, a.dtype) for a in operands[:5]]
        + [(height, LANES), (2 * EDGE * (rows // LANES), LANES), pltpu.SemaphoreType.DMA((INPUTS,))]
        + [pltpu.SemaphoreType.DMA((count * chunk // height,))],
        [pltpu.HBM] * INPUTS,
        [pltpu.HBM] + [pltpu.VMEM] * 6,
    )
    rims = [yb, xb, xa, ya]
    rims = rims + [to_other(yb, "gy"), to_other(xb, "gx"), to_pair(xa, "gx"), to_pair(ya, "gy")]
    gathered = everyone(sums, count)
    (given,) = call(
        main_terms,
        [(GRIDS,) + grid],
        [given, sums, flags] + slots,
        [(rows, lanes)],
        [pltpu.VMEM, pl.ANY] + [pltpu.VMEM] * 4,
        None,
        {0: 0},
    )
    given, bound, flank = call(
        outer_terms,
        [(GRIDS,) + grid, (2, layers, lanes), (EDGE, rows)],
        [given] + rims,
        [(rows, 3 * lanes)],
        aliases={0: 0},
    )
    height = whole_tiles(well_rows, min(8, count), count)
    given, sums, yb, xb, xa, ya, known = call(
        first_update,
        [
            (GRIDS,) + grid, (count * well_rows, LANES), (1, rows), (layers, lanes), (layers, lanes), (1, rows),
            (3, well_rows, LANES),
        ],
        [given, gathered] + slots,
        [(height, LANES), pltpu.SemaphoreType.DMA((count * well_rows // height,))],
        None,
        [pltpu.VMEM, pltpu.HBM] + [pltpu.VMEM] * 5,
        {0: 0},
    )
    gathered = everyone(sums, count)
    rims = [to_other(yb, "gy"), to_other(xb, "gx"), to_pair(xa, "gx"), to_pair(ya, "gy")]
    (inner,) = call(inner_terms, [grid], [sums, given], (), [pl.ANY, pltpu.VMEM])
    out, bhp = call(
        last_update,
        [grid, (1, owned)],
        [gathered, known] + slots + [given, inner, bound, flank] + rims,
        [(rows, lanes), (rows, lanes)],
    )
    return out, bhp[0]


def solution(mesh):
    return jax.shard_map(
        body,
        mesh=mesh,
        in_specs=(
            P(None, "gx", "gy"),
            P(None, None, "gx", "gy"),
            P(None, None, "gx", "gy"),
            P(None, "gx", "gy"),
            P(None, "gx", "gy"),
            P(None, None, "gx", "gy"),
            P(None, "gx", "gy"),
            P(("gx", "gy"), None),
            P(("gx", "gy"), None),
            P(("gx", "gy"), None),
            P(("gx", "gy")),
            P(("gx", "gy")),
        ),
        out_specs=(P(None, "gx", "gy"), P(("gx", "gy"))),
        check_vma=False,
    )
```

```python
import jax
import jax.numpy as jnp
from jax import lax
from jax.experimental import pallas as pl
from jax.experimental.pallas import tpu as pltpu
from jax.sharding import PartitionSpec as P

COMP_OIL = 0.2
COMP_WATER = 0.05
GRAV_OIL = 0.4
GRAV_WATER = 0.5
GRAV_GAS = 0.08
RELAXATION = 0.8
LANES = 128
PLANES = 6
INPUTS = 10
PRESS, SAT, PERM, DEPTH, PORE, RES, GRIDS = 0, 1, 3, 6, 7, 8, 11
DIAG, RHS, COUP, MOB, AROUND = 1, 2, 3, 9, 10
CURRENT, SCALE, GAIN = 0, 1, 10
EDGE = 8

F32 = jnp.float32
BF16 = jnp.bfloat16
AXES = ("gx", "gy")


def nn(a, b):
    return lax.dot_general(a, b, (((1,), (0,)), ((), ())), preferred_element_type=F32)


def nt(a, b):
    return lax.dot_general(a, b, (((1,), (1,)), ((), ())), preferred_element_type=F32)


def halves(x):
    high = x.astype(BF16).astype(F32)
    return high, x - high


def iota(shape, dim):
    return lax.broadcasted_iota(jnp.int32, shape, dim)


def hot(index, count):
    return iota((count, index.shape[1]), 0) == index


def ones_of(mask):
    return jnp.where(mask, 1.0, 0.0).astype(BF16)


def bits_of(n):
    assert n & (n - 1) == 0
    return n.bit_length() - 1


def places(index, width):
    return lax.shift_right_arithmetic(index, bits_of(width)), lax.bitwise_and(index, width - 1)


def cell_pick(row, lane, rows, lanes):
    pick = ones_of(hot(lane, lanes))
    return jnp.concatenate([pick, pick], axis=0), hot(row, rows)


def cell_find(fields, pick, at_row):
    rows = at_row.shape[0]
    both = [
        jnp.concatenate([part.astype(BF16) for part in halves(field)], axis=1) for field in fields
    ]
    found = nn(jnp.concatenate(both, axis=0), pick)
    return [
        jnp.sum(jnp.where(at_row, found[i * rows : (i + 1) * rows], 0.0), axis=0, keepdims=True)
        for i in range(len(fields))
    ]


def cell_scatter(value, row, lane, rows, lanes):
    spread = jnp.where(hot(lane, lanes), value, 0.0)
    spread = jnp.concatenate([part.astype(BF16) for part in halves(spread)], axis=0)
    total = nt(ones_of(hot(row, rows)), spread)
    return total[:, :lanes] + total[:, lanes:]


def well_scatter(values, row, lane, rows):
    mine = hot(row, rows)
    stack = []
    for value in values:
        stack.extend(halves(jnp.where(mine, value, 0.0)))
    total = nt(jnp.concatenate(stack, axis=0).astype(BF16), ones_of(hot(lane, LANES)))
    return [
        total[2 * i * rows : (2 * i + 1) * rows] + total[(2 * i + 1) * rows : (2 * i + 2) * rows]
        for i in range(len(values))
    ]


def well_gather(field, row, lane):
    rows = field.shape[0]
    both = jnp.concatenate(halves(field), axis=0).astype(BF16)
    found = nn(both, ones_of(hot(lane, LANES)))
    return jnp.sum(
        jnp.where(hot(row, rows), found[:rows] + found[rows:], 0.0), axis=0, keepdims=True
    )


def total_mobility(sat_water, sat_gas):
    sat_oil = 1.0 - sat_water - sat_gas
    return 0.5 * sat_oil * sat_oil + sat_water * sat_water + 5.0 * (sat_gas * sat_gas)


def phase_mobility(pressure, sat_water, sat_gas):
    sat_oil = 1.0 - sat_water - sat_gas
    b_oil = 1.0 + COMP_OIL * (pressure - 1.0)
    b_water = 1.0 + COMP_WATER * (pressure - 1.0)
    return (
        sat_oil * sat_oil * b_oil * 0.5,
        sat_water * sat_water * b_water,
        sat_gas * sat_gas * pressure * 5.0,
    )


def live_index(well_ref, index_ref):
    return jnp.where(well_ref[...] >= 0, index_ref[...], 0.0)


def fetch(sources, holds, sems):
    copies = [
        pltpu.make_async_copy(source, hold, sems.at[i])
        for i, (source, hold) in enumerate(zip(sources, holds))
    ]
    for copy in copies:
        copy.start()
    return copies


def repeat_out(block_ref, out_ref, sem):
    height = block_ref.shape[0]
    copies = [
        pltpu.make_async_copy(block_ref, out_ref.at[pl.ds(i * height, height)], sem.at[i])
        for i in range(out_ref.shape[0] // height)
    ]
    for copy in copies:
        copy.start()
    return copies


def is_even(axis):
    return lax.rem(lax.axis_index(axis), 2) == 0


def opening(*refs):
    inputs, sems = refs[:INPUTS], refs[-1]
    keep_ref, give_ref, grid_ref, flag_ref = refs[INPUTS : INPUTS + 4]
    cell_ref, well_ref, index_ref = slot_refs = refs[INPUTS + 4 : -1]
    holds = list(slot_refs) + [
        grid_ref.at[SAT : SAT + 2], grid_ref.at[PRESS], grid_ref.at[PERM : PERM + 3], grid_ref.at[DEPTH],
        flag_ref, grid_ref.at[PORE], grid_ref.at[RES : RES + 3],
    ]
    copies = fetch(inputs, holds, sems)
    layers, width, lanes = flag_ref.shape
    rows = layers * width
    well_rows = keep_ref.shape[0]
    for copy in copies[: len(slot_refs)]:
        copy.wait()
    row, lane = places(cell_ref[...], lanes)
    well_row, well_lane = places(well_ref[...], LANES)
    pick, at_row = cell_pick(row, lane, rows, lanes)
    index = live_index(well_ref, index_ref)
    later = copies[len(slot_refs) :]
    later[0].wait()
    mobility = total_mobility(grid_ref[SAT].reshape(rows, lanes), grid_ref[SAT + 1].reshape(rows, lanes))
    later[1].wait()
    press = grid_ref[PRESS].reshape(rows, lanes)
    at_mob, at_press = cell_find([mobility, mobility * press], pick, at_row)
    part, base = well_scatter([index * at_press, index * at_mob], well_row, well_lane, well_rows)
    half = well_rows // 2
    keep_ref[...], give_ref[...] = sides(
        jnp.concatenate([part[:half], base[:half]], axis=0),
        jnp.concatenate([part[half:], base[half:]], axis=0),
        "gy",
    )
    for copy in later[2:]:
        copy.wait()


def sides(a, b, axis):
    even = is_even(axis)
    return jnp.where(even, a, b), jnp.where(even, b, a)


def pair_sums(
    keep_ref, given_ref, mode_ref, target_ref, grid_ref, flag_ref,
    out_ref, yb_ref, xb_ref, xa_ref, ya_ref, lying_ref, block_ref, sems,
):
    owned = mode_ref.shape[1]
    group = LANES // owned
    here = lax.shift_right_logical(iota((1, LANES), 1), bits_of(owned)) == lax.rem(
        lax.axis_index(AXES), group
    )
    controls = [
        jnp.where(here, jnp.concatenate([ref[...].astype(F32)] * group, axis=1), 0.0)
        for ref in (mode_ref, target_ref)
    ]
    block = jnp.concatenate([keep_ref[...] + given_ref[...]] + controls, axis=0)
    block_ref[...] = jnp.concatenate([block] * (block_ref.shape[0] // block.shape[0]), axis=0)
    copies = repeat_out(block_ref, out_ref, sems)
    layers, width, lanes = flag_ref.shape
    rows = layers * width
    pair = lax.shift_right_logical(iota((rows, lanes), 1), 1)

    def rim(total, i, plane):
        return jnp.where(pair == i, pltpu.roll(plane.reshape(rows, lanes), 2 * i + 1, 1), total)

    total = rim(jnp.zeros((rows, lanes), F32), 0, grid_ref[PRESS])
    total = rim(rim(total, 1, grid_ref[SAT]), 2, grid_ref[SAT + 1])
    total = rim(total, 3, grid_ref[PERM + 1])
    total = rim(total, 4, grid_ref[DEPTH])
    bit_y = lax.bitwise_and(lax.shift_right_logical(flag_ref[...], 1), 1).astype(F32)
    total = rim(total, PLANES - 1, bit_y)
    pieces = [
        (i * 2 * EDGE, jnp.transpose(total[i * LANES : (i + 1) * LANES])[: 2 * EDGE])
        for i in range(rows // LANES)
    ]
    for first, piece in pieces:
        lying_ref[first : first + 2 * EDGE, :] = piece
    high, low = (
        jnp.concatenate([lying_ref[pl.ds(first + k, EDGE, stride=2), :] for first, _ in pieces], axis=1)
        for k in range(2)
    )
    x_even, y_even = is_even("gx"), is_even("gy")
    ya_ref[...] = jnp.where(y_even, high, low)
    yb_ref[...] = jnp.where(y_even, low, high)
    last = width - 1
    ends = [
        [
            grid_ref[PRESS, :, edge, :],
            grid_ref[SAT, :, edge, :],
            grid_ref[SAT + 1, :, edge, :],
            grid_ref[PERM, :, edge, :],
            grid_ref[DEPTH, :, edge, :],
            lax.bitwise_and(flag_ref[:, edge, :], 1).astype(F32),
        ]
        for edge in (last, 0)
    ]
    for i, (high, low) in enumerate(zip(*ends)):
        xa_ref[i * layers : (i + 1) * layers, :] = jnp.where(x_even, high, low)
        xb_ref[i * layers : (i + 1) * layers, :] = jnp.where(x_even, low, high)
    for copy in copies:
        copy.wait()


def upright(rows_list, lanes):
    stack = jnp.concatenate(rows_list, axis=0)
    stack = jnp.concatenate([stack, jnp.zeros((lanes - stack.shape[0], stack.shape[1]), F32)], axis=0)
    return jnp.transpose(stack)


def inverse(x):
    guess = pl.reciprocal(x, approx=True)
    return guess * (2.0 - x * guess)


def phase_weights(pressure):
    b_oil = 1.0 + COMP_OIL * (pressure - 1.0)
    b_water = 1.0 + COMP_WATER * (pressure - 1.0)
    whole = inverse(b_oil * b_water * pressure)
    other = pressure * whole
    return b_water * other, b_oil * other, b_oil * b_water * whole


def faces(perm, perm_next, mob, mob_next, first_up):
    transmit = 2.0 * perm * perm_next * inverse(perm + perm_next)
    return [transmit * jnp.where(first_up, a, b) for a, b in zip(mob, mob_next)]


def weighted(weights, flux):
    oil, water, gas = (w * f for w, f in zip(weights, flux))
    return oil + water + gas, GRAV_OIL * oil + GRAV_WATER * water + GRAV_GAS * gas


def outer_face(own, other, own_up):
    mob, mob_other = phase_mobility(*own[:3]), phase_mobility(*other[:3])
    coupling, lift = weighted(phase_weights(own[0]), faces(own[3], other[3], mob, mob_other, own_up))
    return coupling, lift * (own[4] - other[4]), coupling * other[0]


def main_terms(given_ref, after_ref, flag_ref, cell_ref, well_ref, index_ref, grid_ref, share_ref):
    layers, width, lanes = flag_ref.shape
    rows = layers * width
    row, lane = places(cell_ref[...], lanes)
    share_ref[...] = cell_scatter(live_index(well_ref, index_ref), row, lane, rows, lanes)
    x_last = iota((width, lanes), 0) == width - 1
    y_last = iota((width, lanes), 1) == lanes - 1

    def layer(z):
        press = grid_ref[PRESS, z]
        return press, phase_mobility(press, grid_ref[SAT, z], grid_ref[SAT + 1, z])

    this = layer(0)
    before = None
    for z in range(layers):
        press, mob = this
        following = layer(z + 1) if z + 1 < layers else None
        sat_water, sat_gas = grid_ref[SAT, z], grid_ref[SAT + 1, z]
        sat_oil = 1.0 - sat_water - sat_gas
        depth = grid_ref[DEPTH, z]
        flags = flag_ref[z]
        weights = phase_weights(press)
        storage = grid_ref[PORE, z] * (
            sat_oil * COMP_OIL * weights[0] + sat_water * COMP_WATER * weights[1] + sat_gas * weights[2]
        )
        mobility = total_mobility(sat_water, sat_gas)
        diag = storage + mobility * share_ref[z * width : (z + 1) * width, :]
        rhs = storage * press
        for i, weight in enumerate(weights):
            rhs = rhs - weight * grid_ref[RES + i, z]
        around = jnp.zeros_like(press)
        couplings = {}

        def add(name, flux, drop, beside):
            nonlocal diag, rhs, around
            coupling, lift = weighted(weights, flux)
            couplings[name] = coupling
            diag = diag + coupling
            rhs = rhs + lift * drop
            around = around + coupling * beside

        for dim, size, end, bit in ((0, width, x_last, 1), (1, lanes, y_last, 2)):
            perm = grid_ref[PERM + dim, z]
            perm_next = jnp.where(end, 0.0, pltpu.roll(perm, size - 1, dim))
            up = lax.bitwise_and(flags, bit) > 0
            flux = faces(perm, perm_next, mob, [pltpu.roll(a, size - 1, dim) for a in mob], up)
            drop = depth - pltpu.roll(depth, size - 1, dim)
            add(2 * dim, flux, drop, pltpu.roll(press, size - 1, dim))
            add(2 * dim + 1, [pltpu.roll(a, 1, dim) for a in flux], -pltpu.roll(drop, 1, dim), pltpu.roll(press, 1, dim))
        if following is not None:
            up = lax.bitwise_and(flags, 4) > 0
            flux = faces(grid_ref[PERM + 2, z], grid_ref[PERM + 2, z + 1], mob, following[1], up)
            drop = depth - grid_ref[DEPTH, z + 1]
            add(4, flux, drop, following[0])
        if before is not None:
            add(5, before[0], -before[1], before[2])
        if following is not None:
            before = (flux, drop, press)
        for name, coupling in couplings.items():
            grid_ref[COUP + name, z] = coupling
        grid_ref[DIAG, z] = diag
        grid_ref[RHS, z] = rhs
        grid_ref[AROUND, z] = around
        grid_ref[MOB, z] = mobility
        this = following


def slot_bhp(bhp, well_ref, index_ref):
    well_row, well_lane = places(well_ref[...], LANES)
    return live_index(well_ref, index_ref) * well_gather(bhp, well_row, well_lane)


def close_ends(nxt, prev, axis):
    me = lax.axis_index(axis)
    nxt[3] = jnp.where(me < lax.axis_size(axis) - 1, nxt[3], 0.0)
    prev[3] = jnp.where(me > 0, prev[3], 0.0)


def outer_terms(
    given_ref, own_yb_ref, own_xb_ref, own_xa_ref, own_ya_ref, yb_ref, xb_ref, xa_ref, ya_ref,
    grid_ref, bound_ref, flank_ref, side_ref,
):
    layers, width, lanes = grid_ref.shape[1:]
    rows = layers * width
    (high, low), (nxt, prev) = (
        sides(own_xa_ref[...], own_xb_ref[...], "gx"), sides(xa_ref[...], xb_ref[...], "gx")
    )
    high, low, nxt, prev = (
        [rim[i * layers : (i + 1) * layers] for i in range(PLANES)] for rim in (high, low, nxt, prev)
    )
    close_ends(nxt, prev, "gx")
    for where, edge, terms in (
        (0, width - 1, outer_face(high, nxt, high[5] > 0.5)),
        (1, 0, outer_face(low, prev, prev[5] < 0.5)),
    ):
        bound_ref[where] = terms[0]
        for name, term in zip((DIAG, RHS, AROUND), terms):
            grid_ref[name, :, edge, :] = grid_ref[name, :, edge, :] + term
    (high, low), (nxt, prev) = (
        sides(own_ya_ref[...], own_yb_ref[...], "gy"), sides(ya_ref[...], yb_ref[...], "gy")
    )
    high, low, nxt, prev = ([rim[i : i + 1] for i in range(PLANES)] for rim in (high, low, nxt, prev))
    close_ends(nxt, prev, "gy")
    after = outer_face(high, nxt, high[5] > 0.5)
    behind = outer_face(low, prev, prev[5] < 0.5)
    flank_ref[0:1, :] = after[0]
    flank_ref[1:2, :] = behind[0]
    stand = upright(list(behind + after), lanes)
    stand = jnp.concatenate([part.astype(BF16) for part in halves(stand)], axis=1)
    wide = (2 * lanes, 3 * lanes)
    from_lane = lax.rem(iota(wide, 0), lanes)
    to_plane, to_lane = places(iota(wide, 1), lanes)
    side_ref[...] = nn(
        stand,
        ones_of(
            ((from_lane == to_plane) & (to_lane == 0)) | ((from_lane == to_plane + 3) & (to_lane == lanes - 1))
        ),
    )
    for z in range(layers):
        here = slice(z * width, (z + 1) * width)
        diag, rhs, around = (
            grid_ref[name, z] + side_ref[here, i * lanes : (i + 1) * lanes]
            for i, name in enumerate((DIAG, RHS, AROUND))
        )
        scale = RELAXATION * inverse(diag)
        rhs = scale * rhs
        grid_ref[CURRENT, z] = (1.0 - RELAXATION) * grid_ref[PRESS, z] + rhs + scale * around
        grid_ref[SCALE, z] = scale
        grid_ref[RHS, z] = rhs
        grid_ref[GAIN, z] = scale * grid_ref[MOB, z]


def first_update(
    given_ref, sums_ref, cell_ref, well_ref, index_ref,
    grid_ref, out_ref, yb_ref, xb_ref, xa_ref, ya_ref, known_ref, block_ref, sems,
):
    layers, width, lanes = grid_ref.shape[1:]
    rows = layers * width
    count = lax.axis_size("gx") * lax.axis_size("gy")
    chunk = sums_ref.shape[0] // count
    well_rows = chunk - 2
    half = well_rows // 2
    group = count // well_rows
    low, high = sums_ref[0:well_rows, :], sums_ref[chunk : chunk + well_rows, :]
    for d in range(2, count, 2):
        low = low + sums_ref[d * chunk : d * chunk + well_rows, :]
        high = high + sums_ref[(d + 1) * chunk : (d + 1) * chunk + well_rows, :]
    part = jnp.concatenate([low[:half], high[:half]], axis=0)
    base = jnp.concatenate([low[half:], high[half:]], axis=0)
    controls = []
    for k in (well_rows, well_rows + 1):
        total = sums_ref[pl.ds(k, well_rows, stride=group * chunk), :]
        for j in range(1, group):
            total = total + sums_ref[pl.ds(j * chunk + k, well_rows, stride=group * chunk), :]
        controls.append(total)
    mode, target = controls
    bhp = jnp.where(mode < 0.5, target, (part - target) / base)
    known_ref[0] = mode
    known_ref[1] = target
    known_ref[2] = base
    row, lane = places(cell_ref[...], lanes)
    well_row, well_lane = places(well_ref[...], LANES)
    push = cell_scatter(slot_bhp(bhp, well_ref, index_ref), row, lane, rows, lanes)
    current = grid_ref[CURRENT].reshape(rows, lanes) + grid_ref[GAIN].reshape(rows, lanes) * push
    grid_ref[CURRENT] = current.reshape(layers, width, lanes)
    xa_ref[...], xb_ref[...] = sides(
        grid_ref[CURRENT, :, width - 1, :], grid_ref[CURRENT, :, 0, :], "gx"
    )
    mobile = grid_ref[MOB].reshape(rows, lanes) * current
    (at_cell,) = cell_find([mobile], *cell_pick(row, lane, rows, lanes))
    (part,) = well_scatter([live_index(well_ref, index_ref) * at_cell], well_row, well_lane, well_rows)
    block_ref[...] = jnp.concatenate([part] * (block_ref.shape[0] // well_rows), axis=0)
    outgoing = repeat_out(block_ref, out_ref, sems)
    both = jnp.concatenate([half.astype(BF16) for half in halves(current)], axis=1)
    pick_row, pick_lane = iota((2 * EDGE, 2 * lanes), 0), lax.rem(iota((2 * EDGE, 2 * lanes), 1), lanes)
    rims = nt(
        ones_of(((pick_row == 0) & (pick_lane == lanes - 1)) | ((pick_row == 1) & (pick_lane == 0))), both
    )
    ya_ref[...], yb_ref[...] = sides(rims[0:1], rims[1:2], "gy")
    for copy in outgoing:
        copy.wait()


def inner_terms(after_ref, grid_ref, out_ref):
    layers, width, lanes = out_ref.shape
    for z in range(layers):
        current = grid_ref[CURRENT, z]
        besides = [
            pltpu.roll(current, width - 1, 0),
            pltpu.roll(current, 1, 0),
            pltpu.roll(current, lanes - 1, 1),
            pltpu.roll(current, 1, 1),
        ]
        around = grid_ref[COUP, z] * besides[0]
        for i in range(1, 4):
            around = around + grid_ref[COUP + i, z] * besides[i]
        if z + 1 < layers:
            around = around + grid_ref[COUP + 4, z] * grid_ref[CURRENT, z + 1]
        if z > 0:
            around = around + grid_ref[COUP + 5, z] * grid_ref[CURRENT, z - 1]
        out_ref[z] = (1.0 - RELAXATION) * current + grid_ref[RHS, z] + grid_ref[SCALE, z] * around


def last_update(
    sums_ref, known_ref, cell_ref, well_ref, index_ref, grid_ref, inner_ref, bound_ref, flank_ref,
    yb_ref, xb_ref, xa_ref, ya_ref, out_ref, bhp_ref, push_ref, side_ref,
):
    layers, width, lanes = out_ref.shape
    rows = layers * width
    count = lax.axis_size("gx") * lax.axis_size("gy")
    height = sums_ref.shape[0] // count
    well_rows = known_ref.shape[1]
    me = lax.axis_index(AXES)
    part = sums_ref[0:well_rows, :]
    for d in range(1, count):
        part = part + sums_ref[d * height : d * height + well_rows, :]
    bhp = jnp.where(known_ref[0] < 0.5, known_ref[1], (part - known_ref[1]) / known_ref[2])
    owned = bhp_ref.shape[1]
    group = LANES // owned
    line = jnp.sum(
        jnp.where(iota(bhp.shape, 0) == me // group, bhp, 0.0), axis=0, keepdims=True
    )
    line = pltpu.roll(line, lax.rem(LANES - lax.rem(me, group) * owned, LANES), 1)
    bhp_ref[...] = line[:, :owned]
    row, lane = places(cell_ref[...], lanes)
    push_ref[...] = cell_scatter(slot_bhp(bhp, well_ref, index_ref), row, lane, rows, lanes)
    nxt, prev = sides(ya_ref[...], yb_ref[...], "gy")
    side_ref[...] = upright([flank_ref[1:2, :] * prev, flank_ref[0:1, :] * nxt], lanes)
    along = iota((width, lanes), 1)
    nxt, prev = sides(xa_ref[...], xb_ref[...], "gx")
    for z in range(layers):
        here = slice(z * width, (z + 1) * width)
        side = side_ref[here, :]
        side = jnp.where(along == 0, side, jnp.where(along == lanes - 1, pltpu.roll(side, lanes - 2, 1), 0.0))
        out_ref[z] = inner_ref[z] + grid_ref[GAIN, z] * push_ref[here, :] + grid_ref[SCALE, z] * side
    for where, edge, beyond in ((0, width - 1, nxt), (1, 0, prev)):
        out_ref[:, edge, :] = out_ref[:, edge, :] + grid_ref[SCALE, :, edge, :] * (bound_ref[where] * beyond)


def call(kernel, outs, args, scratch=(), spaces=None, out_spaces=None, aliases=None):
    shapes = [jax.ShapeDtypeStruct(item, F32) if isinstance(item, tuple) else item for item in outs]
    spaces = spaces or [pltpu.VMEM] * len(args)
    out_spaces = out_spaces or [pltpu.VMEM] * len(outs)
    args = [
        pltpu.with_memory_space_constraint(arg, space) if space is pltpu.HBM else arg
        for arg, space in zip(args, spaces)
    ]
    return pl.pallas_call(
        kernel,
        out_shape=shapes,
        in_specs=[pl.BlockSpec(memory_space=space) for space in spaces],
        out_specs=[pl.BlockSpec(memory_space=space) for space in out_spaces],
        scratch_shapes=[pltpu.VMEM(item, F32) if isinstance(item, tuple) else item for item in scratch],
        input_output_aliases=aliases or {},
        compiler_params=pltpu.CompilerParams(vmem_limit_bytes=24 * 1024 * 1024),
        cost_estimate=pl.CostEstimate(flops=1_000_000, bytes_accessed=4_000_000, transcendentals=0),
    )(*args)


def whole_tiles(height, step, count):
    chunks = step
    while chunks * height % 8:
        chunks += step
    assert count % chunks == 0
    return chunks * height


def everyone(rows, count):
    height = rows.shape[0] // count
    swapped = lax.all_to_all(rows.reshape(count, height, 1, LANES), AXES, 0, 0, tiled=True)
    return swapped.reshape(rows.shape)


def to_pair(block, axis):
    count = lax.axis_size(axis)
    assert count % 2 == 0
    return lax.ppermute(block, axis, [(i, i ^ 1) for i in range(count)])


def to_other(block, axis):
    sizes = {name: lax.axis_size(name) for name in AXES}
    moves = []
    for gx in range(sizes["gx"]):
        for gy in range(sizes["gy"]):
            there = {"gx": gx, "gy": gy}
            away = there[axis] + (1 if there[axis] % 2 else -1)
            if 0 <= away < sizes[axis]:
                there[axis] = away
            else:
                cross = "gy" if axis == "gx" else "gx"
                there[cross] ^= 1
            moves.append((gx * sizes["gy"] + gy, there["gx"] * sizes["gy"] + there["gy"]))
    return lax.ppermute(block, AXES, moves)


def body(
    pressure, saturation, permeability, pore_volume, cell_depth, residual, upstream_flags,
    perf_cell, perf_well, perf_index, well_mode, well_target,
):
    layers, width, lanes = pressure.shape
    rows = layers * width
    count = lax.axis_size("gx") * lax.axis_size("gy")
    owned = well_mode.shape[0]
    well_rows = owned * count // LANES
    chunk = well_rows + 2
    grid = (layers, width, lanes)
    slots = [perf_cell, perf_well, perf_index]
    operands = slots + [
        saturation, pressure, permeability, cell_depth, upstream_flags, pore_volume, residual
    ]
    keep, give, given, flags = call(
        opening,
        [
            (well_rows, LANES), (well_rows, LANES), (GRIDS,) + grid,
            jax.ShapeDtypeStruct(grid, upstream_flags.dtype),
        ],
        operands,
        [pltpu.VMEM(a.shape, a.dtype) for a in slots] + [pltpu.SemaphoreType.DMA((INPUTS,))],
        [pltpu.HBM] * INPUTS,
    )
    height = whole_tiles(chunk, 1, count)
    sums, yb, xb, xa, ya = call(
        pair_sums,
        [
            (count * chunk, LANES), (EDGE, rows), (PLANES * layers, lanes), (PLANES * layers, lanes), (EDGE, rows),
        ],
        [keep, to_pair(give, "gy"), well_mode[None], well_target[None], given, flags],
        [
            (2 * EDGE * (rows // LANES), LANES), (height, LANES),
            pltpu.SemaphoreType.DMA((count * chunk // height,)),
        ],
        None,
        [pltpu.HBM] + [pltpu.VMEM] * 4,
    )
    rims = [yb, xb, xa, ya]
    rims = rims + [to_other(yb, "gy"), to_other(xb, "gx"), to_pair(xa, "gx"), to_pair(ya, "gy")]
    gathered = everyone(sums, count)
    (given,) = call(
        main_terms,
        [(GRIDS,) + grid],
        [given, sums, flags] + slots,
        [(rows, lanes)],
        [pltpu.VMEM, pl.ANY] + [pltpu.VMEM] * 4,
        None,
        {0: 0},
    )
    given, bound, flank = call(
        outer_terms,
        [(GRIDS,) + grid, (2, layers, lanes), (EDGE, rows)],
        [given] + rims,
        [(rows, 3 * lanes)],
        aliases={0: 0},
    )
    height = whole_tiles(well_rows, count, count)
    given, sums, yb, xb, xa, ya, known = call(
        first_update,
        [
            (GRIDS,) + grid, (count * well_rows, LANES), (1, rows), (layers, lanes), (layers, lanes), (1, rows),
            (3, well_rows, LANES),
        ],
        [given, gathered] + slots,
        [(height, LANES), pltpu.SemaphoreType.DMA((count * well_rows // height,))],
        None,
        [pltpu.VMEM, pltpu.HBM] + [pltpu.VMEM] * 5,
        {0: 0},
    )
    gathered = everyone(sums, count)
    rims = [to_other(yb, "gy"), to_other(xb, "gx"), to_pair(xa, "gx"), to_pair(ya, "gy")]
    (inner,) = call(inner_terms, [grid], [sums, given], (), [pl.ANY, pltpu.VMEM])
    out, bhp = call(
        last_update,
        [grid, (1, owned)],
        [gathered, known] + slots + [given, inner, bound, flank] + rims,
        [(rows, lanes), (rows, lanes)],
    )
    return out, bhp[0]


def solution(mesh):
    return jax.shard_map(
        body,
        mesh=mesh,
        in_specs=(
            P(None, "gx", "gy"),
            P(None, None, "gx", "gy"),
            P(None, None, "gx", "gy"),
            P(None, "gx", "gy"),
            P(None, "gx", "gy"),
            P(None, None, "gx", "gy"),
            P(None, "gx", "gy"),
            P(("gx", "gy"), None),
            P(("gx", "gy"), None),
            P(("gx", "gy"), None),
            P(("gx", "gy")),
            P(("gx", "gy")),
        ),
        out_specs=(P(None, "gx", "gy"), P(("gx", "gy"))),
        check_vma=False,
    )
```

```python
import jax
import jax.numpy as jnp
from jax import lax
from jax.experimental import pallas as pl
from jax.experimental.pallas import tpu as pltpu
from jax.sharding import PartitionSpec as P

COMP_OIL = 0.2
COMP_WATER = 0.05
GRAV_OIL = 0.4
GRAV_WATER = 0.5
GRAV_GAS = 0.08
RELAXATION = 0.8
LANES = 128
PLANES = 6
INPUTS = 10
PRESS, SAT, PERM, DEPTH, PORE, RES, GRIDS = 0, 1, 3, 6, 7, 8, 11
DIAG, RHS, COUP, MOB, AROUND = 1, 2, 3, 9, 10
CURRENT, SCALE, GAIN = 0, 1, 10
EDGE = 8

F32 = jnp.float32
BF16 = jnp.bfloat16
AXES = ("gx", "gy")


def nn(a, b):
    return lax.dot_general(a, b, (((1,), (0,)), ((), ())), preferred_element_type=F32)


def nt(a, b):
    return lax.dot_general(a, b, (((1,), (1,)), ((), ())), preferred_element_type=F32)


def halves(x):
    high = x.astype(BF16).astype(F32)
    return high, x - high


def iota(shape, dim):
    return lax.broadcasted_iota(jnp.int32, shape, dim)


def hot(index, count):
    return iota((count, index.shape[1]), 0) == index


def ones_of(mask):
    return jnp.where(mask, 1.0, 0.0).astype(BF16)


def bits_of(n):
    assert n & (n - 1) == 0
    return n.bit_length() - 1


def places(index, width):
    return lax.shift_right_arithmetic(index, bits_of(width)), lax.bitwise_and(index, width - 1)


def cell_pick(row, lane, rows, lanes):
    pick = ones_of(hot(lane, lanes))
    return jnp.concatenate([pick, pick], axis=0), hot(row, rows)


def cell_find(fields, pick, at_row):
    rows = at_row.shape[0]
    both = [
        jnp.concatenate([part.astype(BF16) for part in halves(field)], axis=1) for field in fields
    ]
    found = nn(jnp.concatenate(both, axis=0), pick)
    return [
        jnp.sum(jnp.where(at_row, found[i * rows : (i + 1) * rows], 0.0), axis=0, keepdims=True)
        for i in range(len(fields))
    ]


def cell_scatter(value, row, lane, rows, lanes):
    spread = jnp.where(hot(lane, lanes), value, 0.0)
    spread = jnp.concatenate([part.astype(BF16) for part in halves(spread)], axis=0)
    total = nt(ones_of(hot(row, rows)), spread)
    return total[:, :lanes] + total[:, lanes:]


def well_scatter(values, row, lane, rows):
    mine = hot(row, rows)
    stack = []
    for value in values:
        stack.extend(halves(jnp.where(mine, value, 0.0)))
    total = nt(jnp.concatenate(stack, axis=0).astype(BF16), ones_of(hot(lane, LANES)))
    return [
        total[2 * i * rows : (2 * i + 1) * rows] + total[(2 * i + 1) * rows : (2 * i + 2) * rows]
        for i in range(len(values))
    ]


def well_gather(field, row, lane):
    rows = field.shape[0]
    both = jnp.concatenate(halves(field), axis=0).astype(BF16)
    found = nn(both, ones_of(hot(lane, LANES)))
    return jnp.sum(
        jnp.where(hot(row, rows), found[:rows] + found[rows:], 0.0), axis=0, keepdims=True
    )


def total_mobility(sat_water, sat_gas):
    sat_oil = 1.0 - sat_water - sat_gas
    return 0.5 * sat_oil * sat_oil + sat_water * sat_water + 5.0 * (sat_gas * sat_gas)


def phase_mobility(pressure, sat_water, sat_gas):
    sat_oil = 1.0 - sat_water - sat_gas
    b_oil = 1.0 + COMP_OIL * (pressure - 1.0)
    b_water = 1.0 + COMP_WATER * (pressure - 1.0)
    return (
        sat_oil * sat_oil * b_oil * 0.5,
        sat_water * sat_water * b_water,
        sat_gas * sat_gas * pressure * 5.0,
    )


def live_index(well_ref, index_ref):
    return jnp.where(well_ref[...] >= 0, index_ref[...], 0.0)


def fetch(sources, holds, sems):
    copies = [
        pltpu.make_async_copy(source, hold, sems.at[i])
        for i, (source, hold) in enumerate(zip(sources, holds))
    ]
    for copy in copies:
        copy.start()
    return copies


def repeat_out(block_ref, out_ref, sem):
    height = block_ref.shape[0]
    copies = [
        pltpu.make_async_copy(block_ref, out_ref.at[pl.ds(i * height, height)], sem.at[i])
        for i in range(out_ref.shape[0] // height)
    ]
    for copy in copies:
        copy.start()
    return copies


def is_even(axis):
    return lax.rem(lax.axis_index(axis), 2) == 0


def opening(*refs):
    inputs, sems = refs[:INPUTS], refs[-1]
    keep_ref, give_ref, grid_ref, flag_ref = refs[INPUTS : INPUTS + 4]
    cell_ref, well_ref, index_ref = slot_refs = refs[INPUTS + 4 : -1]
    holds = list(slot_refs) + [
        grid_ref.at[SAT : SAT + 2], grid_ref.at[PRESS], grid_ref.at[PERM : PERM + 3], grid_ref.at[DEPTH],
        flag_ref, grid_ref.at[PORE], grid_ref.at[RES : RES + 3],
    ]
    copies = fetch(inputs, holds, sems)
    layers, width, lanes = flag_ref.shape
    rows = layers * width
    well_rows = keep_ref.shape[0]
    for copy in copies[: len(slot_refs)]:
        copy.wait()
    row, lane = places(cell_ref[...], lanes)
    well_row, well_lane = places(well_ref[...], LANES)
    pick, at_row = cell_pick(row, lane, rows, lanes)
    index = live_index(well_ref, index_ref)
    later = copies[len(slot_refs) :]
    later[0].wait()
    mobility = total_mobility(grid_ref[SAT].reshape(rows, lanes), grid_ref[SAT + 1].reshape(rows, lanes))
    later[1].wait()
    press = grid_ref[PRESS].reshape(rows, lanes)
    at_mob, at_press = cell_find([mobility, mobility * press], pick, at_row)
    part, base = well_scatter([index * at_press, index * at_mob], well_row, well_lane, well_rows)
    half = well_rows // 2
    keep_ref[...], give_ref[...] = sides(
        jnp.concatenate([part[:half], base[:half]], axis=0),
        jnp.concatenate([part[half:], base[half:]], axis=0),
        "gy",
    )
    for copy in later[2:]:
        copy.wait()


def sides(a, b, axis):
    even = is_even(axis)
    return jnp.where(even, a, b), jnp.where(even, b, a)


def pair_sums(
    keep_ref, given_ref, mode_ref, target_ref, grid_ref, flag_ref,
    out_ref, yb_ref, xb_ref, xa_ref, ya_ref, lying_ref, block_ref, sems,
):
    owned = mode_ref.shape[1]
    group = LANES // owned
    controls = [mode_ref[...].astype(F32), target_ref[...]]
    if group > 2:
        controls.append(jnp.zeros((1, LANES - 2 * owned), F32))
    controls = jnp.concatenate(controls, axis=1)
    block = jnp.concatenate([keep_ref[...] + given_ref[...], controls], axis=0)
    block_ref[...] = jnp.concatenate([block] * (block_ref.shape[0] // block.shape[0]), axis=0)
    copies = repeat_out(block_ref, out_ref, sems)
    layers, width, lanes = flag_ref.shape
    rows = layers * width
    pair = lax.shift_right_logical(iota((rows, lanes), 1), 1)

    def rim(total, i, plane):
        return jnp.where(pair == i, pltpu.roll(plane.reshape(rows, lanes), 2 * i + 1, 1), total)

    total = rim(jnp.zeros((rows, lanes), F32), 0, grid_ref[PRESS])
    total = rim(rim(total, 1, grid_ref[SAT]), 2, grid_ref[SAT + 1])
    total = rim(total, 3, grid_ref[PERM + 1])
    total = rim(total, 4, grid_ref[DEPTH])
    bit_y = lax.bitwise_and(lax.shift_right_logical(flag_ref[...], 1), 1).astype(F32)
    total = rim(total, PLANES - 1, bit_y)
    pieces = [
        (i * 2 * EDGE, jnp.transpose(total[i * LANES : (i + 1) * LANES])[: 2 * EDGE])
        for i in range(rows // LANES)
    ]
    for first, piece in pieces:
        lying_ref[first : first + 2 * EDGE, :] = piece
    high, low = (
        jnp.concatenate([lying_ref[pl.ds(first + k, EDGE, stride=2), :] for first, _ in pieces], axis=1)
        for k in range(2)
    )
    x_even, y_even = is_even("gx"), is_even("gy")
    ya_ref[...] = jnp.where(y_even, high, low)
    yb_ref[...] = jnp.where(y_even, low, high)
    last = width - 1
    ends = [
        [
            grid_ref[PRESS, :, edge, :],
            grid_ref[SAT, :, edge, :],
            grid_ref[SAT + 1, :, edge, :],
            grid_ref[PERM, :, edge, :],
            grid_ref[DEPTH, :, edge, :],
            lax.bitwise_and(flag_ref[:, edge, :], 1).astype(F32),
        ]
        for edge in (last, 0)
    ]
    for i, (high, low) in enumerate(zip(*ends)):
        xa_ref[i * layers : (i + 1) * layers, :] = jnp.where(x_even, high, low)
        xb_ref[i * layers : (i + 1) * layers, :] = jnp.where(x_even, low, high)
    for copy in copies:
        copy.wait()


def upright(rows_list, lanes):
    stack = jnp.concatenate(rows_list, axis=0)
    stack = jnp.concatenate([stack, jnp.zeros((lanes - stack.shape[0], stack.shape[1]), F32)], axis=0)
    return jnp.transpose(stack)


def inverse(x):
    guess = pl.reciprocal(x, approx=True)
    return guess * (2.0 - x * guess)


def phase_weights(pressure):
    b_oil = 1.0 + COMP_OIL * (pressure - 1.0)
    b_water = 1.0 + COMP_WATER * (pressure - 1.0)
    whole = inverse(b_oil * b_water * pressure)
    other = pressure * whole
    return b_water * other, b_oil * other, b_oil * b_water * whole


def faces(perm, perm_next, mob, mob_next, first_up):
    transmit = 2.0 * perm * perm_next * inverse(perm + perm_next)
    return [transmit * jnp.where(first_up, a, b) for a, b in zip(mob, mob_next)]


def weighted(weights, flux):
    oil, water, gas = (w * f for w, f in zip(weights, flux))
    return oil + water + gas, GRAV_OIL * oil + GRAV_WATER * water + GRAV_GAS * gas


def outer_face(own, other, own_up):
    mob, mob_other = phase_mobility(*own[:3]), phase_mobility(*other[:3])
    coupling, lift = weighted(phase_weights(own[0]), faces(own[3], other[3], mob, mob_other, own_up))
    return coupling, lift * (own[4] - other[4]), coupling * other[0]


def main_terms(given_ref, after_ref, flag_ref, cell_ref, well_ref, index_ref, grid_ref, share_ref):
    layers, width, lanes = flag_ref.shape
    rows = layers * width
    row, lane = places(cell_ref[...], lanes)
    share_ref[...] = cell_scatter(live_index(well_ref, index_ref), row, lane, rows, lanes)
    x_last = iota((width, lanes), 0) == width - 1
    y_last = iota((width, lanes), 1) == lanes - 1

    def layer(z):
        press = grid_ref[PRESS, z]
        return press, phase_mobility(press, grid_ref[SAT, z], grid_ref[SAT + 1, z])

    this = layer(0)
    before = None
    for z in range(layers):
        press, mob = this
        following = layer(z + 1) if z + 1 < layers else None
        sat_water, sat_gas = grid_ref[SAT, z], grid_ref[SAT + 1, z]
        sat_oil = 1.0 - sat_water - sat_gas
        depth = grid_ref[DEPTH, z]
        flags = flag_ref[z]
        weights = phase_weights(press)
        storage = grid_ref[PORE, z] * (
            sat_oil * COMP_OIL * weights[0] + sat_water * COMP_WATER * weights[1] + sat_gas * weights[2]
        )
        mobility = total_mobility(sat_water, sat_gas)
        diag = storage + mobility * share_ref[z * width : (z + 1) * width, :]
        rhs = storage * press
        for i, weight in enumerate(weights):
            rhs = rhs - weight * grid_ref[RES + i, z]
        around = jnp.zeros_like(press)
        couplings = {}

        def add(name, flux, drop, beside):
            nonlocal diag, rhs, around
            coupling, lift = weighted(weights, flux)
            couplings[name] = coupling
            diag = diag + coupling
            rhs = rhs + lift * drop
            around = around + coupling * beside

        for dim, size, end, bit in ((0, width, x_last, 1), (1, lanes, y_last, 2)):
            perm = grid_ref[PERM + dim, z]
            perm_next = jnp.where(end, 0.0, pltpu.roll(perm, size - 1, dim))
            up = lax.bitwise_and(flags, bit) > 0
            flux = faces(perm, perm_next, mob, [pltpu.roll(a, size - 1, dim) for a in mob], up)
            drop = depth - pltpu.roll(depth, size - 1, dim)
            add(2 * dim, flux, drop, pltpu.roll(press, size - 1, dim))
            add(2 * dim + 1, [pltpu.roll(a, 1, dim) for a in flux], -pltpu.roll(drop, 1, dim), pltpu.roll(press, 1, dim))
        if following is not None:
            up = lax.bitwise_and(flags, 4) > 0
            flux = faces(grid_ref[PERM + 2, z], grid_ref[PERM + 2, z + 1], mob, following[1], up)
            drop = depth - grid_ref[DEPTH, z + 1]
            add(4, flux, drop, following[0])
        if before is not None:
            add(5, before[0], -before[1], before[2])
        if following is not None:
            before = (flux, drop, press)
        for name, coupling in couplings.items():
            grid_ref[COUP + name, z] = coupling
        grid_ref[DIAG, z] = diag
        grid_ref[RHS, z] = rhs
        grid_ref[AROUND, z] = around
        grid_ref[MOB, z] = mobility
        this = following


def slot_bhp(bhp, well_ref, index_ref):
    well_row, well_lane = places(well_ref[...], LANES)
    return live_index(well_ref, index_ref) * well_gather(bhp, well_row, well_lane)


def close_ends(nxt, prev, axis):
    me = lax.axis_index(axis)
    nxt[3] = jnp.where(me < lax.axis_size(axis) - 1, nxt[3], 0.0)
    prev[3] = jnp.where(me > 0, prev[3], 0.0)


def outer_terms(
    given_ref, own_yb_ref, own_xb_ref, own_xa_ref, own_ya_ref, yb_ref, xb_ref, xa_ref, ya_ref,
    grid_ref, bound_ref, flank_ref, side_ref,
):
    layers, width, lanes = grid_ref.shape[1:]
    rows = layers * width
    (high, low), (nxt, prev) = (
        sides(own_xa_ref[...], own_xb_ref[...], "gx"), sides(xa_ref[...], xb_ref[...], "gx")
    )
    high, low, nxt, prev = (
        [rim[i * layers : (i + 1) * layers] for i in range(PLANES)] for rim in (high, low, nxt, prev)
    )
    close_ends(nxt, prev, "gx")
    for where, edge, terms in (
        (0, width - 1, outer_face(high, nxt, high[5] > 0.5)),
        (1, 0, outer_face(low, prev, prev[5] < 0.5)),
    ):
        bound_ref[where] = terms[0]
        for name, term in zip((DIAG, RHS, AROUND), terms):
            grid_ref[name, :, edge, :] = grid_ref[name, :, edge, :] + term
    (high, low), (nxt, prev) = (
        sides(own_ya_ref[...], own_yb_ref[...], "gy"), sides(ya_ref[...], yb_ref[...], "gy")
    )
    high, low, nxt, prev = ([rim[i : i + 1] for i in range(PLANES)] for rim in (high, low, nxt, prev))
    close_ends(nxt, prev, "gy")
    after = outer_face(high, nxt, high[5] > 0.5)
    behind = outer_face(low, prev, prev[5] < 0.5)
    flank_ref[0:1, :] = after[0]
    flank_ref[1:2, :] = behind[0]
    stand = upright(list(behind + after), lanes)
    stand = jnp.concatenate([part.astype(BF16) for part in halves(stand)], axis=1)
    wide = (2 * lanes, 3 * lanes)
    from_lane = lax.rem(iota(wide, 0), lanes)
    to_plane, to_lane = places(iota(wide, 1), lanes)
    side_ref[...] = nn(
        stand,
        ones_of(
            ((from_lane == to_plane) & (to_lane == 0)) | ((from_lane == to_plane + 3) & (to_lane == lanes - 1))
        ),
    )
    for z in range(layers):
        here = slice(z * width, (z + 1) * width)
        diag, rhs, around = (
            grid_ref[name, z] + side_ref[here, i * lanes : (i + 1) * lanes]
            for i, name in enumerate((DIAG, RHS, AROUND))
        )
        scale = RELAXATION * inverse(diag)
        rhs = scale * rhs
        grid_ref[CURRENT, z] = (1.0 - RELAXATION) * grid_ref[PRESS, z] + rhs + scale * around
        grid_ref[SCALE, z] = scale
        grid_ref[RHS, z] = rhs
        grid_ref[GAIN, z] = scale * grid_ref[MOB, z]


def first_update(
    given_ref, sums_ref, cell_ref, well_ref, index_ref,
    grid_ref, out_ref, yb_ref, xb_ref, xa_ref, ya_ref, known_ref, line_ref, block_ref, sems,
):
    layers, width, lanes = grid_ref.shape[1:]
    rows = layers * width
    count = lax.axis_size("gx") * lax.axis_size("gy")
    chunk = sums_ref.shape[0] // count
    well_rows = chunk - 1
    half = well_rows // 2
    group = count // well_rows
    across = lax.axis_size("gx")
    low = high = jnp.zeros((well_rows, LANES), F32)
    for d in range(count):
        sums = sums_ref[d * chunk : d * chunk + well_rows, :]
        if d // across % 2:
            high = high + sums
        else:
            low = low + sums
    part = jnp.concatenate([low[:half], high[:half]], axis=0)
    base = jnp.concatenate([low[half:], high[half:]], axis=0)
    owned = LANES // group
    place = lax.shift_right_logical(iota((well_rows, LANES), 1), bits_of(owned))
    mode = target = jnp.zeros((well_rows, LANES), F32)
    for j in range(group):
        for r in range(well_rows // across):
            first = (r * group + j) * across * chunk + well_rows
            line_ref[pl.ds(r, across, stride=well_rows // across), :] = sums_ref[
                pl.ds(first, across, stride=chunk), :
            ]
        line = line_ref[...]
        mode = jnp.where(place == j, pltpu.roll(line, j * owned, 1) if j else line, mode)
        shift = (j - 1) % group * owned
        target = jnp.where(place == j, pltpu.roll(line, shift, 1) if shift else line, target)
    bhp = jnp.where(mode < 0.5, target, (part - target) / base)
    known_ref[0] = mode
    known_ref[1] = target
    known_ref[2] = base
    row, lane = places(cell_ref[...], lanes)
    well_row, well_lane = places(well_ref[...], LANES)
    push = cell_scatter(slot_bhp(bhp, well_ref, index_ref), row, lane, rows, lanes)
    current = grid_ref[CURRENT].reshape(rows, lanes) + grid_ref[GAIN].reshape(rows, lanes) * push
    grid_ref[CURRENT] = current.reshape(layers, width, lanes)
    xa_ref[...], xb_ref[...] = sides(
        grid_ref[CURRENT, :, width - 1, :], grid_ref[CURRENT, :, 0, :], "gx"
    )
    mobile = grid_ref[MOB].reshape(rows, lanes) * current
    (at_cell,) = cell_find([mobile], *cell_pick(row, lane, rows, lanes))
    (part,) = well_scatter([live_index(well_ref, index_ref) * at_cell], well_row, well_lane, well_rows)
    block_ref[...] = jnp.concatenate([part] * (block_ref.shape[0] // well_rows), axis=0)
    outgoing = repeat_out(block_ref, out_ref, sems)
    both = jnp.concatenate([half.astype(BF16) for half in halves(current)], axis=1)
    pick_row, pick_lane = iota((2 * EDGE, 2 * lanes), 0), lax.rem(iota((2 * EDGE, 2 * lanes), 1), lanes)
    rims = nt(
        ones_of(((pick_row == 0) & (pick_lane == lanes - 1)) | ((pick_row == 1) & (pick_lane == 0))), both
    )
    ya_ref[...], yb_ref[...] = sides(rims[0:1], rims[1:2], "gy")
    for copy in outgoing:
        copy.wait()


def inner_terms(after_ref, grid_ref, out_ref):
    layers, width, lanes = out_ref.shape
    for z in range(layers):
        current = grid_ref[CURRENT, z]
        besides = [
            pltpu.roll(current, width - 1, 0),
            pltpu.roll(current, 1, 0),
            pltpu.roll(current, lanes - 1, 1),
            pltpu.roll(current, 1, 1),
        ]
        around = grid_ref[COUP, z] * besides[0]
        for i in range(1, 4):
            around = around + grid_ref[COUP + i, z] * besides[i]
        if z + 1 < layers:
            around = around + grid_ref[COUP + 4, z] * grid_ref[CURRENT, z + 1]
        if z > 0:
            around = around + grid_ref[COUP + 5, z] * grid_ref[CURRENT, z - 1]
        out_ref[z] = (1.0 - RELAXATION) * current + grid_ref[RHS, z] + grid_ref[SCALE, z] * around


def last_update(
    sums_ref, known_ref, cell_ref, well_ref, index_ref, grid_ref, inner_ref, bound_ref, flank_ref,
    yb_ref, xb_ref, xa_ref, ya_ref, out_ref, bhp_ref, push_ref, side_ref,
):
    layers, width, lanes = out_ref.shape
    rows = layers * width
    count = lax.axis_size("gx") * lax.axis_size("gy")
    height = sums_ref.shape[0] // count
    well_rows = known_ref.shape[1]
    me = lax.axis_index(AXES)
    part = sums_ref[0:well_rows, :]
    for d in range(1, count):
        part = part + sums_ref[d * height : d * height + well_rows, :]
    bhp = jnp.where(known_ref[0] < 0.5, known_ref[1], (part - known_ref[1]) / known_ref[2])
    owned = bhp_ref.shape[1]
    group = LANES // owned
    line = jnp.sum(
        jnp.where(iota(bhp.shape, 0) == me // group, bhp, 0.0), axis=0, keepdims=True
    )
    line = pltpu.roll(line, lax.rem(LANES - lax.rem(me, group) * owned, LANES), 1)
    bhp_ref[...] = line[:, :owned]
    row, lane = places(cell_ref[...], lanes)
    push_ref[...] = cell_scatter(slot_bhp(bhp, well_ref, index_ref), row, lane, rows, lanes)
    nxt, prev = sides(ya_ref[...], yb_ref[...], "gy")
    side_ref[...] = upright([flank_ref[1:2, :] * prev, flank_ref[0:1, :] * nxt], lanes)
    along = iota((width, lanes), 1)
    nxt, prev = sides(xa_ref[...], xb_ref[...], "gx")
    for z in range(layers):
        here = slice(z * width, (z + 1) * width)
        side = side_ref[here, :]
        side = jnp.where(along == 0, side, jnp.where(along == lanes - 1, pltpu.roll(side, lanes - 2, 1), 0.0))
        out_ref[z] = inner_ref[z] + grid_ref[GAIN, z] * push_ref[here, :] + grid_ref[SCALE, z] * side
    for where, edge, beyond in ((0, width - 1, nxt), (1, 0, prev)):
        out_ref[:, edge, :] = out_ref[:, edge, :] + grid_ref[SCALE, :, edge, :] * (bound_ref[where] * beyond)


def call(kernel, outs, args, scratch=(), spaces=None, out_spaces=None, aliases=None):
    shapes = [jax.ShapeDtypeStruct(item, F32) if isinstance(item, tuple) else item for item in outs]
    spaces = spaces or [pltpu.VMEM] * len(args)
    out_spaces = out_spaces or [pltpu.VMEM] * len(outs)
    args = [
        pltpu.with_memory_space_constraint(arg, space) if space is pltpu.HBM else arg
        for arg, space in zip(args, spaces)
    ]
    return pl.pallas_call(
        kernel,
        out_shape=shapes,
        in_specs=[pl.BlockSpec(memory_space=space) for space in spaces],
        out_specs=[pl.BlockSpec(memory_space=space) for space in out_spaces],
        scratch_shapes=[pltpu.VMEM(item, F32) if isinstance(item, tuple) else item for item in scratch],
        input_output_aliases=aliases or {},
        compiler_params=pltpu.CompilerParams(vmem_limit_bytes=24 * 1024 * 1024),
        cost_estimate=pl.CostEstimate(flops=1_000_000, bytes_accessed=4_000_000, transcendentals=0),
    )(*args)


def whole_tiles(height, step, count):
    chunks = step
    while chunks * height % 8:
        chunks += step
    assert count % chunks == 0
    return chunks * height


def everyone(rows, count):
    height = rows.shape[0] // count
    swapped = lax.all_to_all(rows.reshape(count, height, 1, LANES), AXES[::-1], 0, 0, tiled=True)
    return swapped.reshape(rows.shape)


def to_pair(block, axis):
    count = lax.axis_size(axis)
    assert count % 2 == 0
    return lax.ppermute(block, axis, [(i, i ^ 1) for i in range(count)])


def to_other(block, axis):
    sizes = {name: lax.axis_size(name) for name in AXES}
    moves = []
    for gx in range(sizes["gx"]):
        for gy in range(sizes["gy"]):
            there = {"gx": gx, "gy": gy}
            away = there[axis] + (1 if there[axis] % 2 else -1)
            if 0 <= away < sizes[axis]:
                there[axis] = away
            else:
                cross = "gy" if axis == "gx" else "gx"
                there[cross] ^= 1
            moves.append((gx * sizes["gy"] + gy, there["gx"] * sizes["gy"] + there["gy"]))
    return lax.ppermute(block, AXES, moves)


def body(
    pressure, saturation, permeability, pore_volume, cell_depth, residual, upstream_flags,
    perf_cell, perf_well, perf_index, well_mode, well_target,
):
    layers, width, lanes = pressure.shape
    rows = layers * width
    count = lax.axis_size("gx") * lax.axis_size("gy")
    owned = well_mode.shape[0]
    well_rows = owned * count // LANES
    chunk = well_rows + 1
    grid = (layers, width, lanes)
    slots = [perf_cell, perf_well, perf_index]
    operands = slots + [
        saturation, pressure, permeability, cell_depth, upstream_flags, pore_volume, residual
    ]
    keep, give, given, flags = call(
        opening,
        [
            (well_rows, LANES), (well_rows, LANES), (GRIDS,) + grid,
            jax.ShapeDtypeStruct(grid, upstream_flags.dtype),
        ],
        operands,
        [pltpu.VMEM(a.shape, a.dtype) for a in slots] + [pltpu.SemaphoreType.DMA((INPUTS,))],
        [pltpu.HBM] * INPUTS,
    )
    height = whole_tiles(chunk, 1, count)
    sums, yb, xb, xa, ya = call(
        pair_sums,
        [
            (count * chunk, LANES), (EDGE, rows), (PLANES * layers, lanes), (PLANES * layers, lanes), (EDGE, rows),
        ],
        [keep, to_pair(give, "gy"), well_mode[None], well_target[None], given, flags],
        [
            (2 * EDGE * (rows // LANES), LANES), (height, LANES),
            pltpu.SemaphoreType.DMA((count * chunk // height,)),
        ],
        None,
        [pltpu.HBM] + [pltpu.VMEM] * 4,
    )
    rims = [yb, xb, xa, ya]
    rims = rims + [to_other(yb, "gy"), to_other(xb, "gx"), to_pair(xa, "gx"), to_pair(ya, "gy")]
    gathered = everyone(sums, count)
    (given,) = call(
        main_terms,
        [(GRIDS,) + grid],
        [given, sums, flags] + slots,
        [(rows, lanes)],
        [pltpu.VMEM, pl.ANY] + [pltpu.VMEM] * 4,
        None,
        {0: 0},
    )
    given, bound, flank = call(
        outer_terms,
        [(GRIDS,) + grid, (2, layers, lanes), (EDGE, rows)],
        [given] + rims,
        [(rows, 3 * lanes)],
        aliases={0: 0},
    )
    height = whole_tiles(well_rows, count, count)
    given, sums, yb, xb, xa, ya, known = call(
        first_update,
        [
            (GRIDS,) + grid, (count * well_rows, LANES), (1, rows), (layers, lanes), (layers, lanes), (1, rows),
            (3, well_rows, LANES),
        ],
        [given, gathered] + slots,
        [(well_rows, LANES), (height, LANES), pltpu.SemaphoreType.DMA((count * well_rows // height,))],
        None,
        [pltpu.VMEM, pltpu.HBM] + [pltpu.VMEM] * 5,
        {0: 0},
    )
    gathered = everyone(sums, count)
    rims = [to_other(yb, "gy"), to_other(xb, "gx"), to_pair(xa, "gx"), to_pair(ya, "gy")]
    (inner,) = call(inner_terms, [grid], [sums, given], (), [pl.ANY, pltpu.VMEM])
    out, bhp = call(
        last_update,
        [grid, (1, owned)],
        [gathered, known] + slots + [given, inner, bound, flank] + rims,
        [(rows, lanes), (rows, lanes)],
    )
    return out, bhp[0]


def solution(mesh):
    return jax.shard_map(
        body,
        mesh=mesh,
        in_specs=(
            P(None, "gx", "gy"),
            P(None, None, "gx", "gy"),
            P(None, None, "gx", "gy"),
            P(None, "gx", "gy"),
            P(None, "gx", "gy"),
            P(None, None, "gx", "gy"),
            P(None, "gx", "gy"),
            P(("gx", "gy"), None),
            P(("gx", "gy"), None),
            P(("gx", "gy"), None),
            P(("gx", "gy")),
            P(("gx", "gy")),
        ),
        out_specs=(P(None, "gx", "gy"), P(("gx", "gy"))),
        check_vma=False,
    )
```

```python
import jax
import jax.numpy as jnp
from jax import lax
from jax.experimental import pallas as pl
from jax.experimental.pallas import tpu as pltpu
from jax.sharding import PartitionSpec as P

COMP_OIL = 0.2
COMP_WATER = 0.05
GRAV_OIL = 0.4
GRAV_WATER = 0.5
GRAV_GAS = 0.08
RELAXATION = 0.8
LANES = 128
PLANES = 6
INPUTS = 10
PRESS, SAT, PERM, DEPTH, PORE, RES, GRIDS = 0, 1, 3, 6, 7, 8, 11
DIAG, RHS, COUP, MOB, AROUND = 1, 2, 3, 9, 10
CURRENT, SCALE, GAIN = 0, 1, 10
EDGE = 8

F32 = jnp.float32
BF16 = jnp.bfloat16
AXES = ("gx", "gy")


def nn(a, b):
    return lax.dot_general(a, b, (((1,), (0,)), ((), ())), preferred_element_type=F32)


def nt(a, b):
    return lax.dot_general(a, b, (((1,), (1,)), ((), ())), preferred_element_type=F32)


def halves(x):
    high = x.astype(BF16).astype(F32)
    return high, x - high


def iota(shape, dim):
    return lax.broadcasted_iota(jnp.int32, shape, dim)


def hot(index, count):
    return iota((count, index.shape[1]), 0) == index


def ones_of(mask):
    return jnp.where(mask, 1.0, 0.0).astype(BF16)


def bits_of(n):
    assert n & (n - 1) == 0
    return n.bit_length() - 1


def places(index, width):
    return lax.shift_right_arithmetic(index, bits_of(width)), lax.bitwise_and(index, width - 1)


def cell_pick(row, lane, rows, lanes):
    pick = ones_of(hot(lane, lanes))
    return jnp.concatenate([pick, pick], axis=0), hot(row, rows)


def cell_find(fields, pick, at_row):
    rows = at_row.shape[0]
    both = [
        jnp.concatenate([part.astype(BF16) for part in halves(field)], axis=1) for field in fields
    ]
    found = nn(jnp.concatenate(both, axis=0), pick)
    return [
        jnp.sum(jnp.where(at_row, found[i * rows : (i + 1) * rows], 0.0), axis=0, keepdims=True)
        for i in range(len(fields))
    ]


def cell_scatter(value, row, lane, rows, lanes):
    spread = jnp.where(hot(lane, lanes), value, 0.0)
    spread = jnp.concatenate([part.astype(BF16) for part in halves(spread)], axis=0)
    total = nt(ones_of(hot(row, rows)), spread)
    return total[:, :lanes] + total[:, lanes:]


def well_scatter(values, row, lane, rows):
    mine = hot(row, rows)
    stack = []
    for value in values:
        stack.extend(halves(jnp.where(mine, value, 0.0)))
    total = nt(jnp.concatenate(stack, axis=0).astype(BF16), ones_of(hot(lane, LANES)))
    return [
        total[2 * i * rows : (2 * i + 1) * rows] + total[(2 * i + 1) * rows : (2 * i + 2) * rows]
        for i in range(len(values))
    ]


def well_gather(field, row, lane):
    rows = field.shape[0]
    both = jnp.concatenate(halves(field), axis=0).astype(BF16)
    found = nn(both, ones_of(hot(lane, LANES)))
    return jnp.sum(
        jnp.where(hot(row, rows), found[:rows] + found[rows:], 0.0), axis=0, keepdims=True
    )


def total_mobility(sat_water, sat_gas):
    sat_oil = 1.0 - sat_water - sat_gas
    return 0.5 * sat_oil * sat_oil + sat_water * sat_water + 5.0 * (sat_gas * sat_gas)


def phase_mobility(pressure, sat_water, sat_gas):
    sat_oil = 1.0 - sat_water - sat_gas
    b_oil = 1.0 + COMP_OIL * (pressure - 1.0)
    b_water = 1.0 + COMP_WATER * (pressure - 1.0)
    return (
        sat_oil * sat_oil * b_oil * 0.5,
        sat_water * sat_water * b_water,
        sat_gas * sat_gas * pressure * 5.0,
    )


def live_index(well_ref, index_ref):
    return jnp.where(well_ref[...] >= 0, index_ref[...], 0.0)


def fetch(sources, holds, sems):
    copies = [
        pltpu.make_async_copy(source, hold, sems.at[i])
        for i, (source, hold) in enumerate(zip(sources, holds))
    ]
    for copy in copies:
        copy.start()
    return copies


def repeat_out(block_ref, out_ref, sem):
    height = block_ref.shape[0]
    copies = [
        pltpu.make_async_copy(block_ref, out_ref.at[pl.ds(i * height, height)], sem.at[i])
        for i in range(out_ref.shape[0] // height)
    ]
    for copy in copies:
        copy.start()
    return copies


def is_even(axis):
    return lax.rem(lax.axis_index(axis), 2) == 0


def opening(*refs):
    inputs, sems = refs[:INPUTS], refs[-1]
    keep_ref, give_ref, grid_ref, flag_ref = refs[INPUTS : INPUTS + 4]
    cell_ref, well_ref, index_ref = slot_refs = refs[INPUTS + 4 : -1]
    holds = list(slot_refs) + [
        grid_ref.at[SAT : SAT + 2], grid_ref.at[PRESS], grid_ref.at[PERM : PERM + 3], grid_ref.at[DEPTH],
        flag_ref, grid_ref.at[PORE], grid_ref.at[RES : RES + 3],
    ]
    copies = fetch(inputs, holds, sems)
    layers, width, lanes = flag_ref.shape
    rows = layers * width
    well_rows = keep_ref.shape[0]
    for copy in copies[: len(slot_refs)]:
        copy.wait()
    row, lane = places(cell_ref[...], lanes)
    well_row, well_lane = places(well_ref[...], LANES)
    pick, at_row = cell_pick(row, lane, rows, lanes)
    index = live_index(well_ref, index_ref)
    later = copies[len(slot_refs) :]
    later[0].wait()
    mobility = total_mobility(grid_ref[SAT].reshape(rows, lanes), grid_ref[SAT + 1].reshape(rows, lanes))
    later[1].wait()
    press = grid_ref[PRESS].reshape(rows, lanes)
    at_mob, at_press = cell_find([mobility, mobility * press], pick, at_row)
    part, base = well_scatter([index * at_press, index * at_mob], well_row, well_lane, well_rows)
    half = well_rows // 2
    keep_ref[...], give_ref[...] = sides(
        jnp.concatenate([part[:half], base[:half]], axis=0),
        jnp.concatenate([part[half:], base[half:]], axis=0),
        "gy",
    )
    for copy in later[2:]:
        copy.wait()


def sides(a, b, axis):
    even = is_even(axis)
    return jnp.where(even, a, b), jnp.where(even, b, a)


def pair_sums(
    keep_ref, given_ref, mode_ref, target_ref, grid_ref, flag_ref,
    out_ref, yb_ref, xb_ref, xa_ref, ya_ref, lying_ref, block_ref, sems,
):
    owned = mode_ref.shape[1]
    group = LANES // owned
    controls = [mode_ref[...].astype(F32), target_ref[...]]
    if group > 2:
        controls.append(jnp.zeros((1, LANES - 2 * owned), F32))
    controls = jnp.concatenate(controls, axis=1)
    block = jnp.concatenate([keep_ref[...] + given_ref[...], controls], axis=0)
    block_ref[...] = jnp.concatenate([block] * (block_ref.shape[0] // block.shape[0]), axis=0)
    copies = repeat_out(block_ref, out_ref, sems)
    layers, width, lanes = flag_ref.shape
    rows = layers * width
    pair = lax.shift_right_logical(iota((rows, lanes), 1), 1)

    def rim(total, i, plane):
        return jnp.where(pair == i, pltpu.roll(plane.reshape(rows, lanes), 2 * i + 1, 1), total)

    total = rim(jnp.zeros((rows, lanes), F32), 0, grid_ref[PRESS])
    total = rim(rim(total, 1, grid_ref[SAT]), 2, grid_ref[SAT + 1])
    total = rim(total, 3, grid_ref[PERM + 1])
    total = rim(total, 4, grid_ref[DEPTH])
    bit_y = lax.bitwise_and(lax.shift_right_logical(flag_ref[...], 1), 1).astype(F32)
    total = rim(total, PLANES - 1, bit_y)
    pieces = [
        (i * 2 * EDGE, jnp.transpose(total[i * LANES : (i + 1) * LANES])[: 2 * EDGE])
        for i in range(rows // LANES)
    ]
    for first, piece in pieces:
        lying_ref[first : first + 2 * EDGE, :] = piece
    high, low = (
        jnp.concatenate([lying_ref[pl.ds(first + k, EDGE, stride=2), :] for first, _ in pieces], axis=1)
        for k in range(2)
    )
    x_even, y_even = is_even("gx"), is_even("gy")
    ya_ref[...] = jnp.where(y_even, high, low)
    yb_ref[...] = jnp.where(y_even, low, high)
    last = width - 1
    ends = [
        [
            grid_ref[PRESS, :, edge, :],
            grid_ref[SAT, :, edge, :],
            grid_ref[SAT + 1, :, edge, :],
            grid_ref[PERM, :, edge, :],
            grid_ref[DEPTH, :, edge, :],
            lax.bitwise_and(flag_ref[:, edge, :], 1).astype(F32),
        ]
        for edge in (last, 0)
    ]
    for i, (high, low) in enumerate(zip(*ends)):
        xa_ref[i * layers : (i + 1) * layers, :] = jnp.where(x_even, high, low)
        xb_ref[i * layers : (i + 1) * layers, :] = jnp.where(x_even, low, high)
    for copy in copies:
        copy.wait()


def upright(rows_list, lanes):
    stack = jnp.concatenate(rows_list, axis=0)
    stack = jnp.concatenate([stack, jnp.zeros((lanes - stack.shape[0], stack.shape[1]), F32)], axis=0)
    return jnp.transpose(stack)


def inverse(x):
    guess = pl.reciprocal(x, approx=True)
    return guess * (2.0 - x * guess)


def phase_weights(pressure):
    b_oil = 1.0 + COMP_OIL * (pressure - 1.0)
    b_water = 1.0 + COMP_WATER * (pressure - 1.0)
    whole = inverse(b_oil * b_water * pressure)
    other = pressure * whole
    return b_water * other, b_oil * other, b_oil * b_water * whole


def faces(perm, perm_next, mob, mob_next, first_up):
    transmit = 2.0 * perm * perm_next * inverse(perm + perm_next)
    return [transmit * jnp.where(first_up, a, b) for a, b in zip(mob, mob_next)]


def weighted(weights, flux):
    oil, water, gas = (w * f for w, f in zip(weights, flux))
    return oil + water + gas, GRAV_OIL * oil + GRAV_WATER * water + GRAV_GAS * gas


def outer_face(own, other, own_up):
    mob, mob_other = phase_mobility(*own[:3]), phase_mobility(*other[:3])
    coupling, lift = weighted(phase_weights(own[0]), faces(own[3], other[3], mob, mob_other, own_up))
    return coupling, lift * (own[4] - other[4]), coupling * other[0]


def main_terms(given_ref, after_ref, flag_ref, cell_ref, well_ref, index_ref, grid_ref, share_ref):
    layers, width, lanes = flag_ref.shape
    rows = layers * width
    row, lane = places(cell_ref[...], lanes)
    share_ref[...] = cell_scatter(live_index(well_ref, index_ref), row, lane, rows, lanes)
    x_last = iota((width, lanes), 0) == width - 1
    y_last = iota((width, lanes), 1) == lanes - 1

    def layer(z):
        press = grid_ref[PRESS, z]
        return press, phase_mobility(press, grid_ref[SAT, z], grid_ref[SAT + 1, z])

    this = layer(0)
    before = None
    for z in range(layers):
        press, mob = this
        following = layer(z + 1) if z + 1 < layers else None
        sat_water, sat_gas = grid_ref[SAT, z], grid_ref[SAT + 1, z]
        sat_oil = 1.0 - sat_water - sat_gas
        depth = grid_ref[DEPTH, z]
        flags = flag_ref[z]
        weights = phase_weights(press)
        storage = grid_ref[PORE, z] * (
            sat_oil * COMP_OIL * weights[0] + sat_water * COMP_WATER * weights[1] + sat_gas * weights[2]
        )
        mobility = total_mobility(sat_water, sat_gas)
        diag = storage + mobility * share_ref[z * width : (z + 1) * width, :]
        rhs = storage * press
        for i, weight in enumerate(weights):
            rhs = rhs - weight * grid_ref[RES + i, z]
        around = jnp.zeros_like(press)
        couplings = {}

        def add(name, flux, drop, beside):
            nonlocal diag, rhs, around
            coupling, lift = weighted(weights, flux)
            couplings[name] = coupling
            diag = diag + coupling
            rhs = rhs + lift * drop
            around = around + coupling * beside

        for dim, size, end, bit in ((0, width, x_last, 1), (1, lanes, y_last, 2)):
            perm = grid_ref[PERM + dim, z]
            perm_next = jnp.where(end, 0.0, pltpu.roll(perm, size - 1, dim))
            up = lax.bitwise_and(flags, bit) > 0
            flux = faces(perm, perm_next, mob, [pltpu.roll(a, size - 1, dim) for a in mob], up)
            drop = depth - pltpu.roll(depth, size - 1, dim)
            add(2 * dim, flux, drop, pltpu.roll(press, size - 1, dim))
            add(2 * dim + 1, [pltpu.roll(a, 1, dim) for a in flux], -pltpu.roll(drop, 1, dim), pltpu.roll(press, 1, dim))
        if following is not None:
            up = lax.bitwise_and(flags, 4) > 0
            flux = faces(grid_ref[PERM + 2, z], grid_ref[PERM + 2, z + 1], mob, following[1], up)
            drop = depth - grid_ref[DEPTH, z + 1]
            add(4, flux, drop, following[0])
        if before is not None:
            add(5, before[0], -before[1], before[2])
        if following is not None:
            before = (flux, drop, press)
        for name, coupling in couplings.items():
            grid_ref[COUP + name, z] = coupling
        grid_ref[DIAG, z] = diag
        grid_ref[RHS, z] = rhs
        grid_ref[AROUND, z] = around
        grid_ref[MOB, z] = mobility
        this = following


def slot_bhp(bhp, well_ref, index_ref):
    well_row, well_lane = places(well_ref[...], LANES)
    return live_index(well_ref, index_ref) * well_gather(bhp, well_row, well_lane)


def close_ends(nxt, prev, axis):
    me = lax.axis_index(axis)
    nxt[3] = jnp.where(me < lax.axis_size(axis) - 1, nxt[3], 0.0)
    prev[3] = jnp.where(me > 0, prev[3], 0.0)


def outer_terms(
    given_ref, own_yb_ref, own_xb_ref, own_xa_ref, own_ya_ref, yb_ref, xb_ref, xa_ref, ya_ref,
    grid_ref, bound_ref, flank_ref, side_ref,
):
    layers, width, lanes = grid_ref.shape[1:]
    rows = layers * width
    (high, low), (nxt, prev) = (
        sides(own_xa_ref[...], own_xb_ref[...], "gx"), sides(xa_ref[...], xb_ref[...], "gx")
    )
    high, low, nxt, prev = (
        [rim[i * layers : (i + 1) * layers] for i in range(PLANES)] for rim in (high, low, nxt, prev)
    )
    close_ends(nxt, prev, "gx")
    for where, edge, terms in (
        (0, width - 1, outer_face(high, nxt, high[5] > 0.5)),
        (1, 0, outer_face(low, prev, prev[5] < 0.5)),
    ):
        bound_ref[where] = terms[0]
        for name, term in zip((DIAG, RHS, AROUND), terms):
            grid_ref[name, :, edge, :] = grid_ref[name, :, edge, :] + term
    (high, low), (nxt, prev) = (
        sides(own_ya_ref[...], own_yb_ref[...], "gy"), sides(ya_ref[...], yb_ref[...], "gy")
    )
    high, low, nxt, prev = ([rim[i : i + 1] for i in range(PLANES)] for rim in (high, low, nxt, prev))
    close_ends(nxt, prev, "gy")
    after = outer_face(high, nxt, high[5] > 0.5)
    behind = outer_face(low, prev, prev[5] < 0.5)
    flank_ref[0:1, :] = after[0]
    flank_ref[1:2, :] = behind[0]
    stand = upright(list(behind + after), lanes)
    stand = jnp.concatenate([part.astype(BF16) for part in halves(stand)], axis=1)
    wide = (2 * lanes, 3 * lanes)
    from_lane = lax.rem(iota(wide, 0), lanes)
    to_plane, to_lane = places(iota(wide, 1), lanes)
    side_ref[...] = nn(
        stand,
        ones_of(
            ((from_lane == to_plane) & (to_lane == 0)) | ((from_lane == to_plane + 3) & (to_lane == lanes - 1))
        ),
    )
    for z in range(layers):
        here = slice(z * width, (z + 1) * width)
        diag, rhs, around = (
            grid_ref[name, z] + side_ref[here, i * lanes : (i + 1) * lanes]
            for i, name in enumerate((DIAG, RHS, AROUND))
        )
        scale = RELAXATION * inverse(diag)
        rhs = scale * rhs
        grid_ref[CURRENT, z] = (1.0 - RELAXATION) * grid_ref[PRESS, z] + rhs + scale * around
        grid_ref[SCALE, z] = scale
        grid_ref[RHS, z] = rhs
        grid_ref[GAIN, z] = scale * grid_ref[MOB, z]


def first_update(
    given_ref, sums_ref, cell_ref, well_ref, index_ref,
    grid_ref, out_ref, yb_ref, xb_ref, xa_ref, ya_ref, known_ref, line_ref, block_ref, sems,
):
    layers, width, lanes = grid_ref.shape[1:]
    rows = layers * width
    count = lax.axis_size("gx") * lax.axis_size("gy")
    chunk = sums_ref.shape[0] // count
    well_rows = chunk - 1
    half = well_rows // 2
    group = count // well_rows
    across = lax.axis_size("gx")
    low = high = jnp.zeros((well_rows, LANES), F32)
    for d in range(count):
        sums = sums_ref[d * chunk : d * chunk + well_rows, :]
        if d // across % 2:
            high = high + sums
        else:
            low = low + sums
    part = jnp.concatenate([low[:half], high[:half]], axis=0)
    base = jnp.concatenate([low[half:], high[half:]], axis=0)
    owned = LANES // group
    place = lax.shift_right_logical(iota((well_rows, LANES), 1), bits_of(owned))
    mode = target = jnp.zeros((well_rows, LANES), F32)
    for j in range(group):
        for r in range(well_rows // across):
            first = (r * group + j) * across * chunk + well_rows
            line_ref[pl.ds(r, across, stride=well_rows // across), :] = sums_ref[
                pl.ds(first, across, stride=chunk), :
            ]
        line = line_ref[...]
        mode = jnp.where(place == j, pltpu.roll(line, j * owned, 1) if j else line, mode)
        shift = (j - 1) % group * owned
        target = jnp.where(place == j, pltpu.roll(line, shift, 1) if shift else line, target)
    bhp = jnp.where(mode < 0.5, target, (part - target) / base)
    known_ref[0] = mode
    known_ref[1] = target
    known_ref[2] = base
    row, lane = places(cell_ref[...], lanes)
    well_row, well_lane = places(well_ref[...], LANES)
    push = cell_scatter(slot_bhp(bhp, well_ref, index_ref), row, lane, rows, lanes)
    current = grid_ref[CURRENT].reshape(rows, lanes) + grid_ref[GAIN].reshape(rows, lanes) * push
    grid_ref[CURRENT] = current.reshape(layers, width, lanes)
    xa_ref[...], xb_ref[...] = sides(
        grid_ref[CURRENT, :, width - 1, :], grid_ref[CURRENT, :, 0, :], "gx"
    )
    mobile = grid_ref[MOB].reshape(rows, lanes) * current
    (at_cell,) = cell_find([mobile], *cell_pick(row, lane, rows, lanes))
    (part,) = well_scatter([live_index(well_ref, index_ref) * at_cell], well_row, well_lane, well_rows)
    block_ref[...] = jnp.concatenate([part] * (block_ref.shape[0] // well_rows), axis=0)
    outgoing = repeat_out(block_ref, out_ref, sems)
    both = jnp.concatenate([half.astype(BF16) for half in halves(current)], axis=1)
    pick_row, pick_lane = iota((2 * EDGE, 2 * lanes), 0), lax.rem(iota((2 * EDGE, 2 * lanes), 1), lanes)
    rims = nt(
        ones_of(((pick_row == 0) & (pick_lane == lanes - 1)) | ((pick_row == 1) & (pick_lane == 0))), both
    )
    ya_ref[...], yb_ref[...] = sides(rims[0:1], rims[1:2], "gy")
    for copy in outgoing:
        copy.wait()


def whole_first_update(*refs):
    given_ref, sums_ref, cell_ref, well_ref, index_ref = refs[:5]
    rims, (grid_ref, bound_ref, flank_ref) = refs[5:13], refs[13:16]
    outs, side_ref, scratch = refs[16:22], refs[22], refs[23:]
    outer_terms(given_ref, *rims, grid_ref, bound_ref, flank_ref, side_ref)
    first_update(given_ref, sums_ref, cell_ref, well_ref, index_ref, grid_ref, *outs, *scratch)


def inner_terms(after_ref, grid_ref, out_ref):
    layers, width, lanes = out_ref.shape
    for z in range(layers):
        current = grid_ref[CURRENT, z]
        besides = [
            pltpu.roll(current, width - 1, 0),
            pltpu.roll(current, 1, 0),
            pltpu.roll(current, lanes - 1, 1),
            pltpu.roll(current, 1, 1),
        ]
        around = grid_ref[COUP, z] * besides[0]
        for i in range(1, 4):
            around = around + grid_ref[COUP + i, z] * besides[i]
        if z + 1 < layers:
            around = around + grid_ref[COUP + 4, z] * grid_ref[CURRENT, z + 1]
        if z > 0:
            around = around + grid_ref[COUP + 5, z] * grid_ref[CURRENT, z - 1]
        out_ref[z] = (1.0 - RELAXATION) * current + grid_ref[RHS, z] + grid_ref[SCALE, z] * around


def last_update(
    sums_ref, known_ref, cell_ref, well_ref, index_ref, grid_ref, inner_ref, bound_ref, flank_ref,
    yb_ref, xb_ref, xa_ref, ya_ref, out_ref, bhp_ref, push_ref, side_ref,
):
    layers, width, lanes = out_ref.shape
    rows = layers * width
    count = lax.axis_size("gx") * lax.axis_size("gy")
    height = sums_ref.shape[0] // count
    well_rows = known_ref.shape[1]
    me = lax.axis_index(AXES)
    part = sums_ref[0:well_rows, :]
    for d in range(1, count):
        part = part + sums_ref[d * height : d * height + well_rows, :]
    bhp = jnp.where(known_ref[0] < 0.5, known_ref[1], (part - known_ref[1]) / known_ref[2])
    owned = bhp_ref.shape[1]
    group = LANES // owned
    line = jnp.sum(
        jnp.where(iota(bhp.shape, 0) == me // group, bhp, 0.0), axis=0, keepdims=True
    )
    line = pltpu.roll(line, lax.rem(LANES - lax.rem(me, group) * owned, LANES), 1)
    bhp_ref[...] = line[:, :owned]
    row, lane = places(cell_ref[...], lanes)
    push_ref[...] = cell_scatter(slot_bhp(bhp, well_ref, index_ref), row, lane, rows, lanes)
    nxt, prev = sides(ya_ref[...], yb_ref[...], "gy")
    side_ref[...] = upright([flank_ref[1:2, :] * prev, flank_ref[0:1, :] * nxt], lanes)
    along = iota((width, lanes), 1)
    nxt, prev = sides(xa_ref[...], xb_ref[...], "gx")
    for z in range(layers):
        here = slice(z * width, (z + 1) * width)
        side = side_ref[here, :]
        side = jnp.where(along == 0, side, jnp.where(along == lanes - 1, pltpu.roll(side, lanes - 2, 1), 0.0))
        out_ref[z] = inner_ref[z] + grid_ref[GAIN, z] * push_ref[here, :] + grid_ref[SCALE, z] * side
    for where, edge, beyond in ((0, width - 1, nxt), (1, 0, prev)):
        out_ref[:, edge, :] = out_ref[:, edge, :] + grid_ref[SCALE, :, edge, :] * (bound_ref[where] * beyond)


def call(kernel, outs, args, scratch=(), spaces=None, out_spaces=None, aliases=None):
    shapes = [jax.ShapeDtypeStruct(item, F32) if isinstance(item, tuple) else item for item in outs]
    spaces = spaces or [pltpu.VMEM] * len(args)
    out_spaces = out_spaces or [pltpu.VMEM] * len(outs)
    args = [
        pltpu.with_memory_space_constraint(arg, space) if space is pltpu.HBM else arg
        for arg, space in zip(args, spaces)
    ]
    return pl.pallas_call(
        kernel,
        out_shape=shapes,
        in_specs=[pl.BlockSpec(memory_space=space) for space in spaces],
        out_specs=[pl.BlockSpec(memory_space=space) for space in out_spaces],
        scratch_shapes=[pltpu.VMEM(item, F32) if isinstance(item, tuple) else item for item in scratch],
        input_output_aliases=aliases or {},
        compiler_params=pltpu.CompilerParams(vmem_limit_bytes=24 * 1024 * 1024),
        cost_estimate=pl.CostEstimate(flops=1_000_000, bytes_accessed=4_000_000, transcendentals=0),
    )(*args)


def whole_tiles(height, step, count):
    chunks = step
    while chunks * height % 8:
        chunks += step
    assert count % chunks == 0
    return chunks * height


def everyone(rows, count):
    height = rows.shape[0] // count
    swapped = lax.all_to_all(rows.reshape(count, height, 1, LANES), AXES[::-1], 0, 0, tiled=True)
    return swapped.reshape(rows.shape)


def to_pair(block, axis):
    count = lax.axis_size(axis)
    assert count % 2 == 0
    return lax.ppermute(block, axis, [(i, i ^ 1) for i in range(count)])


def to_other(block, axis):
    sizes = {name: lax.axis_size(name) for name in AXES}
    moves = []
    for gx in range(sizes["gx"]):
        for gy in range(sizes["gy"]):
            there = {"gx": gx, "gy": gy}
            away = there[axis] + (1 if there[axis] % 2 else -1)
            if 0 <= away < sizes[axis]:
                there[axis] = away
            else:
                cross = "gy" if axis == "gx" else "gx"
                there[cross] ^= 1
            moves.append((gx * sizes["gy"] + gy, there["gx"] * sizes["gy"] + there["gy"]))
    return lax.ppermute(block, AXES, moves)


def body(
    pressure, saturation, permeability, pore_volume, cell_depth, residual, upstream_flags,
    perf_cell, perf_well, perf_index, well_mode, well_target,
):
    layers, width, lanes = pressure.shape
    rows = layers * width
    count = lax.axis_size("gx") * lax.axis_size("gy")
    owned = well_mode.shape[0]
    well_rows = owned * count // LANES
    chunk = well_rows + 1
    grid = (layers, width, lanes)
    slots = [perf_cell, perf_well, perf_index]
    operands = slots + [
        saturation, pressure, permeability, cell_depth, upstream_flags, pore_volume, residual
    ]
    keep, give, given, flags = call(
        opening,
        [
            (well_rows, LANES), (well_rows, LANES), (GRIDS,) + grid,
            jax.ShapeDtypeStruct(grid, upstream_flags.dtype),
        ],
        operands,
        [pltpu.VMEM(a.shape, a.dtype) for a in slots] + [pltpu.SemaphoreType.DMA((INPUTS,))],
        [pltpu.HBM] * INPUTS,
    )
    height = whole_tiles(chunk, 1, count)
    sums, yb, xb, xa, ya = call(
        pair_sums,
        [
            (count * chunk, LANES), (EDGE, rows), (PLANES * layers, lanes), (PLANES * layers, lanes), (EDGE, rows),
        ],
        [keep, to_pair(give, "gy"), well_mode[None], well_target[None], given, flags],
        [
            (2 * EDGE * (rows // LANES), LANES), (height, LANES),
            pltpu.SemaphoreType.DMA((count * chunk // height,)),
        ],
        None,
        [pltpu.HBM] + [pltpu.VMEM] * 4,
    )
    rims = [yb, xb, xa, ya]
    rims = rims + [to_other(yb, "gy"), to_other(xb, "gx"), to_pair(xa, "gx"), to_pair(ya, "gy")]
    gathered = everyone(sums, count)
    (given,) = call(
        main_terms,
        [(GRIDS,) + grid],
        [given, sums, flags] + slots,
        [(rows, lanes)],
        [pltpu.VMEM, pl.ANY] + [pltpu.VMEM] * 4,
        None,
        {0: 0},
    )
    height = whole_tiles(well_rows, count, count)
    given, bound, flank, sums, yb, xb, xa, ya, known = call(
        whole_first_update,
        [
            (GRIDS,) + grid, (2, layers, lanes), (EDGE, rows),
            (count * well_rows, LANES), (1, rows), (layers, lanes), (layers, lanes), (1, rows),
            (3, well_rows, LANES),
        ],
        [given, gathered] + slots + rims,
        [
            (rows, 3 * lanes), (well_rows, LANES), (height, LANES),
            pltpu.SemaphoreType.DMA((count * well_rows // height,)),
        ],
        None,
        [pltpu.VMEM] * 3 + [pltpu.HBM] + [pltpu.VMEM] * 5,
        {0: 0},
    )
    gathered = everyone(sums, count)
    rims = [to_other(yb, "gy"), to_other(xb, "gx"), to_pair(xa, "gx"), to_pair(ya, "gy")]
    (inner,) = call(inner_terms, [grid], [sums, given], (), [pl.ANY, pltpu.VMEM])
    out, bhp = call(
        last_update,
        [grid, (1, owned)],
        [gathered, known] + slots + [given, inner, bound, flank] + rims,
        [(rows, lanes), (rows, lanes)],
    )
    return out, bhp[0]


def solution(mesh):
    return jax.shard_map(
        body,
        mesh=mesh,
        in_specs=(
            P(None, "gx", "gy"),
            P(None, None, "gx", "gy"),
            P(None, None, "gx", "gy"),
            P(None, "gx", "gy"),
            P(None, "gx", "gy"),
            P(None, None, "gx", "gy"),
            P(None, "gx", "gy"),
            P(("gx", "gy"), None),
            P(("gx", "gy"), None),
            P(("gx", "gy"), None),
            P(("gx", "gy")),
            P(("gx", "gy")),
        ),
        out_specs=(P(None, "gx", "gy"), P(("gx", "gy"))),
        check_vma=False,
    )
```

```python
import jax
import jax.numpy as jnp
from jax import lax
from jax.experimental import pallas as pl
from jax.experimental.pallas import tpu as pltpu
from jax.sharding import PartitionSpec as P

COMP_OIL = 0.2
COMP_WATER = 0.05
GRAV_OIL = 0.4
GRAV_WATER = 0.5
GRAV_GAS = 0.08
RELAXATION = 0.8
LANES = 128
PLANES = 6
INPUTS = 10
PRESS, SAT, PERM, DEPTH, PORE, RES, GRIDS = 0, 1, 3, 6, 7, 8, 11
DIAG, RHS, COUP, MOB, AROUND = 1, 2, 3, 9, 10
CURRENT, SCALE, GAIN = 0, 1, 10
EDGE = 8

F32 = jnp.float32
BF16 = jnp.bfloat16
AXES = ("gx", "gy")


def nn(a, b):
    return lax.dot_general(a, b, (((1,), (0,)), ((), ())), preferred_element_type=F32)


def nt(a, b):
    return lax.dot_general(a, b, (((1,), (1,)), ((), ())), preferred_element_type=F32)


def halves(x):
    high = x.astype(BF16).astype(F32)
    return high, x - high


def iota(shape, dim):
    return lax.broadcasted_iota(jnp.int32, shape, dim)


def hot(index, count):
    return iota((count, index.shape[1]), 0) == index


def ones_of(mask):
    return jnp.where(mask, 1.0, 0.0).astype(BF16)


def bits_of(n):
    assert n & (n - 1) == 0
    return n.bit_length() - 1


def places(index, width):
    return lax.shift_right_arithmetic(index, bits_of(width)), lax.bitwise_and(index, width - 1)


def cell_pick(row, lane, rows, lanes):
    pick = ones_of(hot(lane, lanes))
    return jnp.concatenate([pick, pick], axis=0), hot(row, rows)


def cell_find(fields, pick, at_row):
    rows = at_row.shape[0]
    both = [
        jnp.concatenate([part.astype(BF16) for part in halves(field)], axis=1) for field in fields
    ]
    found = nn(jnp.concatenate(both, axis=0), pick)
    return [
        jnp.sum(jnp.where(at_row, found[i * rows : (i + 1) * rows], 0.0), axis=0, keepdims=True)
        for i in range(len(fields))
    ]


def cell_scatter(value, row, lane, rows, lanes):
    spread = jnp.where(hot(lane, lanes), value, 0.0)
    spread = jnp.concatenate([part.astype(BF16) for part in halves(spread)], axis=0)
    total = nt(ones_of(hot(row, rows)), spread)
    return total[:, :lanes] + total[:, lanes:]


def well_scatter(values, row, lane, rows):
    mine = hot(row, rows)
    stack = []
    for value in values:
        stack.extend(halves(jnp.where(mine, value, 0.0)))
    total = nt(jnp.concatenate(stack, axis=0).astype(BF16), ones_of(hot(lane, LANES)))
    return [
        total[2 * i * rows : (2 * i + 1) * rows] + total[(2 * i + 1) * rows : (2 * i + 2) * rows]
        for i in range(len(values))
    ]


def well_gather(field, row, lane):
    rows = field.shape[0]
    both = jnp.concatenate(halves(field), axis=0).astype(BF16)
    found = nn(both, ones_of(hot(lane, LANES)))
    return jnp.sum(
        jnp.where(hot(row, rows), found[:rows] + found[rows:], 0.0), axis=0, keepdims=True
    )


def total_mobility(sat_water, sat_gas):
    sat_oil = 1.0 - sat_water - sat_gas
    return 0.5 * sat_oil * sat_oil + sat_water * sat_water + 5.0 * (sat_gas * sat_gas)


def phase_mobility(pressure, sat_water, sat_gas):
    sat_oil = 1.0 - sat_water - sat_gas
    b_oil = 1.0 + COMP_OIL * (pressure - 1.0)
    b_water = 1.0 + COMP_WATER * (pressure - 1.0)
    return (
        sat_oil * sat_oil * b_oil * 0.5,
        sat_water * sat_water * b_water,
        sat_gas * sat_gas * pressure * 5.0,
    )


def live_index(well_ref, index_ref):
    return jnp.where(well_ref[...] >= 0, index_ref[...], 0.0)


def fetch(sources, holds, sems):
    copies = [
        pltpu.make_async_copy(source, hold, sems.at[i])
        for i, (source, hold) in enumerate(zip(sources, holds))
    ]
    for copy in copies:
        copy.start()
    return copies


def repeat_out(block_ref, out_ref, sem):
    height = block_ref.shape[0]
    copies = [
        pltpu.make_async_copy(block_ref, out_ref.at[pl.ds(i * height, height)], sem.at[i])
        for i in range(out_ref.shape[0] // height)
    ]
    for copy in copies:
        copy.start()
    return copies


def is_even(axis):
    return lax.rem(lax.axis_index(axis), 2) == 0


def opening(*refs):
    inputs, sems = refs[:INPUTS], refs[-1]
    keep_ref, give_ref, grid_ref, flag_ref = refs[INPUTS : INPUTS + 4]
    cell_ref, well_ref, index_ref = slot_refs = refs[INPUTS + 4 : -1]
    holds = list(slot_refs) + [
        grid_ref.at[SAT : SAT + 2], grid_ref.at[PRESS], grid_ref.at[PERM : PERM + 3], grid_ref.at[DEPTH],
        flag_ref, grid_ref.at[PORE], grid_ref.at[RES : RES + 3],
    ]
    copies = fetch(inputs, holds, sems)
    layers, width, lanes = flag_ref.shape
    rows = layers * width
    well_rows = keep_ref.shape[0]
    for copy in copies[: len(slot_refs)]:
        copy.wait()
    row, lane = places(cell_ref[...], lanes)
    well_row, well_lane = places(well_ref[...], LANES)
    pick, at_row = cell_pick(row, lane, rows, lanes)
    index = live_index(well_ref, index_ref)
    later = copies[len(slot_refs) :]
    later[0].wait()
    mobility = total_mobility(grid_ref[SAT].reshape(rows, lanes), grid_ref[SAT + 1].reshape(rows, lanes))
    later[1].wait()
    press = grid_ref[PRESS].reshape(rows, lanes)
    at_mob, at_press = cell_find([mobility, mobility * press], pick, at_row)
    part, base = well_scatter([index * at_press, index * at_mob], well_row, well_lane, well_rows)
    half = well_rows // 2
    keep_ref[...], give_ref[...] = sides(
        jnp.concatenate([part[:half], base[:half]], axis=0),
        jnp.concatenate([part[half:], base[half:]], axis=0),
        "gy",
    )
    for copy in later[2:]:
        copy.wait()


def sides(a, b, axis):
    even = is_even(axis)
    return jnp.where(even, a, b), jnp.where(even, b, a)


def pair_sums(
    keep_ref, given_ref, mode_ref, target_ref, grid_ref, flag_ref,
    out_ref, yb_ref, xb_ref, xa_ref, ya_ref, lying_ref, block_ref, sems,
):
    owned = mode_ref.shape[1]
    group = LANES // owned
    controls = [mode_ref[...].astype(F32), target_ref[...]]
    if group > 2:
        controls.append(jnp.zeros((1, LANES - 2 * owned), F32))
    controls = jnp.concatenate(controls, axis=1)
    block = jnp.concatenate([keep_ref[...] + given_ref[...], controls], axis=0)
    block_ref[...] = jnp.concatenate([block] * (block_ref.shape[0] // block.shape[0]), axis=0)
    copies = repeat_out(block_ref, out_ref, sems)
    layers, width, lanes = flag_ref.shape
    rows = layers * width
    pair = lax.shift_right_logical(iota((rows, lanes), 1), 1)

    def rim(total, i, plane):
        return jnp.where(pair == i, pltpu.roll(plane.reshape(rows, lanes), 2 * i + 1, 1), total)

    total = rim(jnp.zeros((rows, lanes), F32), 0, grid_ref[PRESS])
    total = rim(rim(total, 1, grid_ref[SAT]), 2, grid_ref[SAT + 1])
    total = rim(total, 3, grid_ref[PERM + 1])
    total = rim(total, 4, grid_ref[DEPTH])
    bit_y = lax.bitwise_and(lax.shift_right_logical(flag_ref[...], 1), 1).astype(F32)
    total = rim(total, PLANES - 1, bit_y)
    pieces = [
        (i * 2 * EDGE, jnp.transpose(total[i * LANES : (i + 1) * LANES])[: 2 * EDGE])
        for i in range(rows // LANES)
    ]
    for first, piece in pieces:
        lying_ref[first : first + 2 * EDGE, :] = piece
    high, low = (
        jnp.concatenate([lying_ref[pl.ds(first + k, EDGE, stride=2), :] for first, _ in pieces], axis=1)
        for k in range(2)
    )
    x_even, y_even = is_even("gx"), is_even("gy")
    ya_ref[...] = jnp.where(y_even, high, low)
    yb_ref[...] = jnp.where(y_even, low, high)
    last = width - 1
    ends = [
        [
            grid_ref[PRESS, :, edge, :],
            grid_ref[SAT, :, edge, :],
            grid_ref[SAT + 1, :, edge, :],
            grid_ref[PERM, :, edge, :],
            grid_ref[DEPTH, :, edge, :],
            lax.bitwise_and(flag_ref[:, edge, :], 1).astype(F32),
        ]
        for edge in (last, 0)
    ]
    for i, (high, low) in enumerate(zip(*ends)):
        xa_ref[i * layers : (i + 1) * layers, :] = jnp.where(x_even, high, low)
        xb_ref[i * layers : (i + 1) * layers, :] = jnp.where(x_even, low, high)
    for copy in copies:
        copy.wait()


def upright(rows_list, lanes):
    stack = jnp.concatenate(rows_list, axis=0)
    stack = jnp.concatenate([stack, jnp.zeros((lanes - stack.shape[0], stack.shape[1]), F32)], axis=0)
    return jnp.transpose(stack)


def inverse(x):
    guess = pl.reciprocal(x, approx=True)
    return guess * (2.0 - x * guess)


def phase_weights(pressure):
    b_oil = 1.0 + COMP_OIL * (pressure - 1.0)
    b_water = 1.0 + COMP_WATER * (pressure - 1.0)
    whole = inverse(b_oil * b_water * pressure)
    other = pressure * whole
    return b_water * other, b_oil * other, b_oil * b_water * whole


def faces(perm, perm_next, mob, mob_next, first_up):
    transmit = 2.0 * perm * perm_next * inverse(perm + perm_next)
    return [transmit * jnp.where(first_up, a, b) for a, b in zip(mob, mob_next)]


def weighted(weights, flux):
    oil, water, gas = (w * f for w, f in zip(weights, flux))
    return oil + water + gas, GRAV_OIL * oil + GRAV_WATER * water + GRAV_GAS * gas


def outer_face(own, other, own_up):
    mob, mob_other = phase_mobility(*own[:3]), phase_mobility(*other[:3])
    coupling, lift = weighted(phase_weights(own[0]), faces(own[3], other[3], mob, mob_other, own_up))
    return coupling, lift * (own[4] - other[4]), coupling * other[0]


def main_terms(given_ref, after_ref, flag_ref, cell_ref, well_ref, index_ref, grid_ref, share_ref):
    layers, width, lanes = flag_ref.shape
    rows = layers * width
    row, lane = places(cell_ref[...], lanes)
    share_ref[...] = cell_scatter(live_index(well_ref, index_ref), row, lane, rows, lanes)
    x_last = iota((width, lanes), 0) == width - 1
    y_last = iota((width, lanes), 1) == lanes - 1

    def layer(z):
        press = grid_ref[PRESS, z]
        return press, phase_mobility(press, grid_ref[SAT, z], grid_ref[SAT + 1, z])

    this = layer(0)
    before = None
    for z in range(layers):
        press, mob = this
        following = layer(z + 1) if z + 1 < layers else None
        sat_water, sat_gas = grid_ref[SAT, z], grid_ref[SAT + 1, z]
        sat_oil = 1.0 - sat_water - sat_gas
        depth = grid_ref[DEPTH, z]
        flags = flag_ref[z]
        weights = phase_weights(press)
        storage = grid_ref[PORE, z] * (
            sat_oil * COMP_OIL * weights[0] + sat_water * COMP_WATER * weights[1] + sat_gas * weights[2]
        )
        mobility = total_mobility(sat_water, sat_gas)
        diag = storage + mobility * share_ref[z * width : (z + 1) * width, :]
        rhs = storage * press
        for i, weight in enumerate(weights):
            rhs = rhs - weight * grid_ref[RES + i, z]
        around = jnp.zeros_like(press)
        couplings = {}

        def add(name, flux, drop, beside):
            nonlocal diag, rhs, around
            coupling, lift = weighted(weights, flux)
            couplings[name] = coupling
            diag = diag + coupling
            rhs = rhs + lift * drop
            around = around + coupling * beside

        for dim, size, end, bit in ((0, width, x_last, 1), (1, lanes, y_last, 2)):
            perm = grid_ref[PERM + dim, z]
            perm_next = jnp.where(end, 0.0, pltpu.roll(perm, size - 1, dim))
            up = lax.bitwise_and(flags, bit) > 0
            flux = faces(perm, perm_next, mob, [pltpu.roll(a, size - 1, dim) for a in mob], up)
            drop = depth - pltpu.roll(depth, size - 1, dim)
            add(2 * dim, flux, drop, pltpu.roll(press, size - 1, dim))
            add(2 * dim + 1, [pltpu.roll(a, 1, dim) for a in flux], -pltpu.roll(drop, 1, dim), pltpu.roll(press, 1, dim))
        if following is not None:
            up = lax.bitwise_and(flags, 4) > 0
            flux = faces(grid_ref[PERM + 2, z], grid_ref[PERM + 2, z + 1], mob, following[1], up)
            drop = depth - grid_ref[DEPTH, z + 1]
            add(4, flux, drop, following[0])
        if before is not None:
            add(5, before[0], -before[1], before[2])
        if following is not None:
            before = (flux, drop, press)
        for name, coupling in couplings.items():
            grid_ref[COUP + name, z] = coupling
        grid_ref[DIAG, z] = diag
        grid_ref[RHS, z] = rhs
        grid_ref[AROUND, z] = around
        grid_ref[MOB, z] = mobility
        this = following


def slot_bhp(bhp, well_ref, index_ref):
    well_row, well_lane = places(well_ref[...], LANES)
    return live_index(well_ref, index_ref) * well_gather(bhp, well_row, well_lane)


def close_ends(nxt, prev, axis):
    me = lax.axis_index(axis)
    nxt[3] = jnp.where(me < lax.axis_size(axis) - 1, nxt[3], 0.0)
    prev[3] = jnp.where(me > 0, prev[3], 0.0)


def outer_terms(
    given_ref, own_yb_ref, own_xb_ref, own_xa_ref, own_ya_ref, yb_ref, xb_ref, xa_ref, ya_ref,
    grid_ref, bound_ref, flank_ref, side_ref,
):
    layers, width, lanes = grid_ref.shape[1:]
    rows = layers * width
    (high, low), (nxt, prev) = (
        sides(own_xa_ref[...], own_xb_ref[...], "gx"), sides(xa_ref[...], xb_ref[...], "gx")
    )
    high, low, nxt, prev = (
        [rim[i * layers : (i + 1) * layers] for i in range(PLANES)] for rim in (high, low, nxt, prev)
    )
    close_ends(nxt, prev, "gx")
    for where, edge, terms in (
        (0, width - 1, outer_face(high, nxt, high[5] > 0.5)),
        (1, 0, outer_face(low, prev, prev[5] < 0.5)),
    ):
        bound_ref[where] = terms[0]
        for name, term in zip((DIAG, RHS, AROUND), terms):
            grid_ref[name, :, edge, :] = grid_ref[name, :, edge, :] + term
    (high, low), (nxt, prev) = (
        sides(own_ya_ref[...], own_yb_ref[...], "gy"), sides(ya_ref[...], yb_ref[...], "gy")
    )
    high, low, nxt, prev = ([rim[i : i + 1] for i in range(PLANES)] for rim in (high, low, nxt, prev))
    close_ends(nxt, prev, "gy")
    after = outer_face(high, nxt, high[5] > 0.5)
    behind = outer_face(low, prev, prev[5] < 0.5)
    flank_ref[0:1, :] = after[0]
    flank_ref[1:2, :] = behind[0]
    stand = upright(list(behind + after), lanes)
    stand = jnp.concatenate([part.astype(BF16) for part in halves(stand)], axis=1)
    wide = (2 * lanes, 3 * lanes)
    from_lane = lax.rem(iota(wide, 0), lanes)
    to_plane, to_lane = places(iota(wide, 1), lanes)
    side_ref[...] = nn(
        stand,
        ones_of(
            ((from_lane == to_plane) & (to_lane == 0)) | ((from_lane == to_plane + 3) & (to_lane == lanes - 1))
        ),
    )
    for z in range(layers):
        here = slice(z * width, (z + 1) * width)
        diag, rhs, around = (
            grid_ref[name, z] + side_ref[here, i * lanes : (i + 1) * lanes]
            for i, name in enumerate((DIAG, RHS, AROUND))
        )
        scale = RELAXATION * inverse(diag)
        rhs = scale * rhs
        grid_ref[CURRENT, z] = (1.0 - RELAXATION) * grid_ref[PRESS, z] + rhs + scale * around
        grid_ref[SCALE, z] = scale
        grid_ref[RHS, z] = rhs
        grid_ref[GAIN, z] = scale * grid_ref[MOB, z]


def first_update(
    between, sums_ref, cell_ref, well_ref, index_ref,
    grid_ref, out_ref, yb_ref, xb_ref, xa_ref, ya_ref, known_ref, line_ref, block_ref, sems,
):
    layers, width, lanes = grid_ref.shape[1:]
    rows = layers * width
    count = lax.axis_size("gx") * lax.axis_size("gy")
    chunk = sums_ref.shape[0] // count
    well_rows = chunk - 1
    half = well_rows // 2
    group = count // well_rows
    across = lax.axis_size("gx")
    low = high = jnp.zeros((well_rows, LANES), F32)
    for d in range(count):
        sums = sums_ref[d * chunk : d * chunk + well_rows, :]
        if d // across % 2:
            high = high + sums
        else:
            low = low + sums
    part = jnp.concatenate([low[:half], high[:half]], axis=0)
    base = jnp.concatenate([low[half:], high[half:]], axis=0)
    owned = LANES // group
    place = lax.shift_right_logical(iota((well_rows, LANES), 1), bits_of(owned))
    mode = target = jnp.zeros((well_rows, LANES), F32)
    for j in range(group):
        for r in range(well_rows // across):
            first = (r * group + j) * across * chunk + well_rows
            line_ref[pl.ds(r, across, stride=well_rows // across), :] = sums_ref[
                pl.ds(first, across, stride=chunk), :
            ]
        line = line_ref[...]
        mode = jnp.where(place == j, pltpu.roll(line, j * owned, 1) if j else line, mode)
        shift = (j - 1) % group * owned
        target = jnp.where(place == j, pltpu.roll(line, shift, 1) if shift else line, target)
    bhp = jnp.where(mode < 0.5, target, (part - target) / base)
    known_ref[0] = mode
    known_ref[1] = target
    known_ref[2] = base
    row, lane = places(cell_ref[...], lanes)
    well_row, well_lane = places(well_ref[...], LANES)
    push = cell_scatter(slot_bhp(bhp, well_ref, index_ref), row, lane, rows, lanes)
    between()
    current = grid_ref[CURRENT].reshape(rows, lanes) + grid_ref[GAIN].reshape(rows, lanes) * push
    grid_ref[CURRENT] = current.reshape(layers, width, lanes)
    xa_ref[...], xb_ref[...] = sides(
        grid_ref[CURRENT, :, width - 1, :], grid_ref[CURRENT, :, 0, :], "gx"
    )
    mobile = grid_ref[MOB].reshape(rows, lanes) * current
    (at_cell,) = cell_find([mobile], *cell_pick(row, lane, rows, lanes))
    (part,) = well_scatter([live_index(well_ref, index_ref) * at_cell], well_row, well_lane, well_rows)
    block_ref[...] = jnp.concatenate([part] * (block_ref.shape[0] // well_rows), axis=0)
    outgoing = repeat_out(block_ref, out_ref, sems)
    both = jnp.concatenate([half.astype(BF16) for half in halves(current)], axis=1)
    pick_row, pick_lane = iota((2 * EDGE, 2 * lanes), 0), lax.rem(iota((2 * EDGE, 2 * lanes), 1), lanes)
    rims = nt(
        ones_of(((pick_row == 0) & (pick_lane == lanes - 1)) | ((pick_row == 1) & (pick_lane == 0))), both
    )
    ya_ref[...], yb_ref[...] = sides(rims[0:1], rims[1:2], "gy")
    for copy in outgoing:
        copy.wait()


def whole_first_update(*refs):
    given_ref, sums_ref, cell_ref, well_ref, index_ref = refs[:5]
    rims, (grid_ref, bound_ref, flank_ref) = refs[5:13], refs[13:16]
    outs, side_ref, scratch = refs[16:22], refs[22], refs[23:]

    def between():
        outer_terms(given_ref, *rims, grid_ref, bound_ref, flank_ref, side_ref)

    first_update(between, sums_ref, cell_ref, well_ref, index_ref, grid_ref, *outs, *scratch)


def inner_terms(after_ref, grid_ref, out_ref):
    layers, width, lanes = out_ref.shape
    for z in range(layers):
        current = grid_ref[CURRENT, z]
        besides = [
            pltpu.roll(current, width - 1, 0),
            pltpu.roll(current, 1, 0),
            pltpu.roll(current, lanes - 1, 1),
            pltpu.roll(current, 1, 1),
        ]
        around = grid_ref[COUP, z] * besides[0]
        for i in range(1, 4):
            around = around + grid_ref[COUP + i, z] * besides[i]
        if z + 1 < layers:
            around = around + grid_ref[COUP + 4, z] * grid_ref[CURRENT, z + 1]
        if z > 0:
            around = around + grid_ref[COUP + 5, z] * grid_ref[CURRENT, z - 1]
        out_ref[z] = (1.0 - RELAXATION) * current + grid_ref[RHS, z] + grid_ref[SCALE, z] * around


def last_update(
    sums_ref, known_ref, cell_ref, well_ref, index_ref, grid_ref, inner_ref, bound_ref, flank_ref,
    yb_ref, xb_ref, xa_ref, ya_ref, out_ref, bhp_ref, push_ref, side_ref,
):
    layers, width, lanes = out_ref.shape
    rows = layers * width
    count = lax.axis_size("gx") * lax.axis_size("gy")
    height = sums_ref.shape[0] // count
    well_rows = known_ref.shape[1]
    me = lax.axis_index(AXES)
    part = sums_ref[0:well_rows, :]
    for d in range(1, count):
        part = part + sums_ref[d * height : d * height + well_rows, :]
    bhp = jnp.where(known_ref[0] < 0.5, known_ref[1], (part - known_ref[1]) / known_ref[2])
    owned = bhp_ref.shape[1]
    group = LANES // owned
    line = jnp.sum(
        jnp.where(iota(bhp.shape, 0) == me // group, bhp, 0.0), axis=0, keepdims=True
    )
    line = pltpu.roll(line, lax.rem(LANES - lax.rem(me, group) * owned, LANES), 1)
    bhp_ref[...] = line[:, :owned]
    row, lane = places(cell_ref[...], lanes)
    push_ref[...] = cell_scatter(slot_bhp(bhp, well_ref, index_ref), row, lane, rows, lanes)
    nxt, prev = sides(ya_ref[...], yb_ref[...], "gy")
    side_ref[...] = upright([flank_ref[1:2, :] * prev, flank_ref[0:1, :] * nxt], lanes)
    along = iota((width, lanes), 1)
    nxt, prev = sides(xa_ref[...], xb_ref[...], "gx")
    for z in range(layers):
        here = slice(z * width, (z + 1) * width)
        side = side_ref[here, :]
        side = jnp.where(along == 0, side, jnp.where(along == lanes - 1, pltpu.roll(side, lanes - 2, 1), 0.0))
        out_ref[z] = inner_ref[z] + grid_ref[GAIN, z] * push_ref[here, :] + grid_ref[SCALE, z] * side
    for where, edge, beyond in ((0, width - 1, nxt), (1, 0, prev)):
        out_ref[:, edge, :] = out_ref[:, edge, :] + grid_ref[SCALE, :, edge, :] * (bound_ref[where] * beyond)


def call(kernel, outs, args, scratch=(), spaces=None, out_spaces=None, aliases=None):
    shapes = [jax.ShapeDtypeStruct(item, F32) if isinstance(item, tuple) else item for item in outs]
    spaces = spaces or [pltpu.VMEM] * len(args)
    out_spaces = out_spaces or [pltpu.VMEM] * len(outs)
    args = [
        pltpu.with_memory_space_constraint(arg, space) if space is pltpu.HBM else arg
        for arg, space in zip(args, spaces)
    ]
    return pl.pallas_call(
        kernel,
        out_shape=shapes,
        in_specs=[pl.BlockSpec(memory_space=space) for space in spaces],
        out_specs=[pl.BlockSpec(memory_space=space) for space in out_spaces],
        scratch_shapes=[pltpu.VMEM(item, F32) if isinstance(item, tuple) else item for item in scratch],
        input_output_aliases=aliases or {},
        compiler_params=pltpu.CompilerParams(vmem_limit_bytes=24 * 1024 * 1024),
        cost_estimate=pl.CostEstimate(flops=1_000_000, bytes_accessed=4_000_000, transcendentals=0),
    )(*args)


def whole_tiles(height, step, count):
    chunks = step
    while chunks * height % 8:
        chunks += step
    assert count % chunks == 0
    return chunks * height


def everyone(rows, count):
    height = rows.shape[0] // count
    swapped = lax.all_to_all(rows.reshape(count, height, 1, LANES), AXES[::-1], 0, 0, tiled=True)
    return swapped.reshape(rows.shape)


def to_pair(block, axis):
    count = lax.axis_size(axis)
    assert count % 2 == 0
    return lax.ppermute(block, axis, [(i, i ^ 1) for i in range(count)])


def to_other(block, axis):
    sizes = {name: lax.axis_size(name) for name in AXES}
    moves = []
    for gx in range(sizes["gx"]):
        for gy in range(sizes["gy"]):
            there = {"gx": gx, "gy": gy}
            away = there[axis] + (1 if there[axis] % 2 else -1)
            if 0 <= away < sizes[axis]:
                there[axis] = away
            else:
                cross = "gy" if axis == "gx" else "gx"
                there[cross] ^= 1
            moves.append((gx * sizes["gy"] + gy, there["gx"] * sizes["gy"] + there["gy"]))
    return lax.ppermute(block, AXES, moves)


def body(
    pressure, saturation, permeability, pore_volume, cell_depth, residual, upstream_flags,
    perf_cell, perf_well, perf_index, well_mode, well_target,
):
    layers, width, lanes = pressure.shape
    rows = layers * width
    count = lax.axis_size("gx") * lax.axis_size("gy")
    owned = well_mode.shape[0]
    well_rows = owned * count // LANES
    chunk = well_rows + 1
    grid = (layers, width, lanes)
    slots = [perf_cell, perf_well, perf_index]
    operands = slots + [
        saturation, pressure, permeability, cell_depth, upstream_flags, pore_volume, residual
    ]
    keep, give, given, flags = call(
        opening,
        [
            (well_rows, LANES), (well_rows, LANES), (GRIDS,) + grid,
            jax.ShapeDtypeStruct(grid, upstream_flags.dtype),
        ],
        operands,
        [pltpu.VMEM(a.shape, a.dtype) for a in slots] + [pltpu.SemaphoreType.DMA((INPUTS,))],
        [pltpu.HBM] * INPUTS,
    )
    height = whole_tiles(chunk, 1, count)
    sums, yb, xb, xa, ya = call(
        pair_sums,
        [
            (count * chunk, LANES), (EDGE, rows), (PLANES * layers, lanes), (PLANES * layers, lanes), (EDGE, rows),
        ],
        [keep, to_pair(give, "gy"), well_mode[None], well_target[None], given, flags],
        [
            (2 * EDGE * (rows // LANES), LANES), (height, LANES),
            pltpu.SemaphoreType.DMA((count * chunk // height,)),
        ],
        None,
        [pltpu.HBM] + [pltpu.VMEM] * 4,
    )
    rims = [yb, xb, xa, ya]
    rims = rims + [to_other(yb, "gy"), to_other(xb, "gx"), to_pair(xa, "gx"), to_pair(ya, "gy")]
    gathered = everyone(sums, count)
    (given,) = call(
        main_terms,
        [(GRIDS,) + grid],
        [given, sums, flags] + slots,
        [(rows, lanes)],
        [pltpu.VMEM, pl.ANY] + [pltpu.VMEM] * 4,
        None,
        {0: 0},
    )
    height = whole_tiles(well_rows, count, count)
    given, bound, flank, sums, yb, xb, xa, ya, known = call(
        whole_first_update,
        [
            (GRIDS,) + grid, (2, layers, lanes), (EDGE, rows),
            (count * well_rows, LANES), (1, rows), (layers, lanes), (layers, lanes), (1, rows),
            (3, well_rows, LANES),
        ],
        [given, gathered] + slots + rims,
        [
            (rows, 3 * lanes), (well_rows, LANES), (height, LANES),
            pltpu.SemaphoreType.DMA((count * well_rows // height,)),
        ],
        None,
        [pltpu.VMEM] * 3 + [pltpu.HBM] + [pltpu.VMEM] * 5,
        {0: 0},
    )
    gathered = everyone(sums, count)
    rims = [to_other(yb, "gy"), to_other(xb, "gx"), to_pair(xa, "gx"), to_pair(ya, "gy")]
    (inner,) = call(inner_terms, [grid], [sums, given], (), [pl.ANY, pltpu.VMEM])
    out, bhp = call(
        last_update,
        [grid, (1, owned)],
        [gathered, known] + slots + [given, inner, bound, flank] + rims,
        [(rows, lanes), (rows, lanes)],
    )
    return out, bhp[0]


def solution(mesh):
    return jax.shard_map(
        body,
        mesh=mesh,
        in_specs=(
            P(None, "gx", "gy"),
            P(None, None, "gx", "gy"),
            P(None, None, "gx", "gy"),
            P(None, "gx", "gy"),
            P(None, "gx", "gy"),
            P(None, None, "gx", "gy"),
            P(None, "gx", "gy"),
            P(("gx", "gy"), None),
            P(("gx", "gy"), None),
            P(("gx", "gy"), None),
            P(("gx", "gy")),
            P(("gx", "gy")),
        ),
        out_specs=(P(None, "gx", "gy"), P(("gx", "gy"))),
        check_vma=False,
    )
```
